256 devices in a mesh: seq: 32 (over z, y), chan: 8 (over x, core).
Axes of the slice: x: 4, y: 4, z: 8, core: 2. Of those that a mesh axis runs over, the one named last changes fastest.
Arguments:
- query: bfloat16 [4096, 4096], P('seq', 'chan'), may hold values from -6 to 6
- key: bfloat16 [4096, 4096], P('seq', 'chan'), may hold values from -6 to 6
- value: bfloat16 [4096, 4096], P('seq', 'chan'), may hold values from -6 to 6
- short_taps: float32 [3, 3, 4096], P(None, None, 'chan'), may hold values from -3 to 3
- residue: float32 [4096, 16], P('chan'), may hold values from -6 to 6
- rate: float32 [4096, 16], P('chan'), may hold values from 0.00012207031 to 0.05
- skip: float32 [4096], P('chan'), may hold values from -4 to 4
- out_weight: bfloat16 [4096, 4096], P(None, 'chan'), may hold values from -0.09375 to 0.09375
Outputs:
- mixed: bfloat16 [4096, 4096], P('seq', 'chan')
The draws below stay inside these ranges and needn't reach their ends.
All inputs are finite; a program needn't handle non-finite values.
Results may differ from the reference program's by a relative error of at most 0.0049.
Values may be sent and summed in bfloat16 or wider, within the bound.
A program may use at most 64 MiB of HBM per device.

```python
import math
import jax
import jax.numpy as jnp
from jax import lax

C = 4096
MODES = 16
TOKENS = 4096


def block_levels(own_key, shape, shards, least, largest):
    def one(position, blocks):
        heights = jax.random.uniform(jax.random.fold_in(jax.random.fold_in(own_key, 6), position), (blocks,), jnp.float32, least / len(shards), largest / len(shards))
        return jnp.repeat(jnp.exp(heights), shape[position] // blocks).reshape((-1,) + (1,) * (len(shape) - position - 1))

    level = one(*shards[0])
    for cut in shards[1:]:
        level = level * one(*cut)
    return level


def noise(own_key, extent, spread, most, cuts=(), kind=jnp.bfloat16):
    loudness = block_levels(own_key, extent, cuts, -0.22, 0.18) if cuts else 1.0
    array = jax.random.normal(own_key, extent, jnp.float32) * spread * loudness
    return jnp.minimum(jnp.maximum(array, -most), most).astype(kind)


def setup_inputs(seed: int = 0) -> dict:
    streams_of = jax.random.split(jax.random.key(seed), 9)
    query = noise(streams_of[0], (TOKENS, C), 1.0, 6.0, ((0, 32), (1, 8)))
    key = noise(streams_of[1], (TOKENS, C), 1.0, 6.0, ((0, 32), (1, 8)))
    value = noise(streams_of[2], (TOKENS, C), 1.0, 6.0, ((0, 32), (1, 8)))
    short_taps = noise(streams_of[3], (3, 3, C), 0.5, 3.0, ((2, 8),), jnp.float32)
    residue = noise(streams_of[4], (C, MODES), 1.0, 6.0, ((0, 8),), jnp.float32)
    rate = jnp.clip(jnp.exp(math.log(0.05) - 6.015181 * jax.random.uniform(streams_of[5], (C, MODES), jnp.float32) ** block_levels(streams_of[5], (C, MODES), ((0, 8),), -0.2, 0.2)), 0.00012207031, 0.05)
    skip = noise(streams_of[6], (C,), 1.0, 4.0, ((0, 8),), jnp.float32)
    out_weight = noise(streams_of[7], (C, C), C ** -0.5, 0.09375, ((1, 8),))
    return dict(query=query, key=key, value=value, short_taps=short_taps, residue=residue, rate=rate, skip=skip, out_weight=out_weight)


def causal_taps(signal, tap_weights):
    first_lag = jnp.pad(signal, ((1, 0), (0, 0)))[:-1]
    second_lag = jnp.pad(signal, ((2, 0), (0, 0)))[:-2]
    return tap_weights[0] * signal + tap_weights[1] * first_lag + tap_weights[2] * second_lag


def long_filter_block(block_args):
    gated, residues, mode_rates = block_args
    length = gated.shape[1]
    positions = jnp.arange(length, dtype=jnp.float32)

    def add_mode(mode_index, kernel_sum):
        mode_rate = mode_rates[:, mode_index]
        weight = -residues[:, mode_index] * jnp.expm1(-mode_rate)
        return kernel_sum + weight[:, None] * jnp.exp(-mode_rate[:, None] * positions[None, :])

    kernel_sum = lax.fori_loop(0, residues.shape[1], add_mode, jnp.zeros(gated.shape, jnp.float32))
    product_spec = jnp.fft.rfft(gated, n=2 * length, axis=1) * jnp.fft.rfft(kernel_sum, n=2 * length, axis=1)
    return jnp.fft.irfft(product_spec, n=2 * length, axis=1)[:, :length]


def reference(query, key, value, short_taps, residue, rate, skip, out_weight):
    query_conv = causal_taps(query.astype(jnp.float32), short_taps[0])
    key_conv = causal_taps(key.astype(jnp.float32), short_taps[1])
    value_conv = causal_taps(value.astype(jnp.float32), short_taps[2])
    gated = key_conv * value_conv
    chan_width = gated.shape[1]
    block_width = min(256, chan_width)
    groups = chan_width // block_width
    convolved = lax.map(long_filter_block, (gated.T.reshape(groups, block_width, -1), residue.reshape(groups, block_width, -1), rate.reshape(groups, block_width, -1)))
    convolved = convolved.reshape(chan_width, -1).T
    hidden = (query_conv * (convolved + skip * gated)).astype(jnp.bfloat16)
    return jnp.dot(hidden, out_weight, preferred_element_type=jnp.float32).astype(jnp.bfloat16)
```

```python
import functools

import jax
import jax.numpy as jnp
from jax import lax
from jax.experimental import pallas as pl
from jax.experimental.pallas import tpu as pltpu
from jax.sharding import PartitionSpec as P

MESH = pl.DeviceIdType.MESH
F32 = jnp.float32
BF16 = jnp.bfloat16
MODES = 16
STEPS = 16
SUBS = 8
ROWS = STEPS * SUBS
LANES = 128
CHIPS = 4
CORES = 2
PIECES = 2


def tree_sum(array):
    while array.shape[0] > 1:
        half = array.shape[0] // 2
        array = array[:half] + array[half:]
    return array[0]


def lagged(block, last, last_but_one):
    one = jnp.concatenate([last[None], block[:-1]], axis=0)
    two = jnp.concatenate([last_but_one[None], one[:-1]], axis=0)
    return one, two


def tapped(taps, which, cols, now, one, two):
    return (
        taps[which, 0:1, cols] * now + taps[which, 1:2, cols] * one + taps[which, 2:3, cols] * two
    )


def kernel(
    zs,
    ys,
    q_hbm,
    k_hbm,
    v_hbm,
    taps_hbm,
    res_hbm,
    rate_hbm,
    skip_hbm,
    w_hbm,
    out_ref,
    q_in,
    k_in,
    v_in,
    taps,
    res,
    rate,
    skip,
    weight,
    rate3,
    decay3,
    gain3,
    xq,
    xk,
    xv,
    gated,
    enter,
    power,
    local,
    query,
    msg,
    ring_y,
    edge,
    halo_out,
    halo_in,
    total,
    ring_z,
    before,
    starts,
    start_in,
    hid,
    acc,
    load_sem,
    p1_send,
    p1_recv,
    halo_sem,
    edge_send,
    edge_recv,
    p2_send,
    p2_recv,
    p3_send,
    p3_recv,
    g_send,
    g_recv,
):
    seq = lax.axis_index("seq")
    chan = lax.axis_index("chan")
    z, y = seq // ys, lax.rem(seq, ys)
    x, core = chan // CORES, lax.rem(chan, CORES)
    width = k_in.shape[1]
    tiles = width // LANES
    count = zs * ys

    loads = [
        pltpu.make_async_copy(src, dst, load_sem.at[i])
        for i, (src, dst) in enumerate(
            [
                (rate_hbm, rate),
                (res_hbm, res),
                (taps_hbm, taps),
                (k_hbm, k_in),
                (v_hbm, v_in),
                (q_hbm, q_in),
                (skip_hbm, skip),
                (w_hbm, weight),
            ]
        )
    ]
    for load in loads:
        load.start()

    def at(zz, yy):
        return zz * ys + yy

    right = lax.rem(x + 1, CHIPS) * CORES + core
    left = lax.rem(x + CHIPS - 1, CHIPS) * CORES + core
    sibling = x * CORES + 1 - core
    z_up = lax.rem(z + 1, zs)
    z_down = lax.rem(z + zs - 1, zs)

    barrier = pltpu.get_barrier_semaphore()

    def greet(s, c):
        pl.semaphore_signal(barrier, inc=1, device_id=(s, c), device_id_type=MESH)

    for e in range(1, ys):
        greet(at(z, lax.rem(y + e, ys)), chan)
    for e in range(1, zs):
        greet(at(lax.rem(z + e, zs), y), chan)
    greet(lax.rem(seq + 1, count), chan)
    greet(lax.rem(seq + count - 1, count), chan)
    greet(at(z_down, ys - 1), chan)
    for c in (right, left, sibling):
        greet(seq, c)

    @pl.when(y == ys - 1)
    def _():
        for e in range(ys):
            greet(at(z_up, e), chan)

    loads[0].wait()
    loads[1].wait()
    r = rate[...]
    series = r * (1.0 - r * (1 / 2) * (1.0 - r * (1 / 3) * (1.0 - r * (1 / 4) * (1.0 - r * (1 / 5) * (1.0 - r * (1 / 6))))))
    gain = res[...] * series
    decay = jnp.exp(-r)
    for m in range(MODES):
        rate3[m] = jnp.broadcast_to(r[m : m + 1], (SUBS, width))
        decay3[m] = jnp.broadcast_to(decay[m : m + 1], (SUBS, width))
        gain3[m] = jnp.broadcast_to(gain[m : m + 1], (SUBS, width))

    row = lax.broadcasted_iota(jnp.int32, (ROWS, ROWS), 0)
    col = lax.broadcasted_iota(jnp.int32, (ROWS, ROWS), 1)
    order = jnp.where(col == (row & 7) * STEPS + (row >> 3), 1.0, 0.0).astype(BF16)
    back = jnp.where(row == (col & 7) * STEPS + (col >> 3), 1.0, 0.0).astype(BF16)

    def arranged(block):
        return jnp.dot(order, block, preferred_element_type=F32).reshape(STEPS, SUBS, width)

    sub = lax.broadcasted_iota(jnp.int32, (SUBS, LANES), 0)
    sub3 = lax.broadcasted_iota(jnp.int32, (MODES, SUBS, LANES), 1)
    first = sub == 0
    subf3 = sub3.astype(F32)

    loads[2].wait()
    loads[3].wait()
    loads[4].wait()
    xk[...] = arranged(k_in[...])
    xv[...] = arranged(v_in[...])

    def lags(block):
        last = jnp.where(first, 0.0, pltpu.roll(block[STEPS - 1], 1, 0))
        last_but_one = jnp.where(first, 0.0, pltpu.roll(block[STEPS - 2], 1, 0))
        return lagged(block, last, last_but_one)

    for l in range(tiles):
        cols = slice(l * LANES, (l + 1) * LANES)
        kb, vb = xk[:, :, cols], xv[:, :, cols]
        g = tapped(taps, 1, cols, kb, *lags(kb)) * tapped(taps, 2, cols, vb, *lags(vb))
        g = jnp.concatenate([jnp.where(first[None], 0.0, g[:2]), g[2:]], axis=0)
        gated[:, :, cols] = g
        a = decay3[:, :, cols]
        state = jnp.broadcast_to(g[0][None], a.shape)
        for j in range(1, STEPS):
            state = state * a + g[j][None]
        step = a
        for _ in range(4):
            step = step * step
        for reach in (1, 2, 4):
            state = state + jnp.where(sub3 >= reach, step, 0.0) * pltpu.roll(state, reach, 1)
            step = step * step
        enter[:, :, cols] = jnp.where(sub3 >= 1, pltpu.roll(state, 1, 1), 0.0)
        for m in range(MODES):
            msg[l, m : m + 1, :] = state[m, SUBS - 1 : SUBS, :]
        for i, block in enumerate((kb, vb)):
            base = MODES + 4 * i
            msg[l, base : base + 1, :] = block[0, 0:1, :]
            msg[l, base + 1 : base + 2, :] = block[1, 0:1, :]
            msg[l, base + 2 : base + 3, :] = block[STEPS - 2, SUBS - 1 : SUBS, :]
            msg[l, base + 3 : base + 4, :] = block[STEPS - 1, SUBS - 1 : SUBS, :]

    pl.semaphore_wait(barrier, 3 + (ys - 1) + (zs - 1) + 3 + jnp.where(y == ys - 1, ys, 0))

    p1 = []
    for e in range(1, ys):
        to = lax.rem(y + e, ys)
        p1.append(
            pltpu.make_async_remote_copy(
                msg.at[to], ring_y.at[y], p1_send.at[e - 1], p1_recv.at[e - 1],
                device_id=(at(z, to), chan), device_id_type=MESH,
            )
        )
    edges = [
        pltpu.make_async_remote_copy(
            msg.at[e, pl.ds(MODES, 8)], edge, edge_send.at[e], edge_recv,
            device_id=(at(z_up, e), chan), device_id_type=MESH,
        )
        for e in range(ys)
    ]

    for copy in p1:
        copy.start()

    @pl.when(y == ys - 1)
    def _():
        for copy in edges:
            copy.start()

    loads[5].wait()
    xq[...] = arranged(q_in[...])
    for i, block in enumerate((xq, xk, xv)):
        halo_out[2 * i : 2 * i + 1, :] = block[STEPS - 2, SUBS - 1 : SUBS, :]
        halo_out[2 * i + 1 : 2 * i + 2, :] = block[STEPS - 1, SUBS - 1 : SUBS, :]
    halo_out[6:8, :] = jnp.zeros((2, width), F32)
    halo = pltpu.make_async_remote_copy(
        halo_out, halo_in, halo_sem.at[0], halo_sem.at[1],
        device_id=(lax.rem(seq + 1, count), chan), device_id_type=MESH,
    )
    halo.start()

    def chunk_start(cols, rows_now, rows_before):
        k0, k1, v0, v1 = rows_now
        k126, k127, v126, v127 = rows_before
        g0 = tapped(taps, 1, cols, k0, k127, k126) * tapped(taps, 2, cols, v0, v127, v126)
        g1 = tapped(taps, 1, cols, k1, k0, k127) * tapped(taps, 2, cols, v1, v0, v127)
        return g0, g1

    mine = pl.ds(pl.multiple_of(y * LANES, LANES), LANES)
    r_mine = rate[:, mine]

    ring_y[y] = msg[y]
    a126 = jnp.exp(-(ROWS - 2.0) * r_mine)
    a127 = jnp.exp(-(ROWS - 1.0) * r_mine)
    a128 = jnp.exp(-float(ROWS) * r_mine)
    for copy in p1:
        copy.wait_recv()
    edges[0].wait_recv()
    ends = [jnp.where(z == 0, 0.0, edge[i : i + 1, :]) for i in (2, 3, 6, 7)]
    states = []
    for e in range(ys):
        now = [ring_y[e, MODES + i : MODES + i + 1, :] for i in (0, 1, 4, 5)]
        g0, g1 = chunk_start(mine, now, ends)
        ends = [ring_y[e, MODES + i : MODES + i + 1, :] for i in (2, 3, 6, 7)]
        states.append(ring_y[e, 0:MODES, :] + a127 * g0 + a126 * g1)
    whole = states[0]
    for e in range(1, ys):
        whole = whole * a128 + states[e]
    total[...] = whole

    p2 = []
    for d in range(1, zs):
        copy = pltpu.make_async_remote_copy(
            total, ring_z.at[d - 1], p2_send.at[d - 1], p2_recv.at[d - 1],
            device_id=(at(lax.rem(z + d, zs), y), chan), device_id_type=MESH,
        )
        p2.append(copy)
        pl.when(z + d < zs)(copy.start)

    halo.wait_recv()
    loads[6].wait()
    for l in range(tiles):
        cols = slice(l * LANES, (l + 1) * LANES)
        ends = [jnp.where(seq == 0, 0.0, halo_in[i : i + 1, cols]) for i in range(6)]
        kb, vb = (xk, xv)
        now = [b[j, 0:1, cols] for b in (kb, vb) for j in (0, 1)]
        g0, g1 = chunk_start(cols, now, ends[2:6])
        g = gated[:, :, cols]
        g = jnp.concatenate(
            [jnp.where(first, g0, g[0])[None], jnp.where(first, g1, g[1])[None], g[2:]], axis=0
        )
        r3, a, w = rate3[:, :, cols], decay3[:, :, cols], gain3[:, :, cols]
        wa = w * a
        pw = jnp.exp(-float(STEPS) * subf3 * r3)
        missing = jnp.where(sub3 >= 1, pw * jnp.exp(2.0 * r3) * (a * g0[None] + g1[None]), 0.0)
        enter[:, :, cols] = wa * (enter[:, :, cols] + missing)
        power[:, :, cols] = wa * pw
        near = w * jnp.exp(-subf3 * r3)
        a8 = a * a
        a8 = a8 * a8
        a8 = a8 * a8
        taps_near = (tree_sum(near), tree_sum(near * a8))
        out = g * skip[0:1, cols]
        for d in range(STEPS):
            tap = taps_near[d // SUBS][d % SUBS : d % SUBS + 1, :]
            add = g[: STEPS - d] * tap[None]
            out = out + add if d == 0 else jnp.concatenate([out[:d], out[d:] + add], axis=0)
        local[:, :, cols] = out
        qb = xq[:, :, cols]
        last = jnp.where(first, ends[1], pltpu.roll(qb[STEPS - 1], 1, 0))
        last_but_one = jnp.where(first, ends[0], pltpu.roll(qb[STEPS - 2], 1, 0))
        query[:, :, cols] = tapped(taps, 0, cols, qb, *lagged(qb, last, last_but_one))

    before[...] = jnp.zeros_like(before)
    for d in range(1, zs):

        @pl.when(z >= d)
        def _():
            p2[d - 1].wait_recv()
            before[...] += jnp.exp(-float(ROWS * ys * (d - 1)) * r_mine) * ring_z[d - 1]

    start = before[...]
    for e in range(ys):
        starts[e] = start
        if e < ys - 1:
            start = start * a128 + states[e]

    p3 = []
    for e in range(1, ys):
        to = lax.rem(y + e, ys)
        copy = pltpu.make_async_remote_copy(
            starts.at[to], start_in.at[y], p3_send.at[e - 1], p3_recv.at[e - 1],
            device_id=(at(z, to), chan), device_id_type=MESH,
        )
        copy.start()
        p3.append(copy)
    start_in[y] = starts[y]
    for copy in p3:
        copy.wait_recv()

    sent = []

    def send(index, slot, piece, to_slot, to):
        copy = pltpu.make_async_remote_copy(
            hid.at[slot, piece], hid.at[to_slot, piece], g_send.at[index], g_recv.at[index],
            device_id=(seq, to), device_id_type=MESH,
        )
        copy.start()
        sent.append(copy)
        return copy

    per = tiles // PIECES
    own_sib, own_right, own_left = {}, {}, {}
    for p in range(PIECES):
        for i in range(per):
            l = p * per + i
            cols = slice(l * LANES, (l + 1) * LANES)
            a = decay3[:, :, cols]
            state = jnp.stack(
                [
                    enter[m, :, cols] + power[m, :, cols] * start_in[l, m : m + 1, :]
                    for m in range(MODES)
                ]
            )
            blocks = []
            for j in range(STEPS):
                blocks.append(query[j, :, cols] * (local[j, :, cols] + tree_sum(state)))
                if j < STEPS - 1:
                    state = state * a
            block = jnp.concatenate(blocks, axis=0)
            hid[0, p, :, i * LANES : (i + 1) * LANES] = block.astype(BF16)
        own_right[p] = send(p, 0, p, 6, right)
        own_sib[p] = send(2 + p, 0, p, 1, sibling)
    for p in (1, 0):
        own_left[p] = send(4 + p, 0, p, 2, left)

    loads[7].wait()
    half = width // PIECES

    def product(slot, piece):
        owner = lax.rem(x + slot // CORES, CHIPS) * CORES + (core if slot % CORES == 0 else 1 - core)
        rows = pl.ds(pl.multiple_of(owner * width + piece * half, half), half)
        return jnp.dot(hid[slot, piece], weight[rows, :], preferred_element_type=F32)

    acc[...] = product(0, 0) + product(0, 1)
    for p in range(PIECES):
        own_sib[p].wait_recv()
        acc[...] += product(1, p)

    own_right[0].wait_recv()
    on_right = send(6, 6, 0, 4, right)
    sib = {(7, 0): send(8, 6, 0, 7, sibling)}
    own_left[1].wait_recv()
    on_left = send(7, 2, 1, 4, left)
    sib[3, 1] = send(9, 2, 1, 3, sibling)
    acc[...] += product(6, 0) + product(2, 1)
    for slot, p in ((7, 0), (3, 1)):
        sib[slot, p].wait_recv()
        acc[...] += product(slot, p)
    own_right[1].wait_recv()
    sib[7, 1] = send(10, 6, 1, 7, sibling)
    own_left[0].wait_recv()
    sib[3, 0] = send(11, 2, 0, 3, sibling)
    acc[...] += product(6, 1) + product(2, 0)
    for slot, p in ((7, 1), (3, 0)):
        sib[slot, p].wait_recv()
        acc[...] += product(slot, p)
    on_right.wait_recv()
    sib[5, 0] = send(12, 4, 0, 5, sibling)
    on_left.wait_recv()
    sib[5, 1] = send(13, 4, 1, 5, sibling)
    acc[...] += product(4, 0) + product(4, 1)
    for p in range(PIECES):
        sib[5, p].wait_recv()
        acc[...] += product(5, p)

    mixed = acc[...].astype(BF16)
    out_ref[...] = jnp.dot(back, mixed, preferred_element_type=F32).astype(BF16)

    for copy in p1 + p3 + sent + [halo]:
        copy.wait_send()
    for d in range(1, zs):
        pl.when(z + d < zs)(p2[d - 1].wait_send)

    @pl.when(y == ys - 1)
    def _():
        for copy in edges:
            copy.wait_send()


def per_device(zs, ys, query, key, value, short_taps, residue, rate, skip, out_weight):
    width = query.shape[1]
    tiles = width // LANES
    table = pltpu.VMEM((MODES, SUBS, width), F32)
    block = pltpu.VMEM((STEPS, SUBS, width), F32)
    dma = pltpu.SemaphoreType.DMA
    scratch = [
        pltpu.VMEM((ROWS, width), BF16),
        pltpu.VMEM((ROWS, width), BF16),
        pltpu.VMEM((ROWS, width), BF16),
        pltpu.VMEM(short_taps.shape, F32),
        pltpu.VMEM((MODES, width), F32),
        pltpu.VMEM((MODES, width), F32),
        pltpu.VMEM((1, width), F32),
        pltpu.VMEM(out_weight.shape, BF16),
        table,
        table,
        table,
        block,
        block,
        block,
        block,
        table,
        table,
        block,
        block,
        pltpu.VMEM((tiles, MODES + 8, LANES), F32),
        pltpu.VMEM((ys, MODES + 8, LANES), F32),
        pltpu.VMEM((8, LANES), F32),
        pltpu.VMEM((8, width), F32),
        pltpu.VMEM((8, width), F32),
        pltpu.VMEM((MODES, LANES), F32),
        pltpu.VMEM((zs - 1, MODES, LANES), F32),
        pltpu.VMEM((MODES, LANES), F32),
        pltpu.VMEM((ys, MODES, LANES), F32),
        pltpu.VMEM((ys, MODES, LANES), F32),
        pltpu.VMEM((CHIPS * CORES, PIECES, ROWS, width // PIECES), BF16),
        pltpu.VMEM((ROWS, width), F32),
        dma((8,)),
        dma((ys - 1,)),
        dma((ys - 1,)),
        dma((2,)),
        dma((ys,)),
        dma,
        dma((zs - 1,)),
        dma((zs - 1,)),
        dma((ys - 1,)),
        dma((ys - 1,)),
        dma((14,)),
        dma((14,)),
    ]
    return pl.pallas_call(
        functools.partial(kernel, zs, ys),
        out_shape=jax.ShapeDtypeStruct((ROWS, width), BF16),
        in_specs=[pl.BlockSpec(memory_space=pl.ANY)] * 8,
        out_specs=pl.BlockSpec(memory_space=pltpu.VMEM),
        scratch_shapes=scratch,
        compiler_params=pltpu.CompilerParams(
            collective_id=0, has_side_effects=True, vmem_limit_bytes=56 * 1024 * 1024
        ),
    )(query, key, value, short_taps, residue.T, rate.T, skip[None, :], out_weight)


def solution(mesh, ys=4):
    placed = (
        P("seq", "chan"),
        P("seq", "chan"),
        P("seq", "chan"),
        P(None, None, "chan"),
        P("chan", None),
        P("chan", None),
        P("chan"),
        P(None, "chan"),
    )
    return jax.shard_map(
        functools.partial(per_device, mesh.shape["seq"] // ys, ys),
        mesh=mesh,
        in_specs=placed,
        out_specs=P("seq", "chan"),
        check_vma=False,
    )
```

```python
import functools

import jax
import jax.numpy as jnp
from jax import lax
from jax.experimental import pallas as pl
from jax.experimental.pallas import tpu as pltpu
from jax.sharding import PartitionSpec as P

MESH = pl.DeviceIdType.MESH
F32 = jnp.float32
BF16 = jnp.bfloat16
MODES = 16
STEPS = 16
SUBS = 8
ROWS = STEPS * SUBS
LANES = 128
CHIPS = 4
CORES = 2
PIECES = 2


def tree_sum(array):
    while array.shape[0] > 1:
        half = array.shape[0] // 2
        array = array[:half] + array[half:]
    return array[0]


def lagged(block, last, last_but_one):
    one = jnp.concatenate([last[None], block[:-1]], axis=0)
    two = jnp.concatenate([last_but_one[None], one[:-1]], axis=0)
    return one, two


def tapped(taps, which, cols, now, one, two):
    return (
        taps[which, 0:1, cols] * now + taps[which, 1:2, cols] * one + taps[which, 2:3, cols] * two
    )


def kernel(
    zs,
    ys,
    q_hbm,
    k_hbm,
    v_hbm,
    taps_hbm,
    res_hbm,
    rate_hbm,
    skip_hbm,
    w_hbm,
    out_ref,
    q_in,
    k_in,
    v_in,
    taps,
    res,
    rate,
    skip,
    weight,
    rate3,
    decay3,
    gain3,
    xk,
    xv,
    enter,
    power,
    near,
    local,
    query,
    edge_y,
    edge_z,
    state_y,
    heads,
    starts,
    total,
    ring_z,
    before,
    hit,
    hit_later,
    hid,
    acc,
    load_sem,
    y_send,
    y_recv,
    e_send,
    e_recv,
    z_send,
    z_recv,
    g_send,
    g_recv,
    ready,
    ready_edge,
):
    seq = lax.axis_index("seq")
    chan = lax.axis_index("chan")
    z, y = seq // ys, lax.rem(seq, ys)
    x, core = chan // CORES, lax.rem(chan, CORES)
    width = k_in.shape[1]
    tiles = width // LANES
    last_y = y == ys - 1

    loads = [
        pltpu.make_async_copy(src, dst, load_sem.at[i])
        for i, (src, dst) in enumerate(
            [
                (rate_hbm, rate),
                (res_hbm, res),
                (taps_hbm, taps),
                (k_hbm, k_in),
                (v_hbm, v_in),
                (q_hbm, q_in),
                (skip_hbm, skip),
                (w_hbm, weight),
            ]
        )
    ]
    for load in loads:
        load.start()
    pending = []

    def at(zz, yy):
        return zz * ys + yy

    def signal(sem, s, c):
        pl.semaphore_signal(sem, inc=1, device_id=(s, c), device_id_type=MESH)

    right = lax.rem(x + 1, CHIPS) * CORES + core
    left = lax.rem(x + CHIPS - 1, CHIPS) * CORES + core
    sibling = x * CORES + 1 - core
    z_up = lax.rem(z + 1, zs)
    z_down = lax.rem(z + zs - 1, zs)

    barrier = pltpu.get_barrier_semaphore()
    for e in range(1, ys):
        signal(barrier, at(z, lax.rem(y + e, ys)), chan)
    for c in (right, left, sibling):
        signal(barrier, seq, c)
    for d in range(1, zs):

        @pl.when(z + d < zs)
        def _():
            signal(barrier, at(lax.rem(z + d, zs), y), chan)

    @pl.when(last_y & (z < zs - 1))
    def _():
        for e in range(ys):
            signal(barrier, at(z_up, e), chan)

    loads[0].wait()
    loads[1].wait()
    r = rate[...]
    series = r * (1.0 - r * (1 / 2) * (1.0 - r * (1 / 3) * (1.0 - r * (1 / 4) * (1.0 - r * (1 / 5) * (1.0 - r * (1 / 6))))))
    gain = res[...] * series
    decay = jnp.exp(-r)
    for m in range(MODES):
        rate3[m] = jnp.broadcast_to(r[m : m + 1], (SUBS, width))
        decay3[m] = jnp.broadcast_to(decay[m : m + 1], (SUBS, width))
        gain3[m] = jnp.broadcast_to(gain[m : m + 1], (SUBS, width))

    row = lax.broadcasted_iota(jnp.int32, (ROWS, ROWS), 0)
    col = lax.broadcasted_iota(jnp.int32, (ROWS, ROWS), 1)
    order = jnp.where(col == (row & 7) * STEPS + (row >> 3), 1.0, 0.0).astype(BF16)
    back = jnp.where(row == (col & 7) * STEPS + (col >> 3), 1.0, 0.0).astype(BF16)

    def arranged(block):
        return jnp.dot(order, block, preferred_element_type=F32).reshape(STEPS, SUBS, width)

    sub = lax.broadcasted_iota(jnp.int32, (SUBS, LANES), 0)
    sub3 = lax.broadcasted_iota(jnp.int32, (MODES, SUBS, LANES), 1)
    first = sub == 0
    subf3 = sub3.astype(F32)

    loads[2].wait()
    loads[3].wait()
    loads[4].wait()
    xk[...] = arranged(k_in[...])
    xv[...] = arranged(v_in[...])

    def lags(block):
        last = jnp.where(first, 0.0, pltpu.roll(block[STEPS - 1], 1, 0))
        last_but_one = jnp.where(first, 0.0, pltpu.roll(block[STEPS - 2], 1, 0))
        return lagged(block, last, last_but_one)

    for l in range(tiles):
        cols = slice(l * LANES, (l + 1) * LANES)
        kb, vb = xk[:, :, cols], xv[:, :, cols]
        g = tapped(taps, 1, cols, kb, *lags(kb)) * tapped(taps, 2, cols, vb, *lags(vb))
        g = jnp.concatenate([jnp.where(first[None], 0.0, g[:2]), g[2:]], axis=0)
        local[:, :, cols] = g
        a = decay3[:, :, cols]
        state = jnp.broadcast_to(g[0][None], a.shape)
        for j in range(1, STEPS):
            state = state * a + g[j][None]
        step = a
        for _ in range(4):
            step = step * step
        for reach in (1, 2, 4):
            state = state + jnp.where(sub3 >= reach, step, 0.0) * pltpu.roll(state, reach, 1)
            step = step * step
        enter[:, :, cols] = jnp.where(sub3 >= 1, pltpu.roll(state, 1, 1), 0.0)
        for m in range(MODES):
            state_y[y, m : m + 1, cols] = state[m, SUBS - 1 : SUBS, :]

    loads[5].wait()
    pick = lax.broadcasted_iota(jnp.int32, (MODES, ROWS), 0)
    pos = lax.broadcasted_iota(jnp.int32, (MODES, ROWS), 1)

    def chosen(base, block):
        i = pick - base
        ends = ((i >= 0) & (i < 2) & (pos == i)) | ((i >= 2) & (i < 4) & (pos == i + ROWS - 4))
        return jnp.dot(
            jnp.where(ends, 1.0, 0.0).astype(BF16), block[...], preferred_element_type=F32
        )

    edge_y[y] = (chosen(0, k_in) + chosen(4, v_in) + chosen(8, q_in)).astype(BF16)

    pl.semaphore_wait(barrier, (ys - 1) + 3 + z + jnp.where(z > 0, 1, 0))
    for d in range(1, zs):

        @pl.when(z >= d)
        def _():
            signal(ready.at[d - 1], at(lax.rem(z + zs - d, zs), y), chan)

    @pl.when(z > 0)
    def _():
        signal(ready_edge, at(z_down, ys - 1), chan)

    y_copies = []
    for e in range(1, ys):
        to = (at(z, lax.rem(y + e, ys)), chan)
        for i, buf in enumerate((state_y, edge_y)):
            copy = pltpu.make_async_remote_copy(
                buf.at[y], buf.at[y], y_send.at[i, e - 1], y_recv.at[i, e - 1],
                device_id=to, device_id_type=MESH,
            )
            copy.start()
            pending.append(copy.wait_send)
            y_copies.append(copy)

    edges = [
        pltpu.make_async_remote_copy(
            edge_y.at[y], edge_z, e_send.at[e], e_recv,
            device_id=(at(z_up, e), chan), device_id_type=MESH,
        )
        for e in range(ys)
    ]

    @pl.when(last_y & (z < zs - 1))
    def _():
        pl.semaphore_wait(ready_edge, ys)
        for copy in edges:
            copy.start()

    @pending.append
    def _():
        @pl.when(last_y & (z < zs - 1))
        def _():
            for copy in edges:
                copy.wait_send()

    loads[6].wait()
    for l in range(tiles):
        cols = slice(l * LANES, (l + 1) * LANES)
        r3, a, w = rate3[:, :, cols], decay3[:, :, cols], gain3[:, :, cols]
        wa = w * a
        enter[:, :, cols] = wa * enter[:, :, cols]
        power[:, :, cols] = wa * jnp.exp(-float(STEPS) * subf3 * r3)
        close = w * jnp.exp(-subf3 * r3)
        a8 = a * a
        a8 = a8 * a8
        a8 = a8 * a8
        near[0:SUBS, cols] = tree_sum(close)
        near[SUBS : 2 * SUBS, cols] = tree_sum(close * a8)
        g = local[:, :, cols]
        out = g * skip[0:1, cols]
        for d in range(STEPS):
            add = g[: STEPS - d] * near[d : d + 1, cols][None]
            out = out + add if d == 0 else jnp.concatenate([out[:d], out[d:] + add], axis=0)
        local[:, :, cols] = out
    for i in range(2):
        half_cols = slice(i * width // 2, (i + 1) * width // 2)
        arranged_q = jnp.dot(order, q_in[:, half_cols], preferred_element_type=F32)
        arranged_q = arranged_q.reshape(STEPS, SUBS, width // 2)
        for l in range(tiles // 2):
            cols = slice(i * width // 2 + l * LANES, i * width // 2 + (l + 1) * LANES)
            qb = arranged_q[:, :, l * LANES : (l + 1) * LANES]
            query[:, :, cols] = tapped(taps, 0, cols, qb, *lags(qb))
    r = rate[...]
    a126 = jnp.exp(-(ROWS - 2.0) * r)
    a127 = jnp.exp(-(ROWS - 1.0) * r)
    a128 = jnp.exp(-float(ROWS) * r)

    everything = slice(0, width)

    @pl.when(z == 0)
    def _():
        edge_z[...] = jnp.zeros_like(edge_z)

    @pl.when(z > 0)
    def _():
        edges[0].wait_recv()

    for copy in y_copies:
        copy.wait_recv()
    ends = edge_z[...].astype(F32)
    start = jnp.zeros_like(r)
    for e in range(ys):
        now = edge_y[e].astype(F32)
        k0, k1, v0, v1 = (now[i : i + 1] for i in (0, 1, 4, 5))
        k126, k127, v126, v127, q126, q127 = (ends[i : i + 1] for i in (2, 3, 6, 7, 10, 11))
        g0 = tapped(taps, 1, everything, k0, k127, k126) * tapped(
            taps, 2, everything, v0, v127, v126
        )
        g1 = tapped(taps, 1, everything, k1, k0, k127) * tapped(taps, 2, everything, v1, v0, v127)
        for i, line in enumerate((g0, g1, q126, q127)):
            heads[e, i : i + 1, :] = line
        starts[e] = start
        start = start * a128 + (state_y[e] + a127 * g0 + a126 * g1)
        ends = now
    total[...] = start

    z_copies = []
    for d in range(1, zs):
        copy = pltpu.make_async_remote_copy(
            total, ring_z.at[d - 1], z_send.at[d - 1], z_recv.at[d - 1],
            device_id=(at(lax.rem(z + d, zs), y), chan), device_id_type=MESH,
        )
        z_copies.append(copy)

        @pl.when(z + d < zs)
        def _():
            pl.semaphore_wait(ready.at[d - 1], 1)
            copy.start()

        pending.append(functools.partial(pl.when(z + d < zs), copy.wait_send))

    g0, g1, q126, q127 = (heads[y, i : i + 1, :] for i in range(4))
    for j in range(STEPS):
        extra = near[j : j + 1, :] * g0
        if j:
            extra = extra + near[j - 1 : j, :] * g1
        if j < 2:
            extra = extra + skip[0:1, :] * (g0, g1)[j]
        local[j, 0:1, :] += extra
    query[0, 0:1, :] += taps[0, 1:2, :] * q127 + taps[0, 2:3, :] * q126
    query[1, 0:1, :] += taps[0, 2:3, :] * q127
    head = jnp.exp(r) * g0 + jnp.exp(2.0 * r) * g1

    before[...] = jnp.zeros_like(before)
    for d in range(1, zs):

        @pl.when(z >= d)
        def _():
            z_copies[d - 1].wait_recv()
            before[...] += jnp.exp(-float(ROWS * ys * (d - 1)) * rate[...]) * ring_z[d - 1]

    start = starts[y] + jnp.exp(-float(ROWS) * y.astype(F32) * r) * before[...]
    hit[...] = start
    hit_later[...] = start + head

    def send(index, slot, piece, to_slot, to):
        copy = pltpu.make_async_remote_copy(
            hid.at[slot, piece], hid.at[to_slot, piece], g_send.at[index], g_recv.at[index],
            device_id=(seq, to), device_id_type=MESH,
        )
        copy.start()
        pending.append(copy.wait_send)
        return copy

    per = tiles // PIECES
    own_sib, own_right, own_left = {}, {}, {}
    for p in range(PIECES):
        for i in range(per):
            l = p * per + i
            cols = slice(l * LANES, (l + 1) * LANES)
            a = decay3[:, :, cols]
            state = jnp.stack(
                [
                    enter[m, :, cols]
                    + power[m, :, cols]
                    * jnp.where(first, hit[m : m + 1, cols], hit_later[m : m + 1, cols])
                    for m in range(MODES)
                ]
            )
            blocks = []
            for j in range(STEPS):
                blocks.append(query[j, :, cols] * (local[j, :, cols] + tree_sum(state)))
                if j < STEPS - 1:
                    state = state * a
            block = jnp.concatenate(blocks, axis=0)
            hid[0, p, :, i * LANES : (i + 1) * LANES] = block.astype(BF16)
        own_right[p] = send(p, 0, p, 6, right)
        own_sib[p] = send(2 + p, 0, p, 1, sibling)
    for p in (1, 0):
        own_left[p] = send(4 + p, 0, p, 2, left)

    loads[7].wait()
    half = width // PIECES

    def product(slot, piece):
        owner = lax.rem(x + slot // CORES, CHIPS) * CORES + (core if slot % CORES == 0 else 1 - core)
        rows = pl.ds(pl.multiple_of(owner * width + piece * half, half), half)
        return jnp.dot(hid[slot, piece], weight[rows, :], preferred_element_type=F32)

    acc[...] = product(0, 0) + product(0, 1)
    for p in range(PIECES):
        own_sib[p].wait_recv()
        acc[...] += product(1, p)

    own_right[0].wait_recv()
    on_right = send(6, 6, 0, 4, right)
    sib = {(7, 0): send(8, 6, 0, 7, sibling)}
    own_left[1].wait_recv()
    on_left = send(7, 2, 1, 4, left)
    sib[3, 1] = send(9, 2, 1, 3, sibling)
    acc[...] += product(6, 0) + product(2, 1)
    for slot, p in ((7, 0), (3, 1)):
        sib[slot, p].wait_recv()
        acc[...] += product(slot, p)
    own_right[1].wait_recv()
    sib[7, 1] = send(10, 6, 1, 7, sibling)
    own_left[0].wait_recv()
    sib[3, 0] = send(11, 2, 0, 3, sibling)
    acc[...] += product(6, 1) + product(2, 0)
    for slot, p in ((7, 1), (3, 0)):
        sib[slot, p].wait_recv()
        acc[...] += product(slot, p)
    on_right.wait_recv()
    sib[5, 0] = send(12, 4, 0, 5, sibling)
    on_left.wait_recv()
    sib[5, 1] = send(13, 4, 1, 5, sibling)
    acc[...] += product(4, 0) + product(4, 1)
    for p in range(PIECES):
        sib[5, p].wait_recv()
        acc[...] += product(5, p)

    mixed = acc[...].astype(BF16)
    out_ref[...] = jnp.dot(back, mixed, preferred_element_type=F32).astype(BF16)

    for wait in pending:
        wait()


def per_device(zs, ys, query, key, value, short_taps, residue, rate, skip, out_weight):
    width = query.shape[1]
    modes = pltpu.VMEM((MODES, width), F32)
    table = pltpu.VMEM((MODES, SUBS, width), F32)
    block = pltpu.VMEM((STEPS, SUBS, width), F32)
    dma = pltpu.SemaphoreType.DMA
    regular = pltpu.SemaphoreType.REGULAR
    scratch = [
        pltpu.VMEM((ROWS, width), BF16),
        pltpu.VMEM((ROWS, width), BF16),
        pltpu.VMEM((ROWS, width), BF16),
        pltpu.VMEM(short_taps.shape, F32),
        modes,
        modes,
        pltpu.VMEM((1, width), F32),
        pltpu.VMEM(out_weight.shape, BF16),
        table,
        table,
        table,
        block,
        block,
        table,
        table,
        pltpu.VMEM((STEPS, width), F32),
        block,
        block,
        pltpu.VMEM((ys, MODES, width), BF16),
        pltpu.VMEM((MODES, width), BF16),
        pltpu.VMEM((ys, MODES, width), F32),
        pltpu.VMEM((ys, 8, width), F32),
        pltpu.VMEM((ys, MODES, width), F32),
        modes,
        pltpu.VMEM((zs - 1, MODES, width), F32),
        modes,
        modes,
        modes,
        pltpu.VMEM((CHIPS * CORES, PIECES, ROWS, width // PIECES), BF16),
        pltpu.VMEM((ROWS, width), F32),
        dma((8,)),
        dma((2, ys - 1)),
        dma((2, ys - 1)),
        dma((ys,)),
        dma,
        dma((zs - 1,)),
        dma((zs - 1,)),
        dma((14,)),
        dma((14,)),
        regular((zs - 1,)),
        regular,
    ]
    return pl.pallas_call(
        functools.partial(kernel, zs, ys),
        out_shape=jax.ShapeDtypeStruct((ROWS, width), BF16),
        in_specs=[pl.BlockSpec(memory_space=pl.ANY)] * 8,
        out_specs=pl.BlockSpec(memory_space=pltpu.VMEM),
        scratch_shapes=scratch,
        compiler_params=pltpu.CompilerParams(
            collective_id=0, has_side_effects=True, vmem_limit_bytes=56 * 1024 * 1024
        ),
    )(query, key, value, short_taps, residue.T, rate.T, skip[None, :], out_weight)


def solution(mesh, ys=4):
    placed = (
        P("seq", "chan"),
        P("seq", "chan"),
        P("seq", "chan"),
        P(None, None, "chan"),
        P("chan", None),
        P("chan", None),
        P("chan"),
        P(None, "chan"),
    )
    return jax.shard_map(
        functools.partial(per_device, mesh.shape["seq"] // ys, ys),
        mesh=mesh,
        in_specs=placed,
        out_specs=P("seq", "chan"),
        check_vma=False,
    )
```

```python
import functools

import jax
import jax.numpy as jnp
import ml_dtypes
import numpy as np
from jax import lax
from jax.experimental import pallas as pl
from jax.experimental.pallas import tpu as pltpu
from jax.sharding import PartitionSpec as P

MESH = pl.DeviceIdType.MESH
F32 = jnp.float32
BF16 = jnp.bfloat16
MODES = 16
STEPS = 16
SUBS = 8
ROWS = STEPS * SUBS
LANES = 128
CHIPS = 4
CORES = 2
PIECES = 2
NODES = STEPS - 2


def tree_sum(array):
    while array.shape[0] > 1:
        half = array.shape[0] // 2
        array = array[:half] + array[half:]
    return array[0]


def lagged(block, last, last_but_one):
    one = jnp.concatenate([last[None], block[:-1]], axis=0)
    two = jnp.concatenate([last_but_one[None], one[:-1]], axis=0)
    return one, two


def tapped(taps, which, cols, now, one, two):
    return (
        taps[which, 0:1, cols] * now + taps[which, 1:2, cols] * one + taps[which, 2:3, cols] * two
    )


def kernel(
    zs,
    ys,
    q_hbm,
    k_hbm,
    v_hbm,
    taps_hbm,
    res_hbm,
    rate_hbm,
    skip_hbm,
    w_hbm,
    weights_hbm,
    places_hbm,
    out_ref,
    q_in,
    k_in,
    v_in,
    taps,
    res,
    rate,
    skip,
    weight,
    weights,
    places,
    rate3,
    decay3,
    gain3,
    xq,
    xk,
    xv,
    enter,
    local,
    near,
    node3,
    msg,
    ring_y,
    edge_z,
    total,
    ring_z,
    before,
    flow_out,
    flow,
    hid,
    acc,
    load_sem,
    y_send,
    y_recv,
    e_send,
    e_recv,
    z_send,
    z_recv,
    g_send,
    g_recv,
    f_send,
    f_recv,
    ready_x,
    ready_y,
    ready_z,
    ready_edge,
):
    seq = lax.axis_index("seq")
    chan = lax.axis_index("chan")
    z, y = seq // ys, lax.rem(seq, ys)
    x, core = chan // CORES, lax.rem(chan, CORES)
    width = k_in.shape[1]
    tiles = width // LANES
    half = width // PIECES
    per = tiles // PIECES
    last_y = y == ys - 1

    loads = [
        pltpu.make_async_copy(src, dst, load_sem.at[i])
        for i, (src, dst) in enumerate(
            [
                (rate_hbm, rate),
                (res_hbm, res),
                (taps_hbm, taps),
                (k_hbm, k_in),
                (v_hbm, v_in),
                (q_hbm, q_in),
                (skip_hbm, skip),
                (places_hbm, places),
                (weights_hbm, weights),
                (w_hbm, weight),
            ]
        )
    ]
    for load in loads:
        load.start()
    pending = []

    def at(zz, yy):
        return zz * ys + yy

    def signal(sem, s, c):
        pl.semaphore_signal(sem, inc=1, device_id=(s, c), device_id_type=MESH)

    def wait_for(sem, amount):
        pl.when(amount > 0)(lambda: pl.semaphore_wait(sem, amount))

    def x_peer(e):
        return lax.rem(x + e, CHIPS) * CORES

    right = x_peer(1) + core
    left = x_peer(CHIPS - 1) + core
    sibling = x * CORES + 1 - core
    z_up = lax.rem(z + 1, zs)
    z_down = lax.rem(z + zs - 1, zs)

    barrier = pltpu.get_barrier_semaphore()
    for e in range(1, CHIPS):

        @pl.when(x + e < CHIPS)
        def _():
            for c in range(CORES):
                signal(barrier, seq, x_peer(e) + c)

    @pl.when(core == 1)
    def _():
        signal(barrier, seq, sibling)

    for e in range(1, ys):

        @pl.when(y + e < ys)
        def _():
            signal(barrier, at(z, lax.rem(y + e, ys)), chan)

    for d in range(1, zs):

        @pl.when(z + d < zs)
        def _():
            signal(barrier, at(lax.rem(z + d, zs), y), chan)

    @pl.when(last_y & (z < zs - 1))
    def _():
        for e in range(ys):
            signal(barrier, at(z_up, e), chan)

    wait_for(barrier, CORES * x + (1 - core) + y + z + jnp.where(z > 0, 1, 0))
    for d in range(1, zs):

        @pl.when(z >= d)
        def _():
            signal(ready_z.at[d - 1], at(lax.rem(z + zs - d, zs), y), chan)

    for e in range(1, ys):

        @pl.when(y >= e)
        def _():
            signal(ready_y, at(z, lax.rem(y + ys - e, ys)), chan)

    for e in range(1, CHIPS):

        @pl.when(x >= e)
        def _():
            for c in range(CORES):
                signal(ready_x, seq, x_peer(CHIPS - e) + c)

    @pl.when(core == 0)
    def _():
        signal(ready_x, seq, sibling)

    @pl.when(z > 0)
    def _():
        signal(ready_edge, at(z_down, ys - 1), chan)

    loads[0].wait()
    loads[1].wait()
    r = rate[...]
    series = r * (1.0 - r * (1 / 2) * (1.0 - r * (1 / 3) * (1.0 - r * (1 / 4) * (1.0 - r * (1 / 5) * (1.0 - r * (1 / 6))))))
    gain = res[...] * series
    decay = jnp.exp(-r)
    for m in range(MODES):
        rate3[m] = jnp.broadcast_to(r[m : m + 1], (SUBS, width))
        decay3[m] = jnp.broadcast_to(decay[m : m + 1], (SUBS, width))
        gain3[m] = jnp.broadcast_to(gain[m : m + 1], (SUBS, width))

    row = lax.broadcasted_iota(jnp.int32, (ROWS, ROWS), 0)
    col = lax.broadcasted_iota(jnp.int32, (ROWS, ROWS), 1)
    order = jnp.where(col == (row & 7) * STEPS + (row >> 3), 1.0, 0.0).astype(BF16)
    back = jnp.where(row == (col & 7) * STEPS + (col >> 3), 1.0, 0.0).astype(BF16)

    def arranged(block):
        return jnp.dot(order, block, preferred_element_type=F32).reshape(STEPS, SUBS, width)

    sub = lax.broadcasted_iota(jnp.int32, (SUBS, LANES), 0)
    sub3 = lax.broadcasted_iota(jnp.int32, (MODES, SUBS, LANES), 1)
    first = sub == 0
    subf3 = sub3.astype(F32)

    for i in (2, 3, 4, 5):
        loads[i].wait()
    xk[...] = arranged(k_in[...])
    xv[...] = arranged(v_in[...])
    xq[...] = arranged(q_in[...])

    def lags(block):
        last = jnp.where(first, 0.0, pltpu.roll(block[STEPS - 1], 1, 0))
        last_but_one = jnp.where(first, 0.0, pltpu.roll(block[STEPS - 2], 1, 0))
        return lagged(block, last, last_but_one)

    for l in range(tiles):
        cols = slice(l * LANES, (l + 1) * LANES)
        kb, vb = xk[:, :, cols], xv[:, :, cols]
        g = tapped(taps, 1, cols, kb, *lags(kb)) * tapped(taps, 2, cols, vb, *lags(vb))
        g = jnp.concatenate([jnp.where(first[None], 0.0, g[:2]), g[2:]], axis=0)
        local[:, :, cols] = g
        a = decay3[:, :, cols]
        state = jnp.broadcast_to(g[0][None], a.shape)
        for j in range(1, STEPS):
            state = state * a + g[j][None]
        step = a
        for _ in range(4):
            step = step * step
        for reach in (1, 2, 4):
            state = state + jnp.where(sub3 >= reach, step, 0.0) * pltpu.roll(state, reach, 1)
            step = step * step
        enter[:, :, cols] = jnp.where(sub3 >= 1, pltpu.roll(state, 1, 1), 0.0)
        for m in range(MODES):
            msg[l, m : m + 1, :] = state[m, SUBS - 1 : SUBS, :]
        for i, block in enumerate((xk, xv, xq)):
            for n, (j, s) in enumerate(((0, 0), (1, 0), (STEPS - 2, SUBS - 1), (STEPS - 1, SUBS - 1))):
                line = MODES + 4 * i + n
                msg[l, line : line + 1, :] = block[j, s : s + 1, cols]
        msg[l, MODES + 12 : MODES + 16, :] = jnp.zeros((4, LANES), F32)

    wait_for(ready_x, CORES * (CHIPS - 1 - x) + core)
    wait_for(ready_y, ys - 1 - y)
    y_copies = []
    for e in range(1, ys):
        to = lax.rem(y + e, ys)
        copy = pltpu.make_async_remote_copy(
            msg.at[to], ring_y.at[y], y_send.at[e - 1], y_recv.at[e - 1],
            device_id=(at(z, to), chan), device_id_type=MESH,
        )
        copy.start()
        pending.append(copy.wait_send)
        y_copies.append(copy)
    ring_y[y] = msg[y]

    def send(index, slot, piece, to_slot, to):
        copy = pltpu.make_async_remote_copy(
            hid.at[slot, piece], hid.at[to_slot, piece], g_send.at[index], g_recv.at[index],
            device_id=(seq, to), device_id_type=MESH,
        )
        copy.start()
        pending.append(copy.wait_send)
        return copy

    loads[6].wait()
    own_sib, own_right, own_left = {}, {}, {}
    for p in range(PIECES):
        for i in range(per):
            l = p * per + i
            cols = slice(l * LANES, (l + 1) * LANES)
            r3, a, w = rate3[:, :, cols], decay3[:, :, cols], gain3[:, :, cols]
            close = w * jnp.exp(-subf3 * r3)
            a8 = a * a
            a8 = a8 * a8
            a8 = a8 * a8
            near[0:SUBS, cols] = tree_sum(close)
            near[SUBS : 2 * SUBS, cols] = tree_sum(close * a8)
            g = local[:, :, cols]
            out = g * skip[0:1, cols]
            for d in range(STEPS):
                add = g[: STEPS - d] * near[d : d + 1, cols][None]
                out = out + add if d == 0 else jnp.concatenate([out[:d], out[d:] + add], axis=0)
            qb = xq[:, :, cols]
            qb = tapped(taps, 0, cols, qb, *lags(qb))
            state = w * a * enter[:, :, cols]
            own, factor = [], []
            for j in range(STEPS):
                line = qb[j] * (out[j] + tree_sum(state))
                if j < STEPS - 1:
                    state = state * a
                own.append(jnp.where(first, 0.0, line) if j < 2 else line)
                factor.append(jnp.where(first, 1.0, qb[j]) if j < 2 else qb[j])
            to = slice(i * LANES, (i + 1) * LANES)
            hid[0, p, 0, :, to] = jnp.concatenate(own, axis=0).astype(BF16)
            hid[0, p, 1, :, to] = jnp.concatenate(factor, axis=0).astype(BF16)
        own_right[p] = send(p, 0, p, 6, right)
        own_sib[p] = send(2 + p, 0, p, 1, sibling)
    for p in (1, 0):
        own_left[p] = send(4 + p, 0, p, 2, left)

    edges = [
        pltpu.make_async_remote_copy(
            msg.at[e, pl.ds(MODES, 16)], edge_z, e_send.at[e], e_recv,
            device_id=(at(z_up, e), chan), device_id_type=MESH,
        )
        for e in range(ys)
    ]

    @pl.when(last_y & (z < zs - 1))
    def _():
        pl.semaphore_wait(ready_edge, ys)
        for copy in edges:
            copy.start()

    @pending.append
    def _():
        @pl.when(last_y & (z < zs - 1))
        def _():
            for copy in edges:
                copy.wait_send()

    mine = pl.ds(pl.multiple_of(y * LANES, LANES), LANES)
    r = rate[:, mine]
    a126 = jnp.exp(-(ROWS - 2.0) * r)
    a127 = jnp.exp(-(ROWS - 1.0) * r)
    a128 = jnp.exp(-float(ROWS) * r)
    loads[7].wait()
    for m in range(MODES):
        node3[m] = gain3[m, 0:1, mine] * jnp.exp(-(places[...] + 1.0) * rate[m : m + 1, mine])

    @pl.when(z == 0)
    def _():
        edge_z[...] = jnp.zeros_like(edge_z)

    @pl.when(z > 0)
    def _():
        edges[0].wait_recv()

    for copy in y_copies:
        copy.wait_recv()
    ends = edge_z[...]
    start = jnp.zeros_like(r)
    starts, heads = [], []
    for e in range(ys):
        now = ring_y[e, MODES : MODES + 16, :]
        k0, k1, v0, v1, q0, q1 = (now[i : i + 1] for i in (0, 1, 4, 5, 8, 9))
        k126, k127, v126, v127, q126, q127 = (ends[i : i + 1] for i in (2, 3, 6, 7, 10, 11))
        g0 = tapped(taps, 1, mine, k0, k127, k126) * tapped(taps, 2, mine, v0, v127, v126)
        g1 = tapped(taps, 1, mine, k1, k0, k127) * tapped(taps, 2, mine, v1, v0, v127)
        s0 = tapped(taps, 0, mine, q0, q127, q126)
        s1 = tapped(taps, 0, mine, q1, q0, q127)
        heads.append((g0, g1, s0, s1))
        starts.append(start)
        start = start * a128 + (ring_y[e, 0:MODES, :] + a127 * g0 + a126 * g1)
        ends = now
    total[...] = start

    z_copies = []
    for d in range(1, zs):
        copy = pltpu.make_async_remote_copy(
            total, ring_z.at[d - 1], z_send.at[d - 1], z_recv.at[d - 1],
            device_id=(at(lax.rem(z + d, zs), y), chan), device_id_type=MESH,
        )
        z_copies.append(copy)

        @pl.when(z + d < zs)
        def _():
            pl.semaphore_wait(ready_z.at[d - 1], 1)
            copy.start()

        pending.append(functools.partial(pl.when(z + d < zs), copy.wait_send))

    own_right[0].wait_recv()
    on_right = send(6, 6, 0, 4, right)
    own_left[1].wait_recv()
    on_left = send(7, 2, 1, 4, left)
    sib = {(7, 0): send(8, 6, 0, 7, sibling), (3, 1): send(11, 2, 1, 3, sibling)}

    before[...] = jnp.zeros_like(before)
    for d in range(1, zs):

        @pl.when(z >= d)
        def _():
            z_copies[d - 1].wait_recv()
            before[...] += jnp.exp(-float(ROWS * ys * (d - 1)) * rate[:, mine]) * ring_z[d - 1]

    sums = before[...]
    rows = lax.broadcasted_iota(jnp.int32, (STEPS, LANES), 0)
    near0, near1, direct = near[0:1, mine], near[1:2, mine], skip[0:1, mine]
    up1, up2 = jnp.exp(r), jnp.exp(2.0 * r)
    for e in range(ys):
        g0, g1, s0, s1 = heads[e]
        entering = sums + starts[e]
        later = entering + up1 * g0 + up2 * g1
        values = jnp.zeros((STEPS, LANES), F32)
        for m in range(MODES):
            values += node3[m] * jnp.where(rows < NODES, later[m : m + 1], entering[m : m + 1])
        h0 = s0 * (values[NODES : NODES + 1] + (near0 + direct) * g0)
        h1 = s1 * (values[NODES + 1 : NODES + 2] + near1 * g0 + (near0 + direct) * g1)
        values = jnp.where(rows == NODES, h0, jnp.where(rows == NODES + 1, h1, values))
        flow_out[e] = values.astype(BF16)
        sums = sums * a128

    f_copies = {}
    for ey in range(ys):
        to_y = lax.rem(y + ey, ys)
        for ex in range(CHIPS):
            for ec in range(CORES):
                if ex == ec == ey == 0:
                    continue
                slot = ex * CORES + ec
                to_c = x_peer(CHIPS - ex) + (core if ec == 0 else 1 - core)
                copy = pltpu.make_async_remote_copy(
                    flow_out.at[to_y], flow.at[slot, y], f_send.at[slot, ey], f_recv.at[slot, ey],
                    device_id=(at(z, to_y), to_c), device_id_type=MESH,
                )
                copy.start()
                pending.append(copy.wait_send)
                f_copies[slot, ey] = copy
    flow[0, y] = flow_out[y]

    own_right[1].wait_recv()
    sib[7, 1] = send(9, 6, 1, 7, sibling)
    own_left[0].wait_recv()
    sib[3, 0] = send(10, 2, 0, 3, sibling)
    on_right.wait_recv()
    sib[5, 0] = send(12, 4, 0, 5, sibling)
    on_left.wait_recv()
    sib[5, 1] = send(13, 4, 1, 5, sibling)

    loads[8].wait()
    loads[9].wait()
    for n, slot in enumerate((0, 1, 6, 2, 7, 3, 4, 5)):
        for p in range(PIECES):
            if slot == 1:
                own_sib[p].wait_recv()
            if slot in (3, 5, 7):
                sib[slot, p].wait_recv()
        for ey in range(ys):
            if slot or ey:
                f_copies[slot, ey].wait_recv()
        values = jnp.concatenate([flow[slot, l] for l in range(tiles)], axis=1)
        entering = jnp.dot(
            weights[...], jnp.concatenate([values, values], axis=0), preferred_element_type=F32
        )
        blocks = []
        for p in range(PIECES):
            own, factor = hid[slot, p, 0].astype(F32), hid[slot, p, 1].astype(F32)
            blocks.append((own + factor * entering[:, p * half : (p + 1) * half]).astype(BF16))
        owner = x_peer(slot // CORES) + (core if slot % CORES == 0 else 1 - core)
        wrows = weight[pl.ds(pl.multiple_of(owner * width, width), width), :]
        part = jnp.dot(jnp.concatenate(blocks, axis=1), wrows, preferred_element_type=F32)
        if n:
            part = part + acc[...]
        acc[...] = part

    mixed = acc[...].astype(BF16)
    out_ref[...] = jnp.dot(back, mixed, preferred_element_type=F32).astype(BF16)

    for wait in pending:
        wait()


def interpolation():
    turn = np.pi * (2 * np.arange(NODES) + 1) / (2 * NODES)
    places = ((ROWS - 1) / 2 * (1 - np.cos(turn))).astype(np.float32)
    at = places.astype(np.float64)
    share = np.array([1 / np.prod(at[i] - np.delete(at, i)) for i in range(NODES)])
    weights = np.zeros((ROWS, STEPS))
    for t in range(2, ROWS):
        part = share / (t - at)
        weights[t, :NODES] = part / part.sum()
    weights[0, NODES] = weights[1, NODES + 1] = 1
    weights = weights.reshape(SUBS, STEPS, STEPS).swapaxes(0, 1).reshape(ROWS, STEPS)
    high = weights.astype(ml_dtypes.bfloat16)
    low = (weights - high.astype(np.float64)).astype(ml_dtypes.bfloat16)
    places = np.broadcast_to(np.append(places, [0, 1]).astype(np.float32)[:, None], (STEPS, LANES))
    return np.concatenate([high, low], axis=1), np.ascontiguousarray(places)


def per_device(zs, ys, query, key, value, short_taps, residue, rate, skip, out_weight):
    width = query.shape[1]
    tiles = width // LANES
    weights, places = interpolation()
    modes = pltpu.VMEM((MODES, width), F32)
    tile = pltpu.VMEM((MODES, LANES), F32)
    table = pltpu.VMEM((MODES, SUBS, width), F32)
    block = pltpu.VMEM((STEPS, SUBS, width), F32)
    dma = pltpu.SemaphoreType.DMA
    regular = pltpu.SemaphoreType.REGULAR
    scratch = [
        pltpu.VMEM((ROWS, width), BF16),
        pltpu.VMEM((ROWS, width), BF16),
        pltpu.VMEM((ROWS, width), BF16),
        pltpu.VMEM(short_taps.shape, F32),
        modes,
        modes,
        pltpu.VMEM((1, width), F32),
        pltpu.VMEM(out_weight.shape, BF16),
        pltpu.VMEM(weights.shape, BF16),
        pltpu.VMEM(places.shape, F32),
        table,
        table,
        table,
        block,
        block,
        block,
        table,
        block,
        pltpu.VMEM((STEPS, width), F32),
        pltpu.VMEM((MODES, STEPS, LANES), F32),
        pltpu.VMEM((tiles, MODES + 16, LANES), F32),
        pltpu.VMEM((ys, MODES + 16, LANES), F32),
        pltpu.VMEM((16, LANES), F32),
        tile,
        pltpu.VMEM((zs - 1, MODES, LANES), F32),
        tile,
        pltpu.VMEM((ys, STEPS, LANES), BF16),
        pltpu.VMEM((CHIPS * CORES, tiles, STEPS, LANES), BF16),
        pltpu.VMEM((CHIPS * CORES, PIECES, 2, ROWS, width // PIECES), BF16),
        pltpu.VMEM((ROWS, width), F32),
        dma((10,)),
        dma((ys - 1,)),
        dma((ys - 1,)),
        dma((ys,)),
        dma,
        dma((zs - 1,)),
        dma((zs - 1,)),
        dma((14,)),
        dma((14,)),
        dma((CHIPS * CORES, ys)),
        dma((CHIPS * CORES, ys)),
        regular,
        regular,
        regular((zs - 1,)),
        regular,
    ]
    return pl.pallas_call(
        functools.partial(kernel, zs, ys),
        out_shape=jax.ShapeDtypeStruct((ROWS, width), BF16),
        in_specs=[pl.BlockSpec(memory_space=pl.ANY)] * 10,
        out_specs=pl.BlockSpec(memory_space=pltpu.VMEM),
        scratch_shapes=scratch,
        compiler_params=pltpu.CompilerParams(
            collective_id=0, has_side_effects=True, vmem_limit_bytes=56 * 1024 * 1024
        ),
    )(
        query,
        key,
        value,
        short_taps,
        residue.T,
        rate.T,
        skip[None, :],
        out_weight,
        jnp.asarray(weights),
        jnp.asarray(places),
    )


def solution(mesh, ys=4):
    placed = (
        P("seq", "chan"),
        P("seq", "chan"),
        P("seq", "chan"),
        P(None, None, "chan"),
        P("chan", None),
        P("chan", None),
        P("chan"),
        P(None, "chan"),
    )
    return jax.shard_map(
        functools.partial(per_device, mesh.shape["seq"] // ys, ys),
        mesh=mesh,
        in_specs=placed,
        out_specs=P("seq", "chan"),
        check_vma=False,
    )
```

```python
import functools

import jax
import jax.numpy as jnp
import ml_dtypes
import numpy as np
from jax import lax
from jax.experimental import pallas as pl
from jax.experimental.pallas import tpu as pltpu
from jax.sharding import PartitionSpec as P

MESH = pl.DeviceIdType.MESH
F32 = jnp.float32
BF16 = jnp.bfloat16
MODES = 16
STEPS = 16
SUBS = 8
ROWS = STEPS * SUBS
LANES = 128
CHIPS = 4
CORES = 2
PIECES = 2
FACTOR, OWN = 0, 1
ROUTES = (
    (0, 6, "right"),
    (0, 2, "left"),
    (0, 1, "sibling"),
    (6, 4, "right"),
    (2, 4, "left"),
    (6, 7, "sibling"),
    (2, 3, "sibling"),
    (4, 5, "sibling"),
)
NODES = STEPS - 2


def tree_sum(array):
    while array.shape[0] > 1:
        half = array.shape[0] // 2
        array = array[:half] + array[half:]
    return array[0]


def lagged(block, last, last_but_one):
    one = jnp.concatenate([last[None], block[:-1]], axis=0)
    two = jnp.concatenate([last_but_one[None], one[:-1]], axis=0)
    return one, two


def tapped(taps, which, cols, now, one, two):
    return (
        taps[which, 0:1, cols] * now + taps[which, 1:2, cols] * one + taps[which, 2:3, cols] * two
    )


def kernel(
    zs,
    ys,
    q_hbm,
    k_hbm,
    v_hbm,
    taps_hbm,
    res_hbm,
    rate_hbm,
    skip_hbm,
    w_hbm,
    weights_hbm,
    places_hbm,
    out_ref,
    q_in,
    k_in,
    v_in,
    taps,
    res,
    rate,
    skip,
    weight,
    weights,
    places,
    rate3,
    decay3,
    gain3,
    xq,
    xk,
    xv,
    enter,
    local,
    query,
    near,
    node3,
    msg,
    ring_y,
    edge_z,
    total,
    ring_z,
    before,
    flow_out,
    flow,
    hid,
    acc,
    load_sem,
    y_send,
    y_recv,
    e_send,
    e_recv,
    z_send,
    z_recv,
    g_send,
    g_recv,
    f_send,
    f_recv,
    ready_x,
    ready_y,
    ready_z,
    ready_edge,
):
    seq = lax.axis_index("seq")
    chan = lax.axis_index("chan")
    z, y = seq // ys, lax.rem(seq, ys)
    x, core = chan // CORES, lax.rem(chan, CORES)
    width = k_in.shape[1]
    tiles = width // LANES
    half = width // PIECES
    per = tiles // PIECES
    last_y = y == ys - 1

    loads = [
        pltpu.make_async_copy(src, dst, load_sem.at[i])
        for i, (src, dst) in enumerate(
            [
                (rate_hbm, rate),
                (res_hbm, res),
                (taps_hbm, taps),
                (k_hbm, k_in),
                (v_hbm, v_in),
                (q_hbm, q_in),
                (skip_hbm, skip),
                (places_hbm, places),
                (weights_hbm, weights),
                (w_hbm, weight),
            ]
        )
    ]
    for load in loads:
        load.start()
    pending = []

    def at(zz, yy):
        return zz * ys + yy

    def signal(sem, s, c):
        pl.semaphore_signal(sem, inc=1, device_id=(s, c), device_id_type=MESH)

    def wait_for(sem, amount):
        pl.when(amount > 0)(lambda: pl.semaphore_wait(sem, amount))

    def x_peer(e):
        return lax.rem(x + e, CHIPS) * CORES

    right = x_peer(1) + core
    left = x_peer(CHIPS - 1) + core
    sibling = x * CORES + 1 - core
    z_up = lax.rem(z + 1, zs)
    z_down = lax.rem(z + zs - 1, zs)

    hub = zs // 2
    barrier = pltpu.get_barrier_semaphore()
    for e in range(1, CHIPS):

        @pl.when(x + e < CHIPS)
        def _():
            for c in range(CORES):
                signal(barrier, seq, x_peer(e) + c)

    @pl.when(core == 1)
    def _():
        signal(barrier, seq, sibling)

    for e in range(1, ys):

        @pl.when(y + e < ys)
        def _():
            signal(barrier, at(z, lax.rem(y + e, ys)), chan)

    for d in range(1, zs):

        @pl.when((z + d < zs) & (z < hub))
        def _():
            signal(barrier, at(lax.rem(z + d, zs), y), chan)

    @pl.when(last_y & (z < hub))
    def _():
        for e in range(ys):
            signal(barrier, at(z_up, e), chan)

    @pl.when(z > hub)
    def _():
        signal(barrier, at(z_down, ys - 1), chan)

    wait_for(
        barrier,
        CORES * x
        + (1 - core)
        + y
        + jnp.minimum(z, hub)
        + jnp.where((z > 0) & (z <= hub), 1, 0)
        + jnp.where(last_y & (z >= hub) & (z < zs - 1), ys, 0),
    )
    for d in range(1, zs):

        @pl.when((z >= d) & (z - d < hub))
        def _():
            signal(ready_z.at[d - 1], at(lax.rem(z + zs - d, zs), y), chan)

    for e in range(1, ys):

        @pl.when(y >= e)
        def _():
            signal(ready_y, at(z, lax.rem(y + ys - e, ys)), chan)

    for e in range(1, CHIPS):

        @pl.when(x >= e)
        def _():
            for c in range(CORES):
                signal(ready_x, seq, x_peer(CHIPS - e) + c)

    @pl.when(core == 0)
    def _():
        signal(ready_x, seq, sibling)

    @pl.when((z > 0) & (z <= hub))
    def _():
        signal(ready_edge, at(z_down, ys - 1), chan)

    loads[0].wait()
    loads[1].wait()
    r = rate[...]
    series = r * (1.0 - r * (1 / 2) * (1.0 - r * (1 / 3) * (1.0 - r * (1 / 4) * (1.0 - r * (1 / 5) * (1.0 - r * (1 / 6))))))
    gain = res[...] * series
    decay = jnp.exp(-r)
    for m in range(MODES):
        rate3[m] = jnp.broadcast_to(r[m : m + 1], (SUBS, width))
        decay3[m] = jnp.broadcast_to(decay[m : m + 1], (SUBS, width))
        gain3[m] = jnp.broadcast_to(gain[m : m + 1], (SUBS, width))

    row = lax.broadcasted_iota(jnp.int32, (ROWS, ROWS), 0)
    col = lax.broadcasted_iota(jnp.int32, (ROWS, ROWS), 1)
    order = jnp.where(col == (row & 7) * STEPS + (row >> 3), 1.0, 0.0).astype(BF16)
    back = jnp.where(row == (col & 7) * STEPS + (col >> 3), 1.0, 0.0).astype(BF16)

    def arranged(block):
        return jnp.dot(order, block, preferred_element_type=F32).reshape(STEPS, SUBS, width)

    sub = lax.broadcasted_iota(jnp.int32, (SUBS, LANES), 0)
    sub3 = lax.broadcasted_iota(jnp.int32, (MODES, SUBS, LANES), 1)
    first = sub == 0
    subf3 = sub3.astype(F32)

    for i in (2, 3, 4, 5):
        loads[i].wait()
    xk[...] = arranged(k_in[...])
    xv[...] = arranged(v_in[...])
    xq[...] = arranged(q_in[...])

    def lags(block):
        last = jnp.where(first, 0.0, pltpu.roll(block[STEPS - 1], 1, 0))
        last_but_one = jnp.where(first, 0.0, pltpu.roll(block[STEPS - 2], 1, 0))
        return lagged(block, last, last_but_one)

    for l in range(tiles):
        cols = slice(l * LANES, (l + 1) * LANES)
        qb = xq[:, :, cols]
        qb = tapped(taps, 0, cols, qb, *lags(qb))
        query[:, :, cols] = qb
        qb = jnp.concatenate([jnp.where(first[None], 1.0, qb[:2]), qb[2:]], axis=0)
        to = slice(l % per * LANES, (l % per + 1) * LANES)
        hid[0, FACTOR, l // per, :, to] = qb.reshape(ROWS, LANES).astype(BF16)
        kb, vb = xk[:, :, cols], xv[:, :, cols]
        g = tapped(taps, 1, cols, kb, *lags(kb)) * tapped(taps, 2, cols, vb, *lags(vb))
        g = jnp.concatenate([jnp.where(first[None], 0.0, g[:2]), g[2:]], axis=0)
        local[:, :, cols] = g
        a = decay3[:, :, cols]
        state = jnp.broadcast_to(g[0][None], a.shape)
        for j in range(1, STEPS):
            state = state * a + g[j][None]
        step = a
        for _ in range(4):
            step = step * step
        for reach in (1, 2, 4):
            state = state + jnp.where(sub3 >= reach, step, 0.0) * pltpu.roll(state, reach, 1)
            step = step * step
        enter[:, :, cols] = jnp.where(sub3 >= 1, pltpu.roll(state, 1, 1), 0.0)
        for m in range(MODES):
            msg[l, m : m + 1, :] = state[m, SUBS - 1 : SUBS, :]
        for i, block in enumerate((xk, xv, xq)):
            for n, (j, s) in enumerate(((0, 0), (1, 0), (STEPS - 2, SUBS - 1), (STEPS - 1, SUBS - 1))):
                line = MODES + 4 * i + n
                msg[l, line : line + 1, :] = block[j, s : s + 1, cols]
        msg[l, MODES + 12 : MODES + 16, :] = jnp.zeros((4, LANES), F32)

    wait_for(ready_x, CORES * (CHIPS - 1 - x) + core)
    wait_for(ready_y, ys - 1 - y)
    y_copies = []
    for e in range(1, ys):
        to = lax.rem(y + e, ys)
        copy = pltpu.make_async_remote_copy(
            msg.at[to], ring_y.at[y], y_send.at[e - 1], y_recv.at[e - 1],
            device_id=(at(z, to), chan), device_id_type=MESH,
        )
        copy.start()
        pending.append(copy.wait_send)
        y_copies.append(copy)
    ring_y[y] = msg[y]

    g_copies = {}

    def send(route, kind, piece):
        slot, to_slot, to = ROUTES[route]
        to = {"right": right, "left": left, "sibling": sibling}[to]
        copy = pltpu.make_async_remote_copy(
            hid.at[slot, kind, piece],
            hid.at[to_slot, kind, piece],
            g_send.at[route, kind, piece],
            g_recv.at[route, kind, piece],
            device_id=(seq, to),
            device_id_type=MESH,
        )
        copy.start()
        pending.append(copy.wait_send)
        g_copies[route, kind, piece] = copy

    def arrived(route, kind, piece):
        g_copies[route, kind, piece].wait_recv()

    for kind in (FACTOR,):
        for p in range(PIECES):
            for route, piece in ((0, p), (1, PIECES - 1 - p), (2, p)):
                send(route, kind, piece)

    loads[6].wait()
    for p in range(PIECES):
        for i in range(per):
            l = p * per + i
            cols = slice(l * LANES, (l + 1) * LANES)
            r3, a, w = rate3[:, :, cols], decay3[:, :, cols], gain3[:, :, cols]
            close = w * jnp.exp(-subf3 * r3)
            a8 = a * a
            a8 = a8 * a8
            a8 = a8 * a8
            near[0:SUBS, cols] = tree_sum(close)
            near[SUBS : 2 * SUBS, cols] = tree_sum(close * a8)
            g = local[:, :, cols]
            out = g * skip[0:1, cols]
            for d in range(STEPS):
                add = g[: STEPS - d] * near[d : d + 1, cols][None]
                out = out + add if d == 0 else jnp.concatenate([out[:d], out[d:] + add], axis=0)
            state = w * a * enter[:, :, cols]
            own = []
            for j in range(STEPS):
                line = query[j, :, cols] * (out[j] + tree_sum(state))
                if j < STEPS - 1:
                    state = state * a
                own.append(jnp.where(first, 0.0, line) if j < 2 else line)
            to = slice(i * LANES, (i + 1) * LANES)
            hid[0, OWN, p, :, to] = jnp.concatenate(own, axis=0).astype(BF16)
        send(0, OWN, p)
        send(2, OWN, p)
    for p in reversed(range(PIECES)):
        send(1, OWN, p)

    edges = [
        pltpu.make_async_remote_copy(
            msg.at[e, pl.ds(MODES, 16)], edge_z, e_send.at[e], e_recv,
            device_id=(at(z_up, e), chan), device_id_type=MESH,
        )
        for e in range(ys)
    ]

    @pl.when(last_y & (z < hub))
    def _():
        pl.semaphore_wait(ready_edge, ys)

    @pl.when(last_y & (z < zs - 1))
    def _():
        for copy in edges:
            copy.start()

    @pending.append
    def _():
        @pl.when(last_y & (z < zs - 1))
        def _():
            for copy in edges:
                copy.wait_send()

    mine = pl.ds(pl.multiple_of(y * LANES, LANES), LANES)
    r = rate[:, mine]
    a126 = jnp.exp(-(ROWS - 2.0) * r)
    a127 = jnp.exp(-(ROWS - 1.0) * r)
    a128 = jnp.exp(-float(ROWS) * r)
    loads[7].wait()
    for m in range(MODES):
        node3[m] = gain3[m, 0:1, mine] * jnp.exp(-(places[...] + 1.0) * rate[m : m + 1, mine])

    @pl.when(z == 0)
    def _():
        edge_z[...] = jnp.zeros_like(edge_z)

    @pl.when(z > 0)
    def _():
        edges[0].wait_recv()

    for copy in y_copies:
        copy.wait_recv()
    ends = edge_z[...]
    start = jnp.zeros_like(r)
    starts, heads = [], []
    for e in range(ys):
        now = ring_y[e, MODES : MODES + 16, :]
        k0, k1, v0, v1, q0, q1 = (now[i : i + 1] for i in (0, 1, 4, 5, 8, 9))
        k126, k127, v126, v127, q126, q127 = (ends[i : i + 1] for i in (2, 3, 6, 7, 10, 11))
        g0 = tapped(taps, 1, mine, k0, k127, k126) * tapped(taps, 2, mine, v0, v127, v126)
        g1 = tapped(taps, 1, mine, k1, k0, k127) * tapped(taps, 2, mine, v1, v0, v127)
        s0 = tapped(taps, 0, mine, q0, q127, q126)
        s1 = tapped(taps, 0, mine, q1, q0, q127)
        heads.append((g0, g1, s0, s1))
        starts.append(start)
        start = start * a128 + (ring_y[e, 0:MODES, :] + a127 * g0 + a126 * g1)
        ends = now
    total[...] = start

    z_copies = []
    for d in range(1, zs):
        copy = pltpu.make_async_remote_copy(
            total, ring_z.at[d - 1], z_send.at[d - 1], z_recv.at[d - 1],
            device_id=(at(lax.rem(z + d, zs), y), chan), device_id_type=MESH,
        )
        z_copies.append(copy)

    @pl.when(z == hub - 1)
    def _():
        for d in range(1, zs - hub + 1):
            pl.semaphore_wait(ready_z.at[d - 1], 1)

    for d in range(1, zs - hub + 1):
        pl.when(z == hub - 1 + d)(z_copies[d - 1].wait_recv)
    for d in range(1, zs):

        @pl.when(z + d < zs)
        def _():
            @pl.when(z < hub - 1)
            def _():
                pl.semaphore_wait(ready_z.at[d - 1], 1)

            z_copies[d - 1].start()

        pending.append(functools.partial(pl.when(z + d < zs), z_copies[d - 1].wait_send))

    arrived(0, FACTOR, 0)
    send(3, FACTOR, 0)
    arrived(1, FACTOR, 1)
    send(4, FACTOR, 1)

    before[...] = jnp.zeros_like(before)
    for d in range(1, zs):

        @pl.when(z >= d)
        def _():
            pl.when(z - d != hub - 1)(z_copies[d - 1].wait_recv)
            before[...] += jnp.exp(-float(ROWS * ys * (d - 1)) * rate[:, mine]) * ring_z[d - 1]

    sums = before[...]
    rows = lax.broadcasted_iota(jnp.int32, (STEPS, LANES), 0)
    near0, near1, direct = near[0:1, mine], near[1:2, mine], skip[0:1, mine]
    up1, up2 = jnp.exp(r), jnp.exp(2.0 * r)
    for e in range(ys):
        g0, g1, s0, s1 = heads[e]
        entering = sums + starts[e]
        later = entering + up1 * g0 + up2 * g1
        values = jnp.zeros((STEPS, LANES), F32)
        for m in range(MODES):
            values += node3[m] * jnp.where(rows < NODES, later[m : m + 1], entering[m : m + 1])
        h0 = s0 * (values[NODES : NODES + 1] + (near0 + direct) * g0)
        h1 = s1 * (values[NODES + 1 : NODES + 2] + near1 * g0 + (near0 + direct) * g1)
        values = jnp.where(rows == NODES, h0, jnp.where(rows == NODES + 1, h1, values))
        flow_out[e] = values.astype(BF16)
        sums = sums * a128

    f_copies = {}
    for ey in range(ys):
        to_y = lax.rem(y + ey, ys)
        for ex in range(CHIPS):
            for ec in range(CORES):
                if ex == ec == ey == 0:
                    continue
                slot = ex * CORES + ec
                to_c = x_peer(CHIPS - ex) + (core if ec == 0 else 1 - core)
                copy = pltpu.make_async_remote_copy(
                    flow_out.at[to_y], flow.at[slot, y], f_send.at[slot, ey], f_recv.at[slot, ey],
                    device_id=(at(z, to_y), to_c), device_id_type=MESH,
                )
                copy.start()
                pending.append(copy.wait_send)
                f_copies[slot, ey] = copy
    flow[0, y] = flow_out[y]

    arrived(0, OWN, 0)
    send(3, OWN, 0)
    arrived(1, OWN, 1)
    send(4, OWN, 1)
    send(5, FACTOR, 0)
    send(6, FACTOR, 1)
    send(5, OWN, 0)
    send(6, OWN, 1)
    for kind in (FACTOR, OWN):
        arrived(0, kind, 1)
        send(5, kind, 1)
        arrived(1, kind, 0)
        send(6, kind, 0)
    for kind in (FACTOR, OWN):
        for p in range(PIECES):
            arrived(3 + p, kind, p)
            send(7, kind, p)

    loads[8].wait()
    loads[9].wait()
    for n, slot in enumerate((0, 1, 6, 2, 7, 3, 4, 5)):
        if slot % CORES:
            for kind in (FACTOR, OWN):
                for p in range(PIECES):
                    arrived({1: 2, 7: 5, 3: 6, 5: 7}[slot], kind, p)
        for ey in range(ys):
            if slot or ey:
                f_copies[slot, ey].wait_recv()
        values = jnp.concatenate([flow[slot, l] for l in range(tiles)], axis=1)
        entering = jnp.dot(
            weights[...], jnp.concatenate([values, values], axis=0), preferred_element_type=F32
        )
        blocks = []
        for p in range(PIECES):
            own, factor = hid[slot, OWN, p].astype(F32), hid[slot, FACTOR, p].astype(F32)
            blocks.append((own + factor * entering[:, p * half : (p + 1) * half]).astype(BF16))
        owner = x_peer(slot // CORES) + (core if slot % CORES == 0 else 1 - core)
        wrows = weight[pl.ds(pl.multiple_of(owner * width, width), width), :]
        part = jnp.dot(jnp.concatenate(blocks, axis=1), wrows, preferred_element_type=F32)
        if n:
            part = part + acc[...]
        acc[...] = part

    mixed = acc[...].astype(BF16)
    out_ref[...] = jnp.dot(back, mixed, preferred_element_type=F32).astype(BF16)

    for wait in pending:
        wait()


def interpolation():
    turn = np.pi * (2 * np.arange(NODES) + 1) / (2 * NODES)
    places = ((ROWS - 1) / 2 * (1 - np.cos(turn))).astype(np.float32)
    at = places.astype(np.float64)
    share = np.array([1 / np.prod(at[i] - np.delete(at, i)) for i in range(NODES)])
    weights = np.zeros((ROWS, STEPS))
    for t in range(2, ROWS):
        part = share / (t - at)
        weights[t, :NODES] = part / part.sum()
    weights[0, NODES] = weights[1, NODES + 1] = 1
    weights = weights.reshape(SUBS, STEPS, STEPS).swapaxes(0, 1).reshape(ROWS, STEPS)
    high = weights.astype(ml_dtypes.bfloat16)
    low = (weights - high.astype(np.float64)).astype(ml_dtypes.bfloat16)
    places = np.broadcast_to(np.append(places, [0, 1]).astype(np.float32)[:, None], (STEPS, LANES))
    return np.concatenate([high, low], axis=1), np.ascontiguousarray(places)


def per_device(zs, ys, query, key, value, short_taps, residue, rate, skip, out_weight):
    width = query.shape[1]
    tiles = width // LANES
    weights, places = interpolation()
    modes = pltpu.VMEM((MODES, width), F32)
    tile = pltpu.VMEM((MODES, LANES), F32)
    table = pltpu.VMEM((MODES, SUBS, width), F32)
    block = pltpu.VMEM((STEPS, SUBS, width), F32)
    dma = pltpu.SemaphoreType.DMA
    regular = pltpu.SemaphoreType.REGULAR
    scratch = [
        pltpu.VMEM((ROWS, width), BF16),
        pltpu.VMEM((ROWS, width), BF16),
        pltpu.VMEM((ROWS, width), BF16),
        pltpu.VMEM(short_taps.shape, F32),
        modes,
        modes,
        pltpu.VMEM((1, width), F32),
        pltpu.VMEM(out_weight.shape, BF16),
        pltpu.VMEM(weights.shape, BF16),
        pltpu.VMEM(places.shape, F32),
        table,
        table,
        table,
        block,
        block,
        block,
        table,
        block,
        block,
        pltpu.VMEM((STEPS, width), F32),
        pltpu.VMEM((MODES, STEPS, LANES), F32),
        pltpu.VMEM((tiles, MODES + 16, LANES), F32),
        pltpu.VMEM((ys, MODES + 16, LANES), F32),
        pltpu.VMEM((16, LANES), F32),
        tile,
        pltpu.VMEM((zs - 1, MODES, LANES), F32),
        tile,
        pltpu.VMEM((ys, STEPS, LANES), BF16),
        pltpu.VMEM((CHIPS * CORES, tiles, STEPS, LANES), BF16),
        pltpu.VMEM((CHIPS * CORES, 2, PIECES, ROWS, width // PIECES), BF16),
        pltpu.VMEM((ROWS, width), F32),
        dma((10,)),
        dma((ys - 1,)),
        dma((ys - 1,)),
        dma((ys,)),
        dma,
        dma((zs - 1,)),
        dma((zs - 1,)),
        dma((len(ROUTES), 2, PIECES)),
        dma((len(ROUTES), 2, PIECES)),
        dma((CHIPS * CORES, ys)),
        dma((CHIPS * CORES, ys)),
        regular,
        regular,
        regular((zs - 1,)),
        regular,
    ]
    return pl.pallas_call(
        functools.partial(kernel, zs, ys),
        out_shape=jax.ShapeDtypeStruct((ROWS, width), BF16),
        in_specs=[pl.BlockSpec(memory_space=pl.ANY)] * 10,
        out_specs=pl.BlockSpec(memory_space=pltpu.VMEM),
        scratch_shapes=scratch,
        compiler_params=pltpu.CompilerParams(
            collective_id=0, has_side_effects=True, vmem_limit_bytes=56 * 1024 * 1024
        ),
    )(
        query,
        key,
        value,
        short_taps,
        residue.T,
        rate.T,
        skip[None, :],
        out_weight,
        jnp.asarray(weights),
        jnp.asarray(places),
    )


def solution(mesh, ys=4):
    placed = (
        P("seq", "chan"),
        P("seq", "chan"),
        P("seq", "chan"),
        P(None, None, "chan"),
        P("chan", None),
        P("chan", None),
        P("chan"),
        P(None, "chan"),
    )
    return jax.shard_map(
        functools.partial(per_device, mesh.shape["seq"] // ys, ys),
        mesh=mesh,
        in_specs=placed,
        out_specs=P("seq", "chan"),
        check_vma=False,
    )
```

```python
import functools

import jax
import jax.numpy as jnp
import ml_dtypes
import numpy as np
from jax import lax
from jax.experimental import pallas as pl
from jax.experimental.pallas import tpu as pltpu
from jax.sharding import PartitionSpec as P

MESH = pl.DeviceIdType.MESH
F32 = jnp.float32
BF16 = jnp.bfloat16
MODES = 16
STEPS = 16
SUBS = 8
ROWS = STEPS * SUBS
LANES = 128
CHIPS = 4
CORES = 2
PIECES = 2
FACTOR, OWN = 0, 1
ROUTES = (
    (0, 6, "right"),
    (0, 2, "left"),
    (0, 1, "sibling"),
    (6, 4, "right"),
    (2, 4, "left"),
    (6, 7, "sibling"),
    (2, 3, "sibling"),
    (4, 5, "sibling"),
)
NODES = STEPS - 2


def tree_sum(array):
    while array.shape[0] > 1:
        half = array.shape[0] // 2
        array = array[:half] + array[half:]
    return array[0]


def lagged(block, last, last_but_one):
    one = jnp.concatenate([last[None], block[:-1]], axis=0)
    two = jnp.concatenate([last_but_one[None], one[:-1]], axis=0)
    return one, two


def tapped(taps, which, cols, now, one, two):
    return (
        taps[which, 0:1, cols] * now + taps[which, 1:2, cols] * one + taps[which, 2:3, cols] * two
    )


def kernel(
    zs,
    ys,
    q_hbm,
    k_hbm,
    v_hbm,
    taps_hbm,
    res_hbm,
    rate_hbm,
    skip_hbm,
    w_hbm,
    weights_hbm,
    places_hbm,
    out_ref,
    q_in,
    k_in,
    v_in,
    taps,
    res,
    rate,
    skip,
    weight,
    weights,
    places,
    rate3,
    decay3,
    gain3,
    xq,
    xk,
    xv,
    enter,
    local,
    query,
    near,
    node3,
    own_state,
    info,
    edge_z,
    heads,
    starts,
    total,
    half_sum,
    ring_z,
    before,
    flow,
    hid,
    acc,
    load_sem,
    y_send,
    y_recv,
    e_send,
    e_recv,
    z_send,
    z_recv,
    g_send,
    g_recv,
    f_send,
    f_recv,
    ready_z,
    known,
    ready_edge,
):
    seq = lax.axis_index("seq")
    chan = lax.axis_index("chan")
    z, y = seq // ys, lax.rem(seq, ys)
    x, core = chan // CORES, lax.rem(chan, CORES)
    width = k_in.shape[1]
    tiles = width // LANES
    half = width // PIECES
    per = tiles // PIECES
    last_y = y == ys - 1

    loads = [
        pltpu.make_async_copy(src, dst, load_sem.at[i])
        for i, (src, dst) in enumerate(
            [
                (rate_hbm, rate),
                (res_hbm, res),
                (taps_hbm, taps),
                (k_hbm, k_in),
                (v_hbm, v_in),
                (q_hbm, q_in),
                (skip_hbm, skip),
                (places_hbm, places),
                (weights_hbm, weights),
                (w_hbm, weight),
            ]
        )
    ]
    for i in (2, 5, 0, 1, 3, 4, 6, 7, 8, 9):
        loads[i].start()
    pending = []

    def at(zz, yy):
        return zz * ys + yy

    def signal(sem, s, c):
        pl.semaphore_signal(sem, inc=1, device_id=(s, c), device_id_type=MESH)

    def x_peer(e):
        return lax.rem(x + e, CHIPS) * CORES

    right = x_peer(1) + core
    left = x_peer(CHIPS - 1) + core
    sibling = x * CORES + 1 - core
    z_up = lax.rem(z + 1, zs)
    z_down = lax.rem(z + zs - 1, zs)

    barrier = pltpu.get_barrier_semaphore()
    for e in range(1, CHIPS):
        for c in range(CORES):
            signal(barrier, seq, x_peer(e) + c)
    signal(barrier, seq, sibling)
    for e in range(1, ys):
        signal(barrier, at(z, lax.rem(y + e, ys)), chan)
    hub = zs // 2
    early = z < hub
    place = lax.rem(z, hub)
    for d in range(1, zs):

        @pl.when(early & (z + d < zs) & ((z + d < hub) | (z >= hub - 2)))
        def _():
            signal(barrier, at(lax.rem(z + d, zs), y), chan)

    @pl.when((z >= hub) & (z < zs - 1))
    def _():
        signal(barrier, at(z_up, y), chan)

    @pl.when(z > hub)
    def _():
        signal(barrier, at(z_down, y), chan)

    @pl.when(last_y & early)
    def _():
        for e in range(ys):
            signal(barrier, at(z_up, e), chan)

    @pl.when(z > hub)
    def _():
        signal(barrier, at(z_down, ys - 1), chan)

    row = lax.broadcasted_iota(jnp.int32, (ROWS, ROWS), 0)
    col = lax.broadcasted_iota(jnp.int32, (ROWS, ROWS), 1)
    order = jnp.where(col == (row & 7) * STEPS + (row >> 3), 1.0, 0.0).astype(BF16)
    back = jnp.where(row == (col & 7) * STEPS + (col >> 3), 1.0, 0.0).astype(BF16)

    def arranged(block):
        return jnp.dot(order, block, preferred_element_type=F32).reshape(STEPS, SUBS, width)

    sub = lax.broadcasted_iota(jnp.int32, (SUBS, LANES), 0)
    sub3 = lax.broadcasted_iota(jnp.int32, (MODES, SUBS, LANES), 1)
    first = sub == 0
    subf3 = sub3.astype(F32)

    loads[2].wait()
    loads[5].wait()
    xq[...] = arranged(q_in[...])

    pick = lax.broadcasted_iota(jnp.int32, (MODES, ROWS), 0)
    pos = lax.broadcasted_iota(jnp.int32, (MODES, ROWS), 1)

    def ends_of(base, block):
        i = pick - base
        ends = ((i >= 0) & (i < 2) & (pos == i)) | ((i >= 2) & (i < 4) & (pos == i + ROWS - 4))
        return jnp.dot(
            jnp.where(ends, 1.0, 0.0).astype(BF16), block[...], preferred_element_type=F32
        )

    def lags(block):
        last = jnp.where(first, 0.0, pltpu.roll(block[STEPS - 1], 1, 0))
        last_but_one = jnp.where(first, 0.0, pltpu.roll(block[STEPS - 2], 1, 0))
        return lagged(block, last, last_but_one)

    g_copies = {}

    def send(route, kind, piece):
        slot, to_slot, to = ROUTES[route]
        to = {"right": right, "left": left, "sibling": sibling}[to]
        copy = pltpu.make_async_remote_copy(
            hid.at[slot, kind, piece],
            hid.at[to_slot, kind, piece],
            g_send.at[route, kind, piece],
            g_recv.at[route, kind, piece],
            device_id=(seq, to),
            device_id_type=MESH,
        )
        copy.start()
        pending.append(copy.wait_send)
        g_copies[route, kind, piece] = copy

    def arrived(route, kind, piece):
        g_copies[route, kind, piece].wait_recv()

    for l in range(tiles):
        cols = slice(l * LANES, (l + 1) * LANES)
        qb = xq[:, :, cols]
        qb = tapped(taps, 0, cols, qb, *lags(qb))
        query[:, :, cols] = qb
        qb = jnp.concatenate([jnp.where(first[None], 1.0, qb[:2]), qb[2:]], axis=0)
        to = slice(l % per * LANES, (l % per + 1) * LANES)
        hid[0, FACTOR, l // per, :, to] = qb.reshape(ROWS, LANES).astype(BF16)
    pl.semaphore_wait(
        barrier,
        (CORES * CHIPS - 1 + ys - 1)
        + jnp.where(early, z, 2 + jnp.where(z > hub, 1, 0) + jnp.where(z < zs - 1, 1, 0))
        + jnp.where((z > 0) & (z <= hub), 1, 0)
        + jnp.where(last_y & (z >= hub) & (z < zs - 1), ys, 0),
    )
    for d in range(1, zs):

        @pl.when((z >= d) & (z - d < hub) & (early | (z - d >= hub - 2)))
        def _():
            signal(ready_z.at[d - 1], at(lax.rem(z + zs - d, zs), y), chan)

    @pl.when((z > hub) & (z < zs - 1))
    def _():
        signal(known.at[0], at(z_down, y), chan)

    @pl.when((z > 0) & (z <= hub))
    def _():
        signal(ready_edge, at(z_down, ys - 1), chan)

    for route, piece in ((0, 0), (1, 1), (0, 1), (1, 0), (2, 0), (2, 1)):
        send(route, FACTOR, piece)

    loads[0].wait()
    loads[1].wait()
    r = rate[...]
    series = r * (1.0 - r * (1 / 2) * (1.0 - r * (1 / 3) * (1.0 - r * (1 / 4) * (1.0 - r * (1 / 5) * (1.0 - r * (1 / 6))))))
    gain = res[...] * series
    decay = jnp.exp(-r)
    for m in range(MODES):
        rate3[m] = jnp.broadcast_to(r[m : m + 1], (SUBS, width))
        decay3[m] = jnp.broadcast_to(decay[m : m + 1], (SUBS, width))
        gain3[m] = jnp.broadcast_to(gain[m : m + 1], (SUBS, width))

    loads[3].wait()
    loads[4].wait()
    xk[...] = arranged(k_in[...])
    xv[...] = arranged(v_in[...])
    info[y, MODES : MODES + 16, :] = (ends_of(0, k_in) + ends_of(4, v_in) + ends_of(8, q_in)).astype(BF16)
    for l in range(tiles):
        cols = slice(l * LANES, (l + 1) * LANES)
        kb, vb = xk[:, :, cols], xv[:, :, cols]
        g = tapped(taps, 1, cols, kb, *lags(kb)) * tapped(taps, 2, cols, vb, *lags(vb))
        g = jnp.concatenate([jnp.where(first[None], 0.0, g[:2]), g[2:]], axis=0)
        local[:, :, cols] = g
        a = decay3[:, :, cols]
        state = jnp.broadcast_to(g[0][None], a.shape)
        for j in range(1, STEPS):
            state = state * a + g[j][None]
        step = a
        for _ in range(4):
            step = step * step
        for reach in (1, 2, 4):
            state = state + jnp.where(sub3 >= reach, step, 0.0) * pltpu.roll(state, reach, 1)
            step = step * step
        enter[:, :, cols] = jnp.where(sub3 >= 1, pltpu.roll(state, 1, 1), 0.0)
        for m in range(MODES):
            own_state[m : m + 1, cols] = state[m, SUBS - 1 : SUBS, :]

    info[y, 0:MODES, :] = own_state[...].astype(BF16)

    y_copies = []
    for e in range(1, ys):
        copy = pltpu.make_async_remote_copy(
            info.at[y], info.at[y], y_send.at[e - 1], y_recv.at[e - 1],
            device_id=(at(z, lax.rem(y + e, ys)), chan), device_id_type=MESH,
        )
        copy.start()
        pending.append(copy.wait_send)
        y_copies.append(copy)

    loads[6].wait()
    for p in range(PIECES):
        for i in range(per):
            l = p * per + i
            cols = slice(l * LANES, (l + 1) * LANES)
            r3, a, w = rate3[:, :, cols], decay3[:, :, cols], gain3[:, :, cols]
            close = w * jnp.exp(-subf3 * r3)
            a8 = a * a
            a8 = a8 * a8
            a8 = a8 * a8
            near[0:SUBS, cols] = tree_sum(close)
            near[SUBS : 2 * SUBS, cols] = tree_sum(close * a8)
            g = local[:, :, cols]
            out = g * skip[0:1, cols]
            for d in range(STEPS):
                add = g[: STEPS - d] * near[d : d + 1, cols][None]
                out = out + add if d == 0 else jnp.concatenate([out[:d], out[d:] + add], axis=0)
            state = w * a * enter[:, :, cols]
            own = []
            for j in range(STEPS):
                line = query[j, :, cols] * (out[j] + tree_sum(state))
                if j < STEPS - 1:
                    state = state * a
                own.append(jnp.where(first, 0.0, line) if j < 2 else line)
            to = slice(i * LANES, (i + 1) * LANES)
            hid[0, OWN, p, :, to] = jnp.concatenate(own, axis=0).astype(BF16)
        send(0, OWN, p)
        send(2, OWN, p)
    for p in reversed(range(PIECES)):
        send(1, OWN, p)

    edges = [
        pltpu.make_async_remote_copy(
            info.at[y, pl.ds(MODES, 16)], edge_z, e_send.at[e], e_recv,
            device_id=(at(z_up, e), chan), device_id_type=MESH,
        )
        for e in range(ys)
    ]

    @pl.when(last_y & early)
    def _():
        pl.semaphore_wait(ready_edge, ys)

    @pl.when(last_y & (z < zs - 1))
    def _():
        for copy in edges:
            copy.start()

    @pending.append
    def _():
        @pl.when(last_y & (z < zs - 1))
        def _():
            for copy in edges:
                copy.wait_send()

    for i in range(hub - 2):

        @pl.when((z >= hub) & (z + 2 + i < zs))
        def _():
            pl.semaphore_wait(known.at[i], 1)
            if i < hub - 3:
                pl.when(z > hub)(lambda: signal(known.at[i + 1], at(z_down, y), chan))

    arrived(0, FACTOR, 0)
    send(3, FACTOR, 0)
    arrived(1, FACTOR, 1)
    send(4, FACTOR, 1)

    r = rate[...]
    a126 = jnp.exp(-(ROWS - 2.0) * r)
    a127 = jnp.exp(-(ROWS - 1.0) * r)
    a128 = jnp.exp(-float(ROWS) * r)
    everything = slice(0, width)
    loads[7].wait()
    for l in range(tiles):
        cols = slice(l * LANES, (l + 1) * LANES)
        for m in range(MODES):
            node3[m, :, cols] = gain3[m, 0:1, cols] * jnp.exp(
                -(places[...] + 1.0) * rate[m : m + 1, cols]
            )

    @pl.when(z == 0)
    def _():
        edge_z[...] = jnp.zeros_like(edge_z)

    @pl.when(z > 0)
    def _():
        edges[0].wait_recv()

    for copy in y_copies:
        copy.wait_recv()
    ends = edge_z[...].astype(F32)
    start = jnp.zeros_like(r)
    for e in range(ys):
        now = info[e, MODES : MODES + 16, :].astype(F32)
        k0, k1, v0, v1 = (now[i : i + 1] for i in (0, 1, 4, 5))
        k126, k127, v126, v127, q126, q127 = (ends[i : i + 1] for i in (2, 3, 6, 7, 10, 11))
        g0 = tapped(taps, 1, everything, k0, k127, k126) * tapped(
            taps, 2, everything, v0, v127, v126
        )
        g1 = tapped(taps, 1, everything, k1, k0, k127) * tapped(taps, 2, everything, v1, v0, v127)
        for i, line in enumerate((g0, g1, q126, q127)):
            heads[e, i : i + 1, :] = line
        starts[e] = start
        start = start * a128 + (info[e, 0:MODES, :].astype(F32) + a127 * g0 + a126 * g1)
        ends = now
    total[...] = start.astype(BF16)

    to_half = hub - z

    def to_later(source, d):
        return pltpu.make_async_remote_copy(
            source, ring_z.at[d - 1], z_send.at[d - 1], z_recv.at[d - 1],
            device_id=(at(lax.rem(z + d, zs), y), chan), device_id_type=MESH,
        )

    def send_sums(source, distances, which):
        for d in distances:

            @pl.when((z + d < zs) & which(d))
            def _():
                @pl.when(early)
                def _():
                    pl.semaphore_wait(ready_z.at[d - 1], 1)

                to_later(source, d).start()

            pending.append(
                functools.partial(
                    pl.when((z + d < zs) & which(d)), to_later(source, d).wait_send
                )
            )

    send_sums(total, range(hub - 1, 0, -1), lambda d: (z >= hub) | (d < to_half))
    send_sums(total, range(hub, 0, -1), lambda d: z == hub - 1)

    arrived(0, OWN, 0)
    send(3, OWN, 0)
    arrived(1, OWN, 1)
    send(4, OWN, 1)
    send(5, FACTOR, 0)
    send(6, FACTOR, 1)
    arrived(0, FACTOR, 1)
    send(5, FACTOR, 1)
    arrived(1, FACTOR, 0)
    send(6, FACTOR, 0)
    before[...] = jnp.zeros_like(before)
    for d in range(1, hub + 2):

        @pl.when((z >= d) & (early | (z - d >= hub - 2)))
        def _():
            to_later(total, d).wait_recv()
            before[...] += (
                jnp.exp(-float(ROWS * ys * (d - 1)) * rate[...]) * ring_z[d - 1].astype(F32)
            )

    @pl.when(z == hub - 2)
    def _():
        half_sum[...] = (
            total[...].astype(F32) + jnp.exp(-float(ROWS * ys) * rate[...]) * before[...]
        ).astype(BF16)

    send_sums(half_sum, range(hub + 1, 1, -1), lambda d: z == hub - 2)

    entering = starts[y] + jnp.exp(-float(ROWS) * y.astype(F32) * r) * before[...]
    g0, g1, q126, q127 = (heads[y, i : i + 1, :] for i in range(4))
    later = entering + jnp.exp(r) * g0 + jnp.exp(2.0 * r) * g1
    rows = lax.broadcasted_iota(jnp.int32, (STEPS, LANES), 0)
    now = info[y, MODES : MODES + 16, :].astype(F32)
    s0 = tapped(taps, 0, everything, now[8:9], q127, q126)
    s1 = tapped(taps, 0, everything, now[9:10], now[8:9], q127)
    for l in range(tiles):
        cols = slice(l * LANES, (l + 1) * LANES)
        near0, near1, direct = near[0:1, cols], near[1:2, cols], skip[0:1, cols]
        values = jnp.zeros((STEPS, LANES), F32)
        for m in range(MODES):
            values += node3[m, :, cols] * jnp.where(
                rows < NODES, later[m : m + 1, cols], entering[m : m + 1, cols]
            )
        c0, c1 = g0[:, cols], g1[:, cols]
        h0 = s0[:, cols] * (values[NODES : NODES + 1] + (near0 + direct) * c0)
        h1 = s1[:, cols] * (values[NODES + 1 : NODES + 2] + near1 * c0 + (near0 + direct) * c1)
        values = jnp.where(rows == NODES, h0, jnp.where(rows == NODES + 1, h1, values))
        flow[0, :, cols] = values.astype(BF16)

    f_copies = {}
    for ex in (2, 1, 3, 0):
        for ec in range(CORES):
            slot = ex * CORES + ec
            if slot:
                to = x_peer(CHIPS - ex) + (core if ec == 0 else 1 - core)
                copy = pltpu.make_async_remote_copy(
                    flow.at[0], flow.at[slot], f_send.at[slot], f_recv.at[slot],
                    device_id=(seq, to), device_id_type=MESH,
                )
                copy.start()
                pending.append(copy.wait_send)
                f_copies[slot] = copy

    send(5, OWN, 0)
    send(6, OWN, 1)
    arrived(0, OWN, 1)
    send(5, OWN, 1)
    arrived(1, OWN, 0)
    send(6, OWN, 0)
    for kind in (FACTOR, OWN):
        for p in range(PIECES):
            arrived(3 + p, kind, p)
            send(7, kind, p)

    loads[8].wait()
    loads[9].wait()
    for n, slot in enumerate((0, 1, 6, 2, 7, 3, 4, 5)):
        if slot % CORES:
            for kind in (FACTOR, OWN):
                for p in range(PIECES):
                    arrived({1: 2, 7: 5, 3: 6, 5: 7}[slot], kind, p)
        if slot:
            f_copies[slot].wait_recv()
        values = flow[slot]
        entering = jnp.dot(
            weights[...], jnp.concatenate([values, values], axis=0), preferred_element_type=F32
        )
        blocks = []
        for p in range(PIECES):
            own, factor = hid[slot, OWN, p].astype(F32), hid[slot, FACTOR, p].astype(F32)
            blocks.append((own + factor * entering[:, p * half : (p + 1) * half]).astype(BF16))
        owner = x_peer(slot // CORES) + (core if slot % CORES == 0 else 1 - core)
        wrows = weight[pl.ds(pl.multiple_of(owner * width, width), width), :]
        part = jnp.dot(jnp.concatenate(blocks, axis=1), wrows, preferred_element_type=F32)
        if n:
            part = part + acc[...]
        acc[...] = part

    mixed = acc[...].astype(BF16)
    out_ref[...] = jnp.dot(back, mixed, preferred_element_type=F32).astype(BF16)

    for wait in pending:
        wait()


def interpolation():
    turn = np.pi * (2 * np.arange(NODES) + 1) / (2 * NODES)
    places = ((ROWS - 1) / 2 * (1 - np.cos(turn))).astype(np.float32)
    at = places.astype(np.float64)
    share = np.array([1 / np.prod(at[i] - np.delete(at, i)) for i in range(NODES)])
    weights = np.zeros((ROWS, STEPS))
    for t in range(2, ROWS):
        part = share / (t - at)
        weights[t, :NODES] = part / part.sum()
    weights[0, NODES] = weights[1, NODES + 1] = 1
    weights = weights.reshape(SUBS, STEPS, STEPS).swapaxes(0, 1).reshape(ROWS, STEPS)
    high = weights.astype(ml_dtypes.bfloat16)
    low = (weights - high.astype(np.float64)).astype(ml_dtypes.bfloat16)
    places = np.broadcast_to(np.append(places, [0, 1]).astype(np.float32)[:, None], (STEPS, LANES))
    return np.concatenate([high, low], axis=1), np.ascontiguousarray(places)


def per_device(zs, ys, query, key, value, short_taps, residue, rate, skip, out_weight):
    width = query.shape[1]
    tiles = width // LANES
    weights, places = interpolation()
    modes = pltpu.VMEM((MODES, width), F32)
    table = pltpu.VMEM((MODES, SUBS, width), F32)
    block = pltpu.VMEM((STEPS, SUBS, width), F32)
    dma = pltpu.SemaphoreType.DMA
    regular = pltpu.SemaphoreType.REGULAR
    scratch = [
        pltpu.VMEM((ROWS, width), BF16),
        pltpu.VMEM((ROWS, width), BF16),
        pltpu.VMEM((ROWS, width), BF16),
        pltpu.VMEM(short_taps.shape, F32),
        modes,
        modes,
        pltpu.VMEM((1, width), F32),
        pltpu.VMEM(out_weight.shape, BF16),
        pltpu.VMEM(weights.shape, BF16),
        pltpu.VMEM(places.shape, F32),
        table,
        table,
        table,
        block,
        block,
        block,
        table,
        block,
        block,
        pltpu.VMEM((STEPS, width), F32),
        pltpu.VMEM((MODES, STEPS, width), F32),
        modes,
        pltpu.VMEM((ys, MODES + 16, width), BF16),
        pltpu.VMEM((16, width), BF16),
        pltpu.VMEM((ys, 8, width), F32),
        pltpu.VMEM((ys, MODES, width), F32),
        pltpu.VMEM((MODES, width), BF16),
        pltpu.VMEM((MODES, width), BF16),
        pltpu.VMEM((zs - 1, MODES, width), BF16),
        modes,
        pltpu.VMEM((CHIPS * CORES, STEPS, width), BF16),
        pltpu.VMEM((CHIPS * CORES, 2, PIECES, ROWS, width // PIECES), BF16),
        pltpu.VMEM((ROWS, width), F32),
        dma((10,)),
        dma((ys - 1,)),
        dma((ys - 1,)),
        dma((ys,)),
        dma,
        dma((zs - 1,)),
        dma((zs - 1,)),
        dma((len(ROUTES), 2, PIECES)),
        dma((len(ROUTES), 2, PIECES)),
        dma((CHIPS * CORES,)),
        dma((CHIPS * CORES,)),
        regular((zs - 1,)),
        regular((zs // 2 - 2,)),
        regular,
    ]
    return pl.pallas_call(
        functools.partial(kernel, zs, ys),
        out_shape=jax.ShapeDtypeStruct((ROWS, width), BF16),
        in_specs=[pl.BlockSpec(memory_space=pl.ANY)] * 10,
        out_specs=pl.BlockSpec(memory_space=pltpu.VMEM),
        scratch_shapes=scratch,
        compiler_params=pltpu.CompilerParams(
            collective_id=0, has_side_effects=True, vmem_limit_bytes=56 * 1024 * 1024
        ),
    )(
        query,
        key,
        value,
        short_taps,
        residue.T,
        rate.T,
        skip[None, :],
        out_weight,
        jnp.asarray(weights),
        jnp.asarray(places),
    )


def solution(mesh, ys=4):
    placed = (
        P("seq", "chan"),
        P("seq", "chan"),
        P("seq", "chan"),
        P(None, None, "chan"),
        P("chan", None),
        P("chan", None),
        P("chan"),
        P(None, "chan"),
    )
    return jax.shard_map(
        functools.partial(per_device, mesh.shape["seq"] // ys, ys),
        mesh=mesh,
        in_specs=placed,
        out_specs=P("seq", "chan"),
        check_vma=False,
    )
```

```python
import functools

import jax
import jax.numpy as jnp
import ml_dtypes
import numpy as np
from jax import lax
from jax.experimental import pallas as pl
from jax.experimental.pallas import tpu as pltpu
from jax.sharding import PartitionSpec as P

MESH = pl.DeviceIdType.MESH
F32 = jnp.float32
BF16 = jnp.bfloat16
MODES = 16
STEPS = 16
SUBS = 8
ROWS = STEPS * SUBS
LANES = 128
CHIPS = 4
CORES = 2
PIECES = 2
FACTOR, OWN = 0, 1
ROUTES = (
    (0, 6, "right"),
    (0, 2, "left"),
    (0, 1, "sibling"),
    (6, 4, "right"),
    (2, 4, "left"),
    (6, 7, "sibling"),
    (2, 3, "sibling"),
    (4, 5, "sibling"),
)
NODES = STEPS - 2


def tree_sum(array):
    while array.shape[0] > 1:
        half = array.shape[0] // 2
        array = array[:half] + array[half:]
    return array[0]


def lagged(block, last, last_but_one):
    one = jnp.concatenate([last[None], block[:-1]], axis=0)
    two = jnp.concatenate([last_but_one[None], one[:-1]], axis=0)
    return one, two


def tapped(taps, which, cols, now, one, two):
    return (
        taps[which, 0:1, cols] * now + taps[which, 1:2, cols] * one + taps[which, 2:3, cols] * two
    )


def kernel(
    zs,
    ys,
    q_hbm,
    k_hbm,
    v_hbm,
    taps_hbm,
    res_hbm,
    rate_hbm,
    skip_hbm,
    w_hbm,
    weights_hbm,
    places_hbm,
    out_ref,
    q_in,
    k_in,
    v_in,
    taps,
    res,
    rate,
    skip,
    weight,
    weights,
    places,
    rate3,
    decay3,
    gain3,
    xq,
    xk,
    xv,
    enter,
    local,
    query,
    near,
    node3,
    own_state,
    info,
    ends_before,
    heads,
    starts,
    total,
    half_sum,
    ring_z,
    before,
    flow,
    hid,
    acc,
    load_sem,
    y_send,
    y_recv,
    z_send,
    z_recv,
    g_send,
    g_recv,
    f_send,
    f_recv,
    ready_z,
    known,
):
    seq = lax.axis_index("seq")
    chan = lax.axis_index("chan")
    z, y = seq // ys, lax.rem(seq, ys)
    x, core = chan // CORES, lax.rem(chan, CORES)
    width = k_in.shape[1]
    tiles = width // LANES
    half = width // PIECES
    per = tiles // PIECES

    loads = [
        pltpu.make_async_copy(src, dst, load_sem.at[i])
        for i, (src, dst) in enumerate(
            [
                (rate_hbm, rate),
                (res_hbm, res),
                (taps_hbm, taps),
                (k_hbm, k_in),
                (v_hbm, v_in),
                (q_hbm, q_in),
                (skip_hbm, skip),
                (places_hbm, places),
                (weights_hbm, weights),
                (w_hbm, weight),
            ]
        )
    ]
    for i in (2, 5, 0, 1, 3, 4, 6, 7, 8, 9):
        loads[i].start()
    pending = []

    def at(zz, yy):
        return zz * ys + yy

    def signal(sem, s, c):
        pl.semaphore_signal(sem, inc=1, device_id=(s, c), device_id_type=MESH)

    def x_peer(e):
        return lax.rem(x + e, CHIPS) * CORES

    right = x_peer(1) + core
    left = x_peer(CHIPS - 1) + core
    sibling = x * CORES + 1 - core
    z_up = lax.rem(z + 1, zs)
    z_down = lax.rem(z + zs - 1, zs)

    barrier = pltpu.get_barrier_semaphore()
    for e in range(1, CHIPS):
        for c in range(CORES):
            signal(barrier, seq, x_peer(e) + c)
    signal(barrier, seq, sibling)
    for e in range(1, ys):
        signal(barrier, at(z, lax.rem(y + e, ys)), chan)
    hub = zs // 2
    early = z < hub
    place = lax.rem(z, hub)
    for d in range(1, zs):

        @pl.when(early & (z + d < zs) & ((z + d < hub) | (z >= hub - 2)))
        def _():
            signal(barrier, at(lax.rem(z + d, zs), y), chan)

    @pl.when((z >= hub) & (z < zs - 1))
    def _():
        signal(barrier, at(z_up, y), chan)

    @pl.when(z > hub)
    def _():
        signal(barrier, at(z_down, y), chan)

    row = lax.broadcasted_iota(jnp.int32, (ROWS, ROWS), 0)
    col = lax.broadcasted_iota(jnp.int32, (ROWS, ROWS), 1)
    order = jnp.where(col == (row & 7) * STEPS + (row >> 3), 1.0, 0.0).astype(BF16)
    back = jnp.where(row == (col & 7) * STEPS + (col >> 3), 1.0, 0.0).astype(BF16)

    def arranged(block):
        return jnp.dot(order, block, preferred_element_type=F32).reshape(STEPS, SUBS, width)

    sub = lax.broadcasted_iota(jnp.int32, (SUBS, LANES), 0)
    sub3 = lax.broadcasted_iota(jnp.int32, (MODES, SUBS, LANES), 1)
    first = sub == 0
    subf3 = sub3.astype(F32)

    loads[2].wait()
    loads[5].wait()
    xq[...] = arranged(q_in[...])

    pick = lax.broadcasted_iota(jnp.int32, (MODES, ROWS), 0)
    pos = lax.broadcasted_iota(jnp.int32, (MODES, ROWS), 1)

    def ends_of(base, block):
        i = pick - base
        ends = ((i >= 0) & (i < 2) & (pos == i)) | ((i >= 2) & (i < 4) & (pos == i + ROWS - 4))
        return jnp.dot(
            jnp.where(ends, 1.0, 0.0).astype(BF16), block[...], preferred_element_type=F32
        )

    def lags(block):
        last = jnp.where(first, 0.0, pltpu.roll(block[STEPS - 1], 1, 0))
        last_but_one = jnp.where(first, 0.0, pltpu.roll(block[STEPS - 2], 1, 0))
        return lagged(block, last, last_but_one)

    g_copies = {}

    def send(route, kind, piece):
        slot, to_slot, to = ROUTES[route]
        to = {"right": right, "left": left, "sibling": sibling}[to]
        copy = pltpu.make_async_remote_copy(
            hid.at[slot, kind, piece],
            hid.at[to_slot, kind, piece],
            g_send.at[route, kind, piece],
            g_recv.at[route, kind, piece],
            device_id=(seq, to),
            device_id_type=MESH,
        )
        copy.start()
        pending.append(copy.wait_send)
        g_copies[route, kind, piece] = copy

    def arrived(route, kind, piece):
        g_copies[route, kind, piece].wait_recv()

    for l in range(tiles):
        cols = slice(l * LANES, (l + 1) * LANES)
        qb = xq[:, :, cols]
        qb = tapped(taps, 0, cols, qb, *lags(qb))
        query[:, :, cols] = qb
        qb = jnp.concatenate([jnp.where(first[None], 1.0, qb[:2]), qb[2:]], axis=0)
        to = slice(l % per * LANES, (l % per + 1) * LANES)
        hid[0, FACTOR, l // per, :, to] = qb.reshape(ROWS, LANES).astype(BF16)
    pl.semaphore_wait(
        barrier,
        (CORES * CHIPS - 1 + ys - 1)
        + jnp.where(early, z, 2 + jnp.where(z > hub, 1, 0) + jnp.where(z < zs - 1, 1, 0))
    )
    for d in range(1, zs):

        @pl.when((z >= d) & (z - d < hub) & (early | (z - d >= hub - 2)))
        def _():
            signal(ready_z.at[d - 1], at(lax.rem(z + zs - d, zs), y), chan)

    @pl.when((z > hub) & (z < zs - 1))
    def _():
        signal(known.at[0], at(z_down, y), chan)

    for route, piece in ((0, 0), (1, 1), (0, 1), (1, 0), (2, 0), (2, 1)):
        send(route, FACTOR, piece)

    loads[0].wait()
    loads[1].wait()
    r = rate[...]
    series = r * (1.0 - r * (1 / 2) * (1.0 - r * (1 / 3) * (1.0 - r * (1 / 4) * (1.0 - r * (1 / 5) * (1.0 - r * (1 / 6))))))
    gain = res[...] * series
    decay = jnp.exp(-r)
    for m in range(MODES):
        rate3[m] = jnp.broadcast_to(r[m : m + 1], (SUBS, width))
        decay3[m] = jnp.broadcast_to(decay[m : m + 1], (SUBS, width))
        gain3[m] = jnp.broadcast_to(gain[m : m + 1], (SUBS, width))

    loads[3].wait()
    loads[4].wait()
    xk[...] = arranged(k_in[...])
    xv[...] = arranged(v_in[...])
    info[y, MODES : MODES + 16, :] = (ends_of(0, k_in) + ends_of(4, v_in) + ends_of(8, q_in)).astype(BF16)
    for l in range(tiles):
        cols = slice(l * LANES, (l + 1) * LANES)
        kb, vb = xk[:, :, cols], xv[:, :, cols]
        g = tapped(taps, 1, cols, kb, *lags(kb)) * tapped(taps, 2, cols, vb, *lags(vb))
        g = jnp.concatenate([jnp.where(first[None], 0.0, g[:2]), g[2:]], axis=0)
        local[:, :, cols] = g
        a = decay3[:, :, cols]
        state = jnp.broadcast_to(g[0][None], a.shape)
        for j in range(1, STEPS):
            state = state * a + g[j][None]
        step = a
        for _ in range(4):
            step = step * step
        for reach in (1, 2, 4):
            state = state + jnp.where(sub3 >= reach, step, 0.0) * pltpu.roll(state, reach, 1)
            step = step * step
        enter[:, :, cols] = jnp.where(sub3 >= 1, pltpu.roll(state, 1, 1), 0.0)
        for m in range(MODES):
            own_state[m : m + 1, cols] = state[m, SUBS - 1 : SUBS, :]

    info[y, 0:MODES, :] = own_state[...].astype(BF16)

    y_copies = []
    for e in range(1, ys):
        copy = pltpu.make_async_remote_copy(
            info.at[y], info.at[y], y_send.at[e - 1], y_recv.at[e - 1],
            device_id=(at(z, lax.rem(y + e, ys)), chan), device_id_type=MESH,
        )
        copy.start()
        pending.append(copy.wait_send)
        y_copies.append(copy)

    loads[6].wait()
    for p in range(PIECES):
        for i in range(per):
            l = p * per + i
            cols = slice(l * LANES, (l + 1) * LANES)
            r3, a, w = rate3[:, :, cols], decay3[:, :, cols], gain3[:, :, cols]
            close = w * jnp.exp(-subf3 * r3)
            a8 = a * a
            a8 = a8 * a8
            a8 = a8 * a8
            near[0:SUBS, cols] = tree_sum(close)
            near[SUBS : 2 * SUBS, cols] = tree_sum(close * a8)
            g = local[:, :, cols]
            out = g * skip[0:1, cols]
            for d in range(STEPS):
                add = g[: STEPS - d] * near[d : d + 1, cols][None]
                out = out + add if d == 0 else jnp.concatenate([out[:d], out[d:] + add], axis=0)
            state = w * a * enter[:, :, cols]
            own = []
            for j in range(STEPS):
                line = query[j, :, cols] * (out[j] + tree_sum(state))
                if j < STEPS - 1:
                    state = state * a
                own.append(jnp.where(first, 0.0, line) if j < 2 else line)
            to = slice(i * LANES, (i + 1) * LANES)
            hid[0, OWN, p, :, to] = jnp.concatenate(own, axis=0).astype(BF16)
        send(0, OWN, p)
        send(2, OWN, p)
    for p in reversed(range(PIECES)):
        send(1, OWN, p)

    for i in range(hub - 2):

        @pl.when((z >= hub) & (z + 2 + i < zs))
        def _():
            pl.semaphore_wait(known.at[i], 1)
            if i < hub - 3:
                pl.when(z > hub)(lambda: signal(known.at[i + 1], at(z_down, y), chan))

    arrived(0, FACTOR, 0)
    send(3, FACTOR, 0)
    arrived(1, FACTOR, 1)
    send(4, FACTOR, 1)

    r = rate[...]
    a126 = jnp.exp(-(ROWS - 2.0) * r)
    a127 = jnp.exp(-(ROWS - 1.0) * r)
    a128 = jnp.exp(-float(ROWS) * r)
    everything = slice(0, width)
    loads[7].wait()
    for l in range(tiles):
        cols = slice(l * LANES, (l + 1) * LANES)
        for m in range(MODES):
            node3[m, :, cols] = gain3[m, 0:1, cols] * jnp.exp(
                -(places[...] + 1.0) * rate[m : m + 1, cols]
            )

    for copy in y_copies:
        copy.wait_recv()
    a384 = jnp.exp(-float(ROWS * (ys - 1)) * r)
    a512 = jnp.exp(-float(ROWS * ys) * r)

    def first_two(now, ends):
        k0, k1, v0, v1 = (now[i : i + 1] for i in (0, 1, 4, 5))
        k126, k127, v126, v127 = (ends[i : i + 1] for i in (2, 3, 6, 7))
        g0 = tapped(taps, 1, everything, k0, k127, k126) * tapped(
            taps, 2, everything, v0, v127, v126
        )
        g1 = tapped(taps, 1, everything, k1, k0, k127) * tapped(taps, 2, everything, v1, v0, v127)
        return g0, g1

    def set_heads(e, now, ends):
        g0, g1 = first_two(now, ends)
        for i, line in enumerate((g0, g1, ends[10:11], ends[11:12])):
            heads[e, i : i + 1, :] = line
        return a127 * g0 + a126 * g1

    firsts = info[0, MODES : MODES + 16, :].astype(F32)
    ends = firsts
    starts[0] = jnp.zeros_like(r)
    start = info[0, 0:MODES, :].astype(F32)
    for e in range(1, ys):
        now = info[e, MODES : MODES + 16, :].astype(F32)
        starts[e] = start
        start = start * a128 + (info[e, 0:MODES, :].astype(F32) + set_heads(e, now, ends))
        ends = now
    total[0:MODES, :] = start.astype(BF16)
    line = lax.broadcasted_iota(jnp.int32, (16, width), 0)
    rows_of_group = jnp.where((line & 3) < 2, firsts, ends)
    total[MODES : MODES + 16, :] = rows_of_group.astype(BF16)

    to_half = hub - z

    def to_later(source, d):
        return pltpu.make_async_remote_copy(
            source, ring_z.at[d - 1], z_send.at[d - 1], z_recv.at[d - 1],
            device_id=(at(lax.rem(z + d, zs), y), chan), device_id_type=MESH,
        )

    def send_sums(source, distances, which):
        for d in distances:

            @pl.when((z + d < zs) & which(d))
            def _():
                @pl.when(early)
                def _():
                    pl.semaphore_wait(ready_z.at[d - 1], 1)

                to_later(source, d).start()

            pending.append(
                functools.partial(
                    pl.when((z + d < zs) & which(d)), to_later(source, d).wait_send
                )
            )

    send_sums(total, range(hub - 1, 0, -1), lambda d: (z >= hub) | (d < to_half))
    send_sums(total, range(hub, 0, -1), lambda d: z == hub - 1)

    arrived(0, OWN, 0)
    send(3, OWN, 0)
    arrived(1, OWN, 1)
    send(4, OWN, 1)
    send(5, FACTOR, 0)
    send(6, FACTOR, 1)
    arrived(0, FACTOR, 1)
    send(5, FACTOR, 1)
    arrived(1, FACTOR, 0)
    send(6, FACTOR, 0)
    before[...] = jnp.zeros_like(before)
    ends_before[...] = jnp.zeros_like(ends_before)
    for d in range(hub + 1, 0, -1):

        @pl.when((z >= d) & (early | (z - d >= hub - 2)))
        def _():
            to_later(total, d).wait_recv()
            now = ring_z[d - 1, MODES : MODES + 16, :].astype(F32)
            g0, g1 = first_two(now, ends_before[...])
            head = jnp.where(early | (z - d > hub - 2), 1.0, 0.0) * (a127 * g0 + a126 * g1)
            arrived_sum = ring_z[d - 1, 0:MODES, :].astype(F32) + a384 * head
            before[...] = before[...] * a512 + arrived_sum
            ends_before[...] = now

    head = set_heads(0, firsts, ends_before[...])

    @pl.when(z == hub - 2)
    def _():
        whole = total[0:MODES, :].astype(F32) + a384 * head + a512 * before[...]
        half_sum[0:MODES, :] = whole.astype(BF16)
        half_sum[MODES : MODES + 16, :] = total[MODES : MODES + 16, :]

    send_sums(half_sum, range(hub + 1, 1, -1), lambda d: z == hub - 2)

    entering = starts[y] + jnp.exp(-float(ROWS) * y.astype(F32) * r) * before[...]
    since = jnp.maximum(y - 1, 0).astype(F32)
    entering = entering + jnp.where(y > 0, jnp.exp(-float(ROWS) * since * r) * head, 0.0)
    g0, g1, q126, q127 = (heads[y, i : i + 1, :] for i in range(4))
    later = entering + jnp.exp(r) * g0 + jnp.exp(2.0 * r) * g1
    rows = lax.broadcasted_iota(jnp.int32, (STEPS, LANES), 0)
    now = info[y, MODES : MODES + 16, :].astype(F32)
    s0 = tapped(taps, 0, everything, now[8:9], q127, q126)
    s1 = tapped(taps, 0, everything, now[9:10], now[8:9], q127)
    for l in range(tiles):
        cols = slice(l * LANES, (l + 1) * LANES)
        near0, near1, direct = near[0:1, cols], near[1:2, cols], skip[0:1, cols]
        values = jnp.zeros((STEPS, LANES), F32)
        for m in range(MODES):
            values += node3[m, :, cols] * jnp.where(
                rows < NODES, later[m : m + 1, cols], entering[m : m + 1, cols]
            )
        c0, c1 = g0[:, cols], g1[:, cols]
        h0 = s0[:, cols] * (values[NODES : NODES + 1] + (near0 + direct) * c0)
        h1 = s1[:, cols] * (values[NODES + 1 : NODES + 2] + near1 * c0 + (near0 + direct) * c1)
        values = jnp.where(rows == NODES, h0, jnp.where(rows == NODES + 1, h1, values))
        flow[0, :, cols] = values.astype(BF16)

    f_copies = {}
    for ex in (2, 1, 3, 0):
        for ec in range(CORES):
            slot = ex * CORES + ec
            if slot:
                to = x_peer(CHIPS - ex) + (core if ec == 0 else 1 - core)
                copy = pltpu.make_async_remote_copy(
                    flow.at[0], flow.at[slot], f_send.at[slot], f_recv.at[slot],
                    device_id=(seq, to), device_id_type=MESH,
                )
                copy.start()
                pending.append(copy.wait_send)
                f_copies[slot] = copy

    send(5, OWN, 0)
    send(6, OWN, 1)
    arrived(0, OWN, 1)
    send(5, OWN, 1)
    arrived(1, OWN, 0)
    send(6, OWN, 0)
    for kind in (FACTOR, OWN):
        for p in range(PIECES):
            arrived(3 + p, kind, p)
            send(7, kind, p)

    loads[8].wait()
    loads[9].wait()
    for n, slot in enumerate((0, 1, 6, 2, 7, 3, 4, 5)):
        if slot % CORES:
            for kind in (FACTOR, OWN):
                for p in range(PIECES):
                    arrived({1: 2, 7: 5, 3: 6, 5: 7}[slot], kind, p)
        if slot:
            f_copies[slot].wait_recv()
        values = flow[slot]
        entering = jnp.dot(
            weights[...], jnp.concatenate([values, values], axis=0), preferred_element_type=F32
        )
        blocks = []
        for p in range(PIECES):
            own, factor = hid[slot, OWN, p].astype(F32), hid[slot, FACTOR, p].astype(F32)
            blocks.append((own + factor * entering[:, p * half : (p + 1) * half]).astype(BF16))
        owner = x_peer(slot // CORES) + (core if slot % CORES == 0 else 1 - core)
        wrows = weight[pl.ds(pl.multiple_of(owner * width, width), width), :]
        part = jnp.dot(jnp.concatenate(blocks, axis=1), wrows, preferred_element_type=F32)
        if n:
            part = part + acc[...]
        acc[...] = part

    mixed = acc[...].astype(BF16)
    out_ref[...] = jnp.dot(back, mixed, preferred_element_type=F32).astype(BF16)

    for wait in pending:
        wait()


def interpolation():
    turn = np.pi * (2 * np.arange(NODES) + 1) / (2 * NODES)
    places = ((ROWS - 1) / 2 * (1 - np.cos(turn))).astype(np.float32)
    at = places.astype(np.float64)
    share = np.array([1 / np.prod(at[i] - np.delete(at, i)) for i in range(NODES)])
    weights = np.zeros((ROWS, STEPS))
    for t in range(2, ROWS):
        part = share / (t - at)
        weights[t, :NODES] = part / part.sum()
    weights[0, NODES] = weights[1, NODES + 1] = 1
    weights = weights.reshape(SUBS, STEPS, STEPS).swapaxes(0, 1).reshape(ROWS, STEPS)
    high = weights.astype(ml_dtypes.bfloat16)
    low = (weights - high.astype(np.float64)).astype(ml_dtypes.bfloat16)
    places = np.broadcast_to(np.append(places, [0, 1]).astype(np.float32)[:, None], (STEPS, LANES))
    return np.concatenate([high, low], axis=1), np.ascontiguousarray(places)


def per_device(zs, ys, query, key, value, short_taps, residue, rate, skip, out_weight):
    width = query.shape[1]
    tiles = width // LANES
    weights, places = interpolation()
    modes = pltpu.VMEM((MODES, width), F32)
    table = pltpu.VMEM((MODES, SUBS, width), F32)
    block = pltpu.VMEM((STEPS, SUBS, width), F32)
    dma = pltpu.SemaphoreType.DMA
    regular = pltpu.SemaphoreType.REGULAR
    scratch = [
        pltpu.VMEM((ROWS, width), BF16),
        pltpu.VMEM((ROWS, width), BF16),
        pltpu.VMEM((ROWS, width), BF16),
        pltpu.VMEM(short_taps.shape, F32),
        modes,
        modes,
        pltpu.VMEM((1, width), F32),
        pltpu.VMEM(out_weight.shape, BF16),
        pltpu.VMEM(weights.shape, BF16),
        pltpu.VMEM(places.shape, F32),
        table,
        table,
        table,
        block,
        block,
        block,
        table,
        block,
        block,
        pltpu.VMEM((STEPS, width), F32),
        pltpu.VMEM((MODES, STEPS, width), F32),
        modes,
        pltpu.VMEM((ys, MODES + 16, width), BF16),
        pltpu.VMEM((16, width), F32),
        pltpu.VMEM((ys, 8, width), F32),
        pltpu.VMEM((ys, MODES, width), F32),
        pltpu.VMEM((MODES + 16, width), BF16),
        pltpu.VMEM((MODES + 16, width), BF16),
        pltpu.VMEM((zs - 1, MODES + 16, width), BF16),
        modes,
        pltpu.VMEM((CHIPS * CORES, STEPS, width), BF16),
        pltpu.VMEM((CHIPS * CORES, 2, PIECES, ROWS, width // PIECES), BF16),
        pltpu.VMEM((ROWS, width), F32),
        dma((10,)),
        dma((ys - 1,)),
        dma((ys - 1,)),
        dma((zs - 1,)),
        dma((zs - 1,)),
        dma((len(ROUTES), 2, PIECES)),
        dma((len(ROUTES), 2, PIECES)),
        dma((CHIPS * CORES,)),
        dma((CHIPS * CORES,)),
        regular((zs - 1,)),
        regular((zs // 2 - 2,)),
    ]
    return pl.pallas_call(
        functools.partial(kernel, zs, ys),
        out_shape=jax.ShapeDtypeStruct((ROWS, width), BF16),
        in_specs=[pl.BlockSpec(memory_space=pl.ANY)] * 10,
        out_specs=pl.BlockSpec(memory_space=pltpu.VMEM),
        scratch_shapes=scratch,
        compiler_params=pltpu.CompilerParams(
            collective_id=0, has_side_effects=True, vmem_limit_bytes=56 * 1024 * 1024
        ),
    )(
        query,
        key,
        value,
        short_taps,
        residue.T,
        rate.T,
        skip[None, :],
        out_weight,
        jnp.asarray(weights),
        jnp.asarray(places),
    )


def solution(mesh, ys=4):
    placed = (
        P("seq", "chan"),
        P("seq", "chan"),
        P("seq", "chan"),
        P(None, None, "chan"),
        P("chan", None),
        P("chan", None),
        P("chan"),
        P(None, "chan"),
    )
    return jax.shard_map(
        functools.partial(per_device, mesh.shape["seq"] // ys, ys),
        mesh=mesh,
        in_specs=placed,
        out_specs=P("seq", "chan"),
        check_vma=False,
    )
```

```python
import functools

import jax
import jax.numpy as jnp
import ml_dtypes
import numpy as np
from jax import lax
from jax.experimental import pallas as pl
from jax.experimental.pallas import tpu as pltpu
from jax.sharding import PartitionSpec as P

MESH = pl.DeviceIdType.MESH
F32 = jnp.float32
BF16 = jnp.bfloat16
MODES = 16
STEPS = 16
SUBS = 8
ROWS = STEPS * SUBS
LANES = 128
CHIPS = 4
CORES = 2
PIECES = 2
FACTOR, OWN = 0, 1
ROUTES = (
    (0, 6, "right"),
    (0, 2, "left"),
    (0, 1, "sibling"),
    (6, 4, "right"),
    (2, 4, "left"),
    (6, 7, "sibling"),
    (2, 3, "sibling"),
    (4, 5, "sibling"),
)
NODES = STEPS - 2


def tree_sum(array):
    while array.shape[0] > 1:
        half = array.shape[0] // 2
        array = array[:half] + array[half:]
    return array[0]


def lagged(block, last, last_but_one):
    one = jnp.concatenate([last[None], block[:-1]], axis=0)
    two = jnp.concatenate([last_but_one[None], one[:-1]], axis=0)
    return one, two


def tapped(taps, which, cols, now, one, two):
    return (
        taps[which, 0:1, cols] * now + taps[which, 1:2, cols] * one + taps[which, 2:3, cols] * two
    )


def kernel(
    zs,
    ys,
    q_hbm,
    k_hbm,
    v_hbm,
    taps_hbm,
    res_hbm,
    rate_hbm,
    skip_hbm,
    w_hbm,
    weights_hbm,
    places_hbm,
    out_ref,
    q_in,
    k_in,
    v_in,
    taps,
    res,
    rate,
    skip,
    weight,
    weights,
    places,
    rate3,
    decay3,
    gain3,
    xq,
    xk,
    xv,
    enter,
    local,
    query,
    near,
    node3,
    own_state,
    info,
    ends_before,
    heads,
    starts,
    total,
    half_sum,
    ring_z,
    before,
    flow,
    hid,
    acc,
    load_sem,
    y_send,
    y_recv,
    z_send,
    z_recv,
    g_send,
    g_recv,
    f_send,
    f_recv,
    ready_z,
    known,
):
    seq = lax.axis_index("seq")
    chan = lax.axis_index("chan")
    z, y = seq // ys, lax.rem(seq, ys)
    x, core = chan // CORES, lax.rem(chan, CORES)
    width = k_in.shape[1]
    tiles = width // LANES
    half = width // PIECES
    per = tiles // PIECES

    loads = [
        pltpu.make_async_copy(src, dst, load_sem.at[i])
        for i, (src, dst) in enumerate(
            [
                (rate_hbm, rate),
                (res_hbm, res),
                (taps_hbm, taps),
                (k_hbm, k_in),
                (v_hbm, v_in),
                (q_hbm, q_in),
                (skip_hbm, skip),
                (places_hbm, places),
                (weights_hbm, weights),
                (w_hbm, weight),
            ]
        )
    ]
    for i in (2, 5, 0, 1, 3, 4, 6, 7, 8, 9):
        loads[i].start()
    pending = []

    def at(zz, yy):
        return zz * ys + yy

    def signal(sem, s, c):
        pl.semaphore_signal(sem, inc=1, device_id=(s, c), device_id_type=MESH)

    def x_peer(e):
        return lax.rem(x + e, CHIPS) * CORES

    right = x_peer(1) + core
    left = x_peer(CHIPS - 1) + core
    sibling = x * CORES + 1 - core
    z_up = lax.rem(z + 1, zs)
    z_down = lax.rem(z + zs - 1, zs)

    barrier = pltpu.get_barrier_semaphore()
    for e in range(1, CHIPS):
        for c in range(CORES):
            signal(barrier, seq, x_peer(e) + c)
    signal(barrier, seq, sibling)
    for e in range(1, ys):
        signal(barrier, at(z, lax.rem(y + e, ys)), chan)
    hub = zs // 2
    early = z < hub
    place = lax.rem(z, hub)
    for d in range(1, zs):

        @pl.when(early & (z + d < zs) & ((z + d < hub) | (z >= hub - 2)))
        def _():
            signal(barrier, at(lax.rem(z + d, zs), y), chan)

    @pl.when((z >= hub) & (z < zs - 1))
    def _():
        signal(barrier, at(z_up, y), chan)

    @pl.when(z > hub)
    def _():
        signal(barrier, at(z_down, y), chan)

    row = lax.broadcasted_iota(jnp.int32, (ROWS, ROWS), 0)
    col = lax.broadcasted_iota(jnp.int32, (ROWS, ROWS), 1)
    order = jnp.where(col == (row & 7) * STEPS + (row >> 3), 1.0, 0.0).astype(BF16)
    back = jnp.where(row == (col & 7) * STEPS + (col >> 3), 1.0, 0.0).astype(BF16)

    def arranged(block):
        return jnp.dot(order, block, preferred_element_type=F32).reshape(STEPS, SUBS, width)

    sub = lax.broadcasted_iota(jnp.int32, (SUBS, LANES), 0)
    sub3 = lax.broadcasted_iota(jnp.int32, (MODES, SUBS, LANES), 1)
    first = sub == 0
    subf3 = sub3.astype(F32)

    loads[2].wait()
    loads[5].wait()
    xq[...] = arranged(q_in[...])

    pick = lax.broadcasted_iota(jnp.int32, (MODES, ROWS), 0)
    pos = lax.broadcasted_iota(jnp.int32, (MODES, ROWS), 1)

    def ends_of(base, block):
        i = pick - base
        ends = ((i >= 0) & (i < 2) & (pos == i)) | ((i >= 2) & (i < 4) & (pos == i + ROWS - 4))
        return jnp.dot(
            jnp.where(ends, 1.0, 0.0).astype(BF16), block[...], preferred_element_type=F32
        )

    def lags(block):
        last = jnp.where(first, 0.0, pltpu.roll(block[STEPS - 1], 1, 0))
        last_but_one = jnp.where(first, 0.0, pltpu.roll(block[STEPS - 2], 1, 0))
        return lagged(block, last, last_but_one)

    g_copies = {}

    def send(route, kind, piece):
        slot, to_slot, to = ROUTES[route]
        to = {"right": right, "left": left, "sibling": sibling}[to]
        copy = pltpu.make_async_remote_copy(
            hid.at[slot, kind, piece],
            hid.at[to_slot, kind, piece],
            g_send.at[route, kind, piece],
            g_recv.at[route, kind, piece],
            device_id=(seq, to),
            device_id_type=MESH,
        )
        copy.start()
        pending.append(copy.wait_send)
        g_copies[route, kind, piece] = copy

    def arrived(route, kind, piece):
        g_copies[route, kind, piece].wait_recv()

    for l in range(tiles):
        cols = slice(l * LANES, (l + 1) * LANES)
        qb = xq[:, :, cols]
        qb = tapped(taps, 0, cols, qb, *lags(qb))
        query[:, :, cols] = qb
        qb = jnp.concatenate([jnp.where(first[None], 1.0, qb[:2]), qb[2:]], axis=0)
        to = slice(l % per * LANES, (l % per + 1) * LANES)
        hid[0, FACTOR, l // per, :, to] = qb.reshape(ROWS, LANES).astype(BF16)
    pl.semaphore_wait(
        barrier,
        (CORES * CHIPS - 1 + ys - 1)
        + jnp.where(early, z, 2 + jnp.where(z > hub, 1, 0) + jnp.where(z < zs - 1, 1, 0))
    )
    for d in range(1, zs):

        @pl.when((z >= d) & (z - d < hub) & (early | (z - d >= hub - 2)))
        def _():
            signal(ready_z.at[d - 1], at(lax.rem(z + zs - d, zs), y), chan)

    @pl.when((z > hub) & (z < zs - 1))
    def _():
        signal(known.at[0], at(z_down, y), chan)

    for route, piece in ((0, 0), (1, 1), (0, 1), (1, 0), (2, 0), (2, 1)):
        send(route, FACTOR, piece)

    loads[0].wait()
    loads[1].wait()
    r = rate[...]
    series = r * (1.0 - r * (1 / 2) * (1.0 - r * (1 / 3) * (1.0 - r * (1 / 4) * (1.0 - r * (1 / 5) * (1.0 - r * (1 / 6))))))
    gain = res[...] * series
    decay = jnp.exp(-r)
    for m in range(MODES):
        rate3[m] = jnp.broadcast_to(r[m : m + 1], (SUBS, width))
        decay3[m] = jnp.broadcast_to(decay[m : m + 1], (SUBS, width))
        gain3[m] = jnp.broadcast_to(gain[m : m + 1], (SUBS, width))

    loads[3].wait()
    loads[4].wait()
    xk[...] = arranged(k_in[...])
    xv[...] = arranged(v_in[...])
    info[y, MODES : MODES + 16, :] = (ends_of(0, k_in) + ends_of(4, v_in) + ends_of(8, q_in)).astype(BF16)
    for l in range(tiles):
        cols = slice(l * LANES, (l + 1) * LANES)
        kb, vb = xk[:, :, cols], xv[:, :, cols]
        g = tapped(taps, 1, cols, kb, *lags(kb)) * tapped(taps, 2, cols, vb, *lags(vb))
        g = jnp.concatenate([jnp.where(first[None], 0.0, g[:2]), g[2:]], axis=0)
        local[:, :, cols] = g
        a = decay3[:, :, cols]
        state = jnp.broadcast_to(g[0][None], a.shape)
        for j in range(1, STEPS):
            state = state * a + g[j][None]
        step = a
        for _ in range(4):
            step = step * step
        for reach in (1, 2, 4):
            state = state + jnp.where(sub3 >= reach, step, 0.0) * pltpu.roll(state, reach, 1)
            step = step * step
        enter[:, :, cols] = jnp.where(sub3 >= 1, pltpu.roll(state, 1, 1), 0.0)
        for m in range(MODES):
            own_state[m : m + 1, cols] = state[m, SUBS - 1 : SUBS, :]

    info[y, 0:MODES, :] = own_state[...].astype(BF16)

    y_copies = []
    for e in range(1, ys):
        copy = pltpu.make_async_remote_copy(
            info.at[y], info.at[y], y_send.at[e - 1], y_recv.at[e - 1],
            device_id=(at(z, lax.rem(y + e, ys)), chan), device_id_type=MESH,
        )
        copy.start()
        pending.append(copy.wait_send)
        y_copies.append(copy)

    loads[6].wait()
    for p in range(PIECES):
        for i in range(per):
            l = p * per + i
            cols = slice(l * LANES, (l + 1) * LANES)
            r3, a, w = rate3[:, :, cols], decay3[:, :, cols], gain3[:, :, cols]
            close = w * jnp.exp(-subf3 * r3)
            a8 = a * a
            a8 = a8 * a8
            a8 = a8 * a8
            near[0:SUBS, cols] = tree_sum(close)
            near[SUBS : 2 * SUBS, cols] = tree_sum(close * a8)
            g = local[:, :, cols]
            out = g * skip[0:1, cols]
            for d in range(STEPS):
                add = g[: STEPS - d] * near[d : d + 1, cols][None]
                out = out + add if d == 0 else jnp.concatenate([out[:d], out[d:] + add], axis=0)
            state = w * a * enter[:, :, cols]
            own = []
            for j in range(STEPS):
                line = query[j, :, cols] * (out[j] + tree_sum(state))
                if j < STEPS - 1:
                    state = state * a
                own.append(jnp.where(first, 0.0, line) if j < 2 else line)
            to = slice(i * LANES, (i + 1) * LANES)
            hid[0, OWN, p, :, to] = jnp.concatenate(own, axis=0).astype(BF16)
        send(0, OWN, p)
        send(2, OWN, p)
    for p in reversed(range(PIECES)):
        send(1, OWN, p)

    for i in range(hub - 2):

        @pl.when((z >= hub) & (z + 2 + i < zs))
        def _():
            pl.semaphore_wait(known.at[i], 1)
            if i < hub - 3:
                pl.when(z > hub)(lambda: signal(known.at[i + 1], at(z_down, y), chan))

    arrived(0, FACTOR, 0)
    send(3, FACTOR, 0)
    arrived(1, FACTOR, 1)
    send(4, FACTOR, 1)

    r = rate[...]
    a126 = jnp.exp(-(ROWS - 2.0) * r)
    a127 = jnp.exp(-(ROWS - 1.0) * r)
    a128 = jnp.exp(-float(ROWS) * r)
    everything = slice(0, width)
    loads[7].wait()
    for l in range(tiles):
        cols = slice(l * LANES, (l + 1) * LANES)
        for m in range(MODES):
            node3[m, :, cols] = gain3[m, 0:1, cols] * jnp.exp(
                -(places[...] + 1.0) * rate[m : m + 1, cols]
            )

    for copy in y_copies:
        copy.wait_recv()
    a384 = jnp.exp(-float(ROWS * (ys - 1)) * r)
    a512 = jnp.exp(-float(ROWS * ys) * r)

    def first_two(now, ends):
        k0, k1, v0, v1 = (now[i : i + 1] for i in (0, 1, 4, 5))
        k126, k127, v126, v127 = (ends[i : i + 1] for i in (2, 3, 6, 7))
        g0 = tapped(taps, 1, everything, k0, k127, k126) * tapped(
            taps, 2, everything, v0, v127, v126
        )
        g1 = tapped(taps, 1, everything, k1, k0, k127) * tapped(taps, 2, everything, v1, v0, v127)
        return g0, g1

    def set_heads(e, now, ends):
        g0, g1 = first_two(now, ends)
        for i, line in enumerate((g0, g1, ends[10:11], ends[11:12])):
            heads[e, i : i + 1, :] = line
        return a127 * g0 + a126 * g1

    firsts = info[0, MODES : MODES + 16, :].astype(F32)
    ends = firsts
    starts[0] = jnp.zeros_like(r)
    start = info[0, 0:MODES, :].astype(F32)
    for e in range(1, ys):
        now = info[e, MODES : MODES + 16, :].astype(F32)
        starts[e] = start
        start = start * a128 + (info[e, 0:MODES, :].astype(F32) + set_heads(e, now, ends))
        ends = now
    total[0:MODES, :] = start.astype(BF16)
    line = lax.broadcasted_iota(jnp.int32, (16, width), 0)
    rows_of_group = jnp.where((line & 3) < 2, firsts, ends)
    total[MODES : MODES + 16, :] = rows_of_group.astype(BF16)

    to_half = hub - z

    def to_later(source, d):
        return pltpu.make_async_remote_copy(
            source, ring_z.at[d - 1], z_send.at[d - 1], z_recv.at[d - 1],
            device_id=(at(lax.rem(z + d, zs), y), chan), device_id_type=MESH,
        )

    def send_sums(source, distances, which):
        for d in distances:

            @pl.when((z + d < zs) & which(d))
            def _():
                @pl.when(early)
                def _():
                    pl.semaphore_wait(ready_z.at[d - 1], 1)

                to_later(source, d).start()

            pending.append(
                functools.partial(
                    pl.when((z + d < zs) & which(d)), to_later(source, d).wait_send
                )
            )

    send_sums(total, range(hub - 1, 0, -1), lambda d: (z >= hub) | (d < to_half))
    send_sums(total, range(hub, 0, -1), lambda d: z == hub - 1)

    arrived(0, OWN, 0)
    send(3, OWN, 0)
    arrived(1, OWN, 1)
    send(4, OWN, 1)
    send(5, FACTOR, 0)
    send(6, FACTOR, 1)
    arrived(0, FACTOR, 1)
    send(5, FACTOR, 1)
    arrived(1, FACTOR, 0)
    send(6, FACTOR, 0)
    before[...] = jnp.zeros_like(before)
    ends_before[...] = jnp.zeros_like(ends_before)
    for d in range(hub + 1, 0, -1):

        @pl.when((z >= d) & (early | (z - d >= hub - 2)))
        def _():
            to_later(total, d).wait_recv()
            now = ring_z[d - 1, MODES : MODES + 16, :].astype(F32)
            g0, g1 = first_two(now, ends_before[...])
            head = jnp.where(early | (z - d > hub - 2), 1.0, 0.0) * (a127 * g0 + a126 * g1)
            arrived_sum = ring_z[d - 1, 0:MODES, :].astype(F32) + a384 * head
            before[...] = before[...] * a512 + arrived_sum
            ends_before[...] = now

    head = set_heads(0, firsts, ends_before[...])

    @pl.when(z == hub - 2)
    def _():
        whole = total[0:MODES, :].astype(F32) + a384 * head + a512 * before[...]
        half_sum[0:MODES, :] = whole.astype(BF16)
        half_sum[MODES : MODES + 16, :] = total[MODES : MODES + 16, :]

    send_sums(half_sum, range(hub + 1, 1, -1), lambda d: z == hub - 2)

    entering = starts[y] + jnp.exp(-float(ROWS) * y.astype(F32) * r) * before[...]
    since = jnp.maximum(y - 1, 0).astype(F32)
    entering = entering + jnp.where(y > 0, jnp.exp(-float(ROWS) * since * r) * head, 0.0)
    g0, g1, q126, q127 = (heads[y, i : i + 1, :] for i in range(4))
    later = entering + jnp.exp(r) * g0 + jnp.exp(2.0 * r) * g1
    rows = lax.broadcasted_iota(jnp.int32, (STEPS, LANES), 0)
    now = info[y, MODES : MODES + 16, :].astype(F32)
    s0 = tapped(taps, 0, everything, now[8:9], q127, q126)
    s1 = tapped(taps, 0, everything, now[9:10], now[8:9], q127)
    for l in range(tiles):
        cols = slice(l * LANES, (l + 1) * LANES)
        near0, near1, direct = near[0:1, cols], near[1:2, cols], skip[0:1, cols]
        values = jnp.zeros((STEPS, LANES), F32)
        for m in range(MODES):
            values += node3[m, :, cols] * jnp.where(
                rows < NODES, later[m : m + 1, cols], entering[m : m + 1, cols]
            )
        c0, c1 = g0[:, cols], g1[:, cols]
        h0 = s0[:, cols] * (values[NODES : NODES + 1] + (near0 + direct) * c0)
        h1 = s1[:, cols] * (values[NODES + 1 : NODES + 2] + near1 * c0 + (near0 + direct) * c1)
        values = jnp.where(rows == NODES, h0, jnp.where(rows == NODES + 1, h1, values))
        flow[0, :, cols] = values.astype(BF16)

    f_copies = {}
    for ex in (2, 1, 3, 0):
        for ec in range(CORES):
            slot = ex * CORES + ec
            if slot:
                to = x_peer(CHIPS - ex) + (core if ec == 0 else 1 - core)
                copy = pltpu.make_async_remote_copy(
                    flow.at[0], flow.at[slot], f_send.at[slot], f_recv.at[slot],
                    device_id=(seq, to), device_id_type=MESH,
                )
                copy.start()
                pending.append(copy.wait_send)
                f_copies[slot] = copy

    send(5, OWN, 0)
    send(6, OWN, 1)
    arrived(0, OWN, 1)
    send(5, OWN, 1)
    arrived(1, OWN, 0)
    send(6, OWN, 0)
    for kind in (FACTOR, OWN):
        for p in range(PIECES):
            arrived(3 + p, kind, p)
            send(7, kind, p)

    loads[8].wait()
    loads[9].wait()
    for n, slot in enumerate((0, 1, 6, 2, 7, 3, 4, 5)):
        if slot % CORES:
            for kind in (FACTOR, OWN):
                for p in range(PIECES):
                    arrived({1: 2, 7: 5, 3: 6, 5: 7}[slot], kind, p)
        if slot:
            f_copies[slot].wait_recv()
        values = flow[slot]
        entering = jnp.dot(
            weights[...], jnp.concatenate([values, values], axis=0), preferred_element_type=F32
        )
        blocks = []
        for p in range(PIECES):
            own, factor = hid[slot, OWN, p].astype(F32), hid[slot, FACTOR, p].astype(F32)
            blocks.append((own + factor * entering[:, p * half : (p + 1) * half]).astype(BF16))
        owner = x_peer(slot // CORES) + (core if slot % CORES == 0 else 1 - core)
        wrows = weight[pl.ds(pl.multiple_of(owner * width, width), width), :]
        part = jnp.dot(jnp.concatenate(blocks, axis=1), wrows, preferred_element_type=F32)
        if n:
            part = part + acc[...]
        acc[...] = part

    mixed = acc[...].astype(BF16)
    out_ref[...] = jnp.dot(back, mixed, preferred_element_type=F32).astype(BF16)

    for wait in pending:
        wait()


def interpolation():
    turn = np.pi * (2 * np.arange(NODES) + 1) / (2 * NODES)
    places = ((ROWS - 1) / 2 * (1 - np.cos(turn))).astype(np.float32)
    at = places.astype(np.float64)
    share = np.array([1 / np.prod(at[i] - np.delete(at, i)) for i in range(NODES)])
    weights = np.zeros((ROWS, STEPS))
    for t in range(2, ROWS):
        part = share / (t - at)
        weights[t, :NODES] = part / part.sum()
    weights[0, NODES] = weights[1, NODES + 1] = 1
    weights = weights.reshape(SUBS, STEPS, STEPS).swapaxes(0, 1).reshape(ROWS, STEPS)
    high = weights.astype(ml_dtypes.bfloat16)
    low = (weights - high.astype(np.float64)).astype(ml_dtypes.bfloat16)
    places = np.broadcast_to(np.append(places, [0, 1]).astype(np.float32)[:, None], (STEPS, LANES))
    return np.concatenate([high, low], axis=1), np.ascontiguousarray(places)


def per_device(zs, ys, query, key, value, short_taps, residue, rate, skip, out_weight):
    width = query.shape[1]
    tiles = width // LANES
    weights, places = interpolation()
    modes = pltpu.VMEM((MODES, width), F32)
    table = pltpu.VMEM((MODES, SUBS, width), F32)
    block = pltpu.VMEM((STEPS, SUBS, width), F32)
    dma = pltpu.SemaphoreType.DMA
    regular = pltpu.SemaphoreType.REGULAR
    scratch = [
        pltpu.VMEM((ROWS, width), BF16),
        pltpu.VMEM((ROWS, width), BF16),
        pltpu.VMEM((ROWS, width), BF16),
        pltpu.VMEM(short_taps.shape, F32),
        modes,
        modes,
        pltpu.VMEM((1, width), F32),
        pltpu.VMEM(out_weight.shape, BF16),
        pltpu.VMEM(weights.shape, BF16),
        pltpu.VMEM(places.shape, F32),
        table,
        table,
        table,
        block,
        block,
        block,
        table,
        block,
        block,
        pltpu.VMEM((STEPS, width), F32),
        pltpu.VMEM((MODES, STEPS, width), F32),
        modes,
        pltpu.VMEM((ys, MODES + 16, width), BF16),
        pltpu.VMEM((16, width), F32),
        pltpu.VMEM((ys, 8, width), F32),
        pltpu.VMEM((ys, MODES, width), F32),
        pltpu.VMEM((MODES + 16, width), BF16),
        pltpu.VMEM((MODES + 16, width), BF16),
        pltpu.VMEM((zs - 1, MODES + 16, width), BF16),
        modes,
        pltpu.VMEM((CHIPS * CORES, STEPS, width), BF16),
        pltpu.VMEM((CHIPS * CORES, 2, PIECES, ROWS, width // PIECES), BF16),
        pltpu.VMEM((ROWS, width), F32),
        dma((10,)),
        dma((ys - 1,)),
        dma((ys - 1,)),
        dma((zs - 1,)),
        dma((zs - 1,)),
        dma((len(ROUTES), 2, PIECES)),
        dma((len(ROUTES), 2, PIECES)),
        dma((CHIPS * CORES,)),
        dma((CHIPS * CORES,)),
        regular((zs - 1,)),
        regular((zs // 2 - 2,)),
    ]
    return pl.pallas_call(
        functools.partial(kernel, zs, ys),
        out_shape=pltpu.VMEM((ROWS, width), BF16),
        in_specs=[pl.BlockSpec(memory_space=pl.ANY)] * 10,
        out_specs=pl.BlockSpec(memory_space=pltpu.VMEM),
        scratch_shapes=scratch,
        compiler_params=pltpu.CompilerParams(
            collective_id=0, has_side_effects=True, vmem_limit_bytes=56 * 1024 * 1024
        ),
    )(
        query,
        key,
        value,
        short_taps,
        residue.T,
        rate.T,
        skip[None, :],
        out_weight,
        jnp.asarray(weights),
        jnp.asarray(places),
    )


def solution(mesh, ys=4):
    placed = (
        P("seq", "chan"),
        P("seq", "chan"),
        P("seq", "chan"),
        P(None, None, "chan"),
        P("chan", None),
        P("chan", None),
        P("chan"),
        P(None, "chan"),
    )
    return jax.shard_map(
        functools.partial(per_device, mesh.shape["seq"] // ys, ys),
        mesh=mesh,
        in_specs=placed,
        out_specs=P("seq", "chan"),
        check_vma=False,
    )
```

```python
import functools

import jax
import jax.numpy as jnp
import ml_dtypes
import numpy as np
from jax import lax
from jax.experimental import pallas as pl
from jax.experimental.pallas import tpu as pltpu
from jax.sharding import PartitionSpec as P

MESH = pl.DeviceIdType.MESH
F32 = jnp.float32
BF16 = jnp.bfloat16
MODES = 16
STEPS = 16
SUBS = 8
ROWS = STEPS * SUBS
LANES = 128
CHIPS = 4
CORES = 2
PIECES = 2
FACTOR, OWN = 0, 1
ROUTES = (
    (0, 6, "right"),
    (0, 2, "left"),
    (0, 1, "sibling"),
    (6, 4, "right"),
    (2, 4, "left"),
    (6, 7, "sibling"),
    (2, 3, "sibling"),
    (4, 5, "sibling"),
)
NODES = STEPS - 2


def tree_sum(array):
    while array.shape[0] > 1:
        half = array.shape[0] // 2
        array = array[:half] + array[half:]
    return array[0]


def lagged(block, last, last_but_one):
    one = jnp.concatenate([last[None], block[:-1]], axis=0)
    two = jnp.concatenate([last_but_one[None], one[:-1]], axis=0)
    return one, two


def tapped(taps, which, cols, now, one, two):
    return (
        taps[which, 0:1, cols] * now + taps[which, 1:2, cols] * one + taps[which, 2:3, cols] * two
    )


def kernel(
    zs,
    ys,
    q_hbm,
    k_hbm,
    v_hbm,
    taps_hbm,
    res_hbm,
    rate_hbm,
    skip_hbm,
    w_hbm,
    weights_hbm,
    places_hbm,
    out_ref,
    q_in,
    k_in,
    v_in,
    taps,
    res,
    rate,
    skip,
    weight,
    weights,
    places,
    rate3,
    decay3,
    gain3,
    xq,
    xk,
    xv,
    enter,
    local,
    query,
    near,
    node3,
    own_state,
    info,
    ends_before,
    heads,
    starts,
    total,
    half_sum,
    ring_z,
    before,
    flow,
    hid,
    acc,
    load_sem,
    y_send,
    y_recv,
    z_send,
    z_recv,
    g_send,
    g_recv,
    f_send,
    f_recv,
    ready_z,
    known,
):
    seq = lax.axis_index("seq")
    chan = lax.axis_index("chan")
    z, y = seq // ys, lax.rem(seq, ys)
    x, core = chan // CORES, lax.rem(chan, CORES)
    width = k_in.shape[1]
    tiles = width // LANES
    half = width // PIECES
    per = tiles // PIECES

    loads = [
        pltpu.make_async_copy(src, dst, load_sem.at[i])
        for i, (src, dst) in enumerate(
            [
                (rate_hbm, rate),
                (res_hbm, res),
                (taps_hbm, taps),
                (k_hbm, k_in),
                (v_hbm, v_in),
                (q_hbm, q_in),
                (skip_hbm, skip),
                (places_hbm, places),
                (weights_hbm, weights),
                (w_hbm, weight),
            ]
        )
    ]
    for i in (2, 5, 0, 1, 3, 4, 6, 7, 8, 9):
        loads[i].start()
    pending = []

    def at(zz, yy):
        return zz * ys + yy

    def signal(sem, s, c):
        pl.semaphore_signal(sem, inc=1, device_id=(s, c), device_id_type=MESH)

    def x_peer(e):
        return lax.rem(x + e, CHIPS) * CORES

    right = x_peer(1) + core
    left = x_peer(CHIPS - 1) + core
    sibling = x * CORES + 1 - core
    z_up = lax.rem(z + 1, zs)
    z_down = lax.rem(z + zs - 1, zs)

    barrier = pltpu.get_barrier_semaphore()
    for e in range(1, CHIPS):
        for c in range(CORES):
            signal(barrier, seq, x_peer(e) + c)
    signal(barrier, seq, sibling)
    for e in range(1, ys):
        signal(barrier, at(z, lax.rem(y + e, ys)), chan)
    hub = zs // 2
    early = z < hub
    place = lax.rem(z, hub)
    for d in range(1, zs):

        @pl.when(early & (z + d < zs) & ((z + d < hub) | (z >= hub - 2)))
        def _():
            signal(barrier, at(lax.rem(z + d, zs), y), chan)

    @pl.when((z >= hub) & (z < zs - 1))
    def _():
        signal(barrier, at(z_up, y), chan)

    @pl.when(z > hub)
    def _():
        signal(barrier, at(z_down, y), chan)

    row = lax.broadcasted_iota(jnp.int32, (ROWS, ROWS), 0)
    col = lax.broadcasted_iota(jnp.int32, (ROWS, ROWS), 1)
    order = jnp.where(col == (row & 7) * STEPS + (row >> 3), 1.0, 0.0).astype(BF16)
    back = jnp.where(row == (col & 7) * STEPS + (col >> 3), 1.0, 0.0).astype(BF16)

    def arranged(block):
        return jnp.dot(order, block, preferred_element_type=F32).reshape(STEPS, SUBS, width)

    sub = lax.broadcasted_iota(jnp.int32, (SUBS, LANES), 0)
    sub3 = lax.broadcasted_iota(jnp.int32, (MODES, SUBS, LANES), 1)
    first = sub == 0
    subf3 = sub3.astype(F32)

    loads[2].wait()
    loads[5].wait()
    xq[...] = arranged(q_in[...])

    pick = lax.broadcasted_iota(jnp.int32, (MODES, ROWS), 0)
    pos = lax.broadcasted_iota(jnp.int32, (MODES, ROWS), 1)

    def ends_of(base, block):
        i = pick - base
        ends = ((i >= 0) & (i < 2) & (pos == i)) | ((i >= 2) & (i < 4) & (pos == i + ROWS - 4))
        return jnp.dot(
            jnp.where(ends, 1.0, 0.0).astype(BF16), block[...], preferred_element_type=F32
        )

    def lags(block):
        last = jnp.where(first, 0.0, pltpu.roll(block[STEPS - 1], 1, 0))
        last_but_one = jnp.where(first, 0.0, pltpu.roll(block[STEPS - 2], 1, 0))
        return lagged(block, last, last_but_one)

    g_copies = {}

    def send(route, kind, piece):
        slot, to_slot, to = ROUTES[route]
        to = {"right": right, "left": left, "sibling": sibling}[to]
        copy = pltpu.make_async_remote_copy(
            hid.at[slot, kind, piece],
            hid.at[to_slot, kind, piece],
            g_send.at[route, kind, piece],
            g_recv.at[route, kind, piece],
            device_id=(seq, to),
            device_id_type=MESH,
        )
        copy.start()
        pending.append(copy.wait_send)
        g_copies[route, kind, piece] = copy

    def arrived(route, kind, piece):
        g_copies[route, kind, piece].wait_recv()

    for l in range(tiles):
        cols = slice(l * LANES, (l + 1) * LANES)
        qb = xq[:, :, cols]
        qb = tapped(taps, 0, cols, qb, *lags(qb))
        query[:, :, cols] = qb
        qb = jnp.concatenate([jnp.where(first[None], 1.0, qb[:2]), qb[2:]], axis=0)
        to = slice(l % per * LANES, (l % per + 1) * LANES)
        hid[0, FACTOR, l // per, :, to] = qb.reshape(ROWS, LANES).astype(BF16)
    loads[3].wait()
    loads[4].wait()
    info[y, MODES : MODES + 16, :] = (ends_of(0, k_in) + ends_of(4, v_in) + ends_of(8, q_in)).astype(BF16)

    pl.semaphore_wait(
        barrier,
        (CORES * CHIPS - 1 + ys - 1)
        + jnp.where(early, z, 2 + jnp.where(z > hub, 1, 0) + jnp.where(z < zs - 1, 1, 0))
    )
    for d in range(1, zs):

        @pl.when((z >= d) & (z - d < hub) & (early | (z - d >= hub - 2)))
        def _():
            signal(ready_z.at[d - 1], at(lax.rem(z + zs - d, zs), y), chan)

    @pl.when((z > hub) & (z < zs - 1))
    def _():
        signal(known.at[0], at(z_down, y), chan)

    def to_group(part):
        copies = []
        for e in range(1, ys):
            copy = pltpu.make_async_remote_copy(
                info.at[y, pl.ds(MODES * part, MODES)],
                info.at[y, pl.ds(MODES * part, MODES)],
                y_send.at[part, e - 1],
                y_recv.at[part, e - 1],
                device_id=(at(z, lax.rem(y + e, ys)), chan),
                device_id_type=MESH,
            )
            copy.start()
            pending.append(copy.wait_send)
            copies.append(copy)
        return copies

    row_copies = to_group(1)

    for route, piece in ((0, 0), (1, 1), (0, 1), (1, 0), (2, 0), (2, 1)):
        send(route, FACTOR, piece)

    xk[...] = arranged(k_in[...])
    xv[...] = arranged(v_in[...])
    loads[0].wait()
    loads[1].wait()
    r = rate[...]
    series = r * (1.0 - r * (1 / 2) * (1.0 - r * (1 / 3) * (1.0 - r * (1 / 4) * (1.0 - r * (1 / 5) * (1.0 - r * (1 / 6))))))
    gain = res[...] * series
    decay = jnp.exp(-r)
    for m in range(MODES):
        rate3[m] = jnp.broadcast_to(r[m : m + 1], (SUBS, width))
        decay3[m] = jnp.broadcast_to(decay[m : m + 1], (SUBS, width))
        gain3[m] = jnp.broadcast_to(gain[m : m + 1], (SUBS, width))

    for l in range(tiles):
        cols = slice(l * LANES, (l + 1) * LANES)
        kb, vb = xk[:, :, cols], xv[:, :, cols]
        g = tapped(taps, 1, cols, kb, *lags(kb)) * tapped(taps, 2, cols, vb, *lags(vb))
        g = jnp.concatenate([jnp.where(first[None], 0.0, g[:2]), g[2:]], axis=0)
        local[:, :, cols] = g
        a = decay3[:, :, cols]
        state = jnp.broadcast_to(g[0][None], a.shape)
        for j in range(1, STEPS):
            state = state * a + g[j][None]
        step = a
        for _ in range(4):
            step = step * step
        for reach in (1, 2, 4):
            state = state + jnp.where(sub3 >= reach, step, 0.0) * pltpu.roll(state, reach, 1)
            step = step * step
        enter[:, :, cols] = jnp.where(sub3 >= 1, pltpu.roll(state, 1, 1), 0.0)
        for m in range(MODES):
            own_state[m : m + 1, cols] = state[m, SUBS - 1 : SUBS, :]

    info[y, 0:MODES, :] = own_state[...].astype(BF16)

    y_copies = to_group(0)

    loads[6].wait()
    for p in range(PIECES):
        for i in range(per):
            l = p * per + i
            cols = slice(l * LANES, (l + 1) * LANES)
            r3, a, w = rate3[:, :, cols], decay3[:, :, cols], gain3[:, :, cols]
            close = w * jnp.exp(-subf3 * r3)
            a8 = a * a
            a8 = a8 * a8
            a8 = a8 * a8
            near[0:SUBS, cols] = tree_sum(close)
            near[SUBS : 2 * SUBS, cols] = tree_sum(close * a8)
            g = local[:, :, cols]
            out = g * skip[0:1, cols]
            for d in range(STEPS):
                add = g[: STEPS - d] * near[d : d + 1, cols][None]
                out = out + add if d == 0 else jnp.concatenate([out[:d], out[d:] + add], axis=0)
            state = w * a * enter[:, :, cols]
            own = []
            for j in range(STEPS):
                line = query[j, :, cols] * (out[j] + tree_sum(state))
                if j < STEPS - 1:
                    state = state * a
                own.append(jnp.where(first, 0.0, line) if j < 2 else line)
            to = slice(i * LANES, (i + 1) * LANES)
            hid[0, OWN, p, :, to] = jnp.concatenate(own, axis=0).astype(BF16)
        send(0, OWN, p)
        send(2, OWN, p)
    for p in reversed(range(PIECES)):
        send(1, OWN, p)

    for i in range(hub - 2):

        @pl.when((z >= hub) & (z + 2 + i < zs))
        def _():
            pl.semaphore_wait(known.at[i], 1)
            if i < hub - 3:
                pl.when(z > hub)(lambda: signal(known.at[i + 1], at(z_down, y), chan))

    to_half = hub - z

    def to_later(part, source, d):
        return pltpu.make_async_remote_copy(
            source.at[pl.ds(MODES * part, MODES)],
            ring_z.at[d - 1, pl.ds(MODES * part, MODES)],
            z_send.at[part, d - 1],
            z_recv.at[part, d - 1],
            device_id=(at(lax.rem(z + d, zs), y), chan),
            device_id_type=MESH,
        )

    def send_later(part, source, distances, among):
        for d in distances:

            @pl.when((z + d < zs) & among(d))
            def _():
                if part or d > 1:

                    @pl.when(early)
                    def _():
                        pl.semaphore_wait(ready_z.at[d - 1], 1)

                to_later(part, source, d).start()

            pending.append(
                functools.partial(
                    pl.when((z + d < zs) & among(d)), to_later(part, source, d).wait_send
                )
            )

    def in_half(d):
        return (z >= hub) | (d < to_half)

    for copy in row_copies:
        copy.wait_recv()
    total[MODES : MODES + 16, :] = info[ys - 1, MODES : MODES + 16, :]
    send_later(1, total, (1,), lambda d: z < zs - 1)

    arrived(0, FACTOR, 0)
    send(3, FACTOR, 0)
    arrived(1, FACTOR, 1)
    send(4, FACTOR, 1)

    r = rate[...]
    a126 = jnp.exp(-(ROWS - 2.0) * r)
    a127 = jnp.exp(-(ROWS - 1.0) * r)
    a128 = jnp.exp(-float(ROWS) * r)
    everything = slice(0, width)
    loads[7].wait()
    for l in range(tiles):
        cols = slice(l * LANES, (l + 1) * LANES)
        for m in range(MODES):
            node3[m, :, cols] = gain3[m, 0:1, cols] * jnp.exp(
                -(places[...] + 1.0) * rate[m : m + 1, cols]
            )

    for copy in y_copies:
        copy.wait_recv()
    a512 = jnp.exp(-float(ROWS * ys) * r)

    def first_two(now, ends):
        k0, k1, v0, v1 = (now[i : i + 1] for i in (0, 1, 4, 5))
        k126, k127, v126, v127 = (ends[i : i + 1] for i in (2, 3, 6, 7))
        g0 = tapped(taps, 1, everything, k0, k127, k126) * tapped(
            taps, 2, everything, v0, v127, v126
        )
        g1 = tapped(taps, 1, everything, k1, k0, k127) * tapped(taps, 2, everything, v1, v0, v127)
        return g0, g1

    def set_heads(e, now, ends):
        g0, g1 = first_two(now, ends)
        for i, line in enumerate((g0, g1, ends[10:11], ends[11:12])):
            heads[e, i : i + 1, :] = line
        return a127 * g0 + a126 * g1

    @pl.when(z == 0)
    def _():
        ends_before[...] = jnp.zeros_like(ends_before)

    @pl.when(z > 0)
    def _():
        to_later(1, total, 1).wait_recv()
        ends_before[...] = ring_z[0, MODES : MODES + 16, :].astype(F32)

    ends = ends_before[...]
    start = jnp.zeros_like(r)
    for e in range(ys):
        now = info[e, MODES : MODES + 16, :].astype(F32)
        starts[e] = start
        start = start * a128 + (info[e, 0:MODES, :].astype(F32) + set_heads(e, now, ends))
        ends = now
    total[0:MODES, :] = start.astype(BF16)

    send_later(0, total, range(hub - 1, 0, -1), in_half)
    send_later(0, total, range(hub, 0, -1), lambda d: z == hub - 1)

    arrived(0, OWN, 0)
    send(3, OWN, 0)
    arrived(1, OWN, 1)
    send(4, OWN, 1)
    send(5, FACTOR, 0)
    send(6, FACTOR, 1)
    arrived(0, FACTOR, 1)
    send(5, FACTOR, 1)
    arrived(1, FACTOR, 0)
    send(6, FACTOR, 0)
    before[...] = jnp.zeros_like(before)
    for d in range(hub + 1, 0, -1):

        @pl.when((z >= d) & (early | (z - d >= hub - 2)))
        def _():
            to_later(0, total, d).wait_recv()
            before[...] = before[...] * a512 + ring_z[d - 1, 0:MODES, :].astype(F32)

    @pl.when(z == hub - 2)
    def _():
        half_sum[...] = (total[0:MODES, :].astype(F32) + a512 * before[...]).astype(BF16)

    send_later(0, half_sum, range(hub + 1, 1, -1), lambda d: z == hub - 2)

    entering = starts[y] + jnp.exp(-float(ROWS) * y.astype(F32) * r) * before[...]
    g0, g1, q126, q127 = (heads[y, i : i + 1, :] for i in range(4))
    later = entering + jnp.exp(r) * g0 + jnp.exp(2.0 * r) * g1
    rows = lax.broadcasted_iota(jnp.int32, (STEPS, LANES), 0)
    now = info[y, MODES : MODES + 16, :].astype(F32)
    s0 = tapped(taps, 0, everything, now[8:9], q127, q126)
    s1 = tapped(taps, 0, everything, now[9:10], now[8:9], q127)
    for l in range(tiles):
        cols = slice(l * LANES, (l + 1) * LANES)
        near0, near1, direct = near[0:1, cols], near[1:2, cols], skip[0:1, cols]
        values = jnp.zeros((STEPS, LANES), F32)
        for m in range(MODES):
            values += node3[m, :, cols] * jnp.where(
                rows < NODES, later[m : m + 1, cols], entering[m : m + 1, cols]
            )
        c0, c1 = g0[:, cols], g1[:, cols]
        h0 = s0[:, cols] * (values[NODES : NODES + 1] + (near0 + direct) * c0)
        h1 = s1[:, cols] * (values[NODES + 1 : NODES + 2] + near1 * c0 + (near0 + direct) * c1)
        values = jnp.where(rows == NODES, h0, jnp.where(rows == NODES + 1, h1, values))
        flow[0, :, cols] = values.astype(BF16)

    f_copies = {}
    for ex in (2, 1, 3, 0):
        for ec in range(CORES):
            slot = ex * CORES + ec
            if slot:
                to = x_peer(CHIPS - ex) + (core if ec == 0 else 1 - core)
                copy = pltpu.make_async_remote_copy(
                    flow.at[0], flow.at[slot], f_send.at[slot], f_recv.at[slot],
                    device_id=(seq, to), device_id_type=MESH,
                )
                copy.start()
                pending.append(copy.wait_send)
                f_copies[slot] = copy

    send(5, OWN, 0)
    send(6, OWN, 1)
    arrived(0, OWN, 1)
    send(5, OWN, 1)
    arrived(1, OWN, 0)
    send(6, OWN, 0)
    for kind in (FACTOR, OWN):
        for p in range(PIECES):
            arrived(3 + p, kind, p)
            send(7, kind, p)

    loads[8].wait()
    loads[9].wait()
    for n, slot in enumerate((0, 1, 6, 2, 7, 3, 4, 5)):
        if slot % CORES:
            for kind in (FACTOR, OWN):
                for p in range(PIECES):
                    arrived({1: 2, 7: 5, 3: 6, 5: 7}[slot], kind, p)
        if slot:
            f_copies[slot].wait_recv()
        values = flow[slot]
        entering = jnp.dot(
            weights[...], jnp.concatenate([values, values], axis=0), preferred_element_type=F32
        )
        blocks = []
        for p in range(PIECES):
            own, factor = hid[slot, OWN, p].astype(F32), hid[slot, FACTOR, p].astype(F32)
            blocks.append((own + factor * entering[:, p * half : (p + 1) * half]).astype(BF16))
        owner = x_peer(slot // CORES) + (core if slot % CORES == 0 else 1 - core)
        wrows = weight[pl.ds(pl.multiple_of(owner * width, width), width), :]
        part = jnp.dot(jnp.concatenate(blocks, axis=1), wrows, preferred_element_type=F32)
        if n:
            part = part + acc[...]
        acc[...] = part

    mixed = acc[...].astype(BF16)
    out_ref[...] = jnp.dot(back, mixed, preferred_element_type=F32).astype(BF16)

    for wait in pending:
        wait()


def interpolation():
    turn = np.pi * (2 * np.arange(NODES) + 1) / (2 * NODES)
    places = ((ROWS - 1) / 2 * (1 - np.cos(turn))).astype(np.float32)
    at = places.astype(np.float64)
    share = np.array([1 / np.prod(at[i] - np.delete(at, i)) for i in range(NODES)])
    weights = np.zeros((ROWS, STEPS))
    for t in range(2, ROWS):
        part = share / (t - at)
        weights[t, :NODES] = part / part.sum()
    weights[0, NODES] = weights[1, NODES + 1] = 1
    weights = weights.reshape(SUBS, STEPS, STEPS).swapaxes(0, 1).reshape(ROWS, STEPS)
    high = weights.astype(ml_dtypes.bfloat16)
    low = (weights - high.astype(np.float64)).astype(ml_dtypes.bfloat16)
    places = np.broadcast_to(np.append(places, [0, 1]).astype(np.float32)[:, None], (STEPS, LANES))
    return np.concatenate([high, low], axis=1), np.ascontiguousarray(places)


def per_device(zs, ys, query, key, value, short_taps, residue, rate, skip, out_weight):
    width = query.shape[1]
    tiles = width // LANES
    weights, places = interpolation()
    modes = pltpu.VMEM((MODES, width), F32)
    table = pltpu.VMEM((MODES, SUBS, width), F32)
    block = pltpu.VMEM((STEPS, SUBS, width), F32)
    dma = pltpu.SemaphoreType.DMA
    regular = pltpu.SemaphoreType.REGULAR
    scratch = [
        pltpu.VMEM((ROWS, width), BF16),
        pltpu.VMEM((ROWS, width), BF16),
        pltpu.VMEM((ROWS, width), BF16),
        pltpu.VMEM(short_taps.shape, F32),
        modes,
        modes,
        pltpu.VMEM((1, width), F32),
        pltpu.VMEM(out_weight.shape, BF16),
        pltpu.VMEM(weights.shape, BF16),
        pltpu.VMEM(places.shape, F32),
        table,
        table,
        table,
        block,
        block,
        block,
        table,
        block,
        block,
        pltpu.VMEM((STEPS, width), F32),
        pltpu.VMEM((MODES, STEPS, width), F32),
        modes,
        pltpu.VMEM((ys, MODES + 16, width), BF16),
        pltpu.VMEM((16, width), F32),
        pltpu.VMEM((ys, 8, width), F32),
        pltpu.VMEM((ys, MODES, width), F32),
        pltpu.VMEM((MODES + 16, width), BF16),
        pltpu.VMEM((MODES, width), BF16),
        pltpu.VMEM((zs - 1, MODES + 16, width), BF16),
        modes,
        pltpu.VMEM((CHIPS * CORES, STEPS, width), BF16),
        pltpu.VMEM((CHIPS * CORES, 2, PIECES, ROWS, width // PIECES), BF16),
        pltpu.VMEM((ROWS, width), F32),
        dma((10,)),
        dma((2, ys - 1)),
        dma((2, ys - 1)),
        dma((2, zs - 1)),
        dma((2, zs - 1)),
        dma((len(ROUTES), 2, PIECES)),
        dma((len(ROUTES), 2, PIECES)),
        dma((CHIPS * CORES,)),
        dma((CHIPS * CORES,)),
        regular((zs - 1,)),
        regular((zs // 2 - 2,)),
    ]
    return pl.pallas_call(
        functools.partial(kernel, zs, ys),
        out_shape=pltpu.VMEM((ROWS, width), BF16),
        in_specs=[pl.BlockSpec(memory_space=pl.ANY)] * 10,
        out_specs=pl.BlockSpec(memory_space=pltpu.VMEM),
        scratch_shapes=scratch,
        compiler_params=pltpu.CompilerParams(
            collective_id=0, has_side_effects=True, vmem_limit_bytes=56 * 1024 * 1024
        ),
    )(
        query,
        key,
        value,
        short_taps,
        residue.T,
        rate.T,
        skip[None, :],
        out_weight,
        jnp.asarray(weights),
        jnp.asarray(places),
    )


def solution(mesh, ys=4):
    placed = (
        P("seq", "chan"),
        P("seq", "chan"),
        P("seq", "chan"),
        P(None, None, "chan"),
        P("chan", None),
        P("chan", None),
        P("chan"),
        P(None, "chan"),
    )
    return jax.shard_map(
        functools.partial(per_device, mesh.shape["seq"] // ys, ys),
        mesh=mesh,
        in_specs=placed,
        out_specs=P("seq", "chan"),
        check_vma=False,
    )
```

```python
import functools

import jax
import jax.numpy as jnp
import ml_dtypes
import numpy as np
from jax import lax
from jax.experimental import pallas as pl
from jax.experimental.pallas import tpu as pltpu
from jax.sharding import PartitionSpec as P

MESH = pl.DeviceIdType.MESH
F32 = jnp.float32
BF16 = jnp.bfloat16
MODES = 16
STEPS = 16
SUBS = 8
ROWS = STEPS * SUBS
LANES = 128
CHIPS = 4
CORES = 2
PIECES = 2
FACTOR, OWN = 0, 1
ROUTES = (
    (0, 6, "right"),
    (0, 2, "left"),
    (0, 1, "sibling"),
    (6, 4, "right"),
    (2, 4, "left"),
    (6, 7, "sibling"),
    (2, 3, "sibling"),
    (4, 5, "sibling"),
)
NODES = STEPS - 2


def tree_sum(array):
    while array.shape[0] > 1:
        half = array.shape[0] // 2
        array = array[:half] + array[half:]
    return array[0]


def lagged(block, last, last_but_one):
    one = jnp.concatenate([last[None], block[:-1]], axis=0)
    two = jnp.concatenate([last_but_one[None], one[:-1]], axis=0)
    return one, two


def tapped(taps, which, cols, now, one, two):
    return (
        taps[which, 0:1, cols] * now + taps[which, 1:2, cols] * one + taps[which, 2:3, cols] * two
    )


def kernel(
    zs,
    ys,
    q_hbm,
    k_hbm,
    v_hbm,
    taps_hbm,
    res_hbm,
    rate_hbm,
    skip_hbm,
    w_hbm,
    weights_hbm,
    places_hbm,
    out_ref,
    q_in,
    k_in,
    v_in,
    taps,
    res,
    rate,
    skip,
    weight,
    weights,
    places,
    rate3,
    decay3,
    gain3,
    xq,
    xk,
    xv,
    enter,
    local,
    query,
    near,
    node3,
    own_state,
    info,
    ends_before,
    heads,
    starts,
    total,
    half_sum,
    ring_z,
    before,
    flow,
    hid,
    acc,
    load_sem,
    y_send,
    y_recv,
    z_send,
    z_recv,
    g_send,
    g_recv,
    f_send,
    f_recv,
    ready_z,
    known,
):
    seq = lax.axis_index("seq")
    chan = lax.axis_index("chan")
    z, y = seq // ys, lax.rem(seq, ys)
    x, core = chan // CORES, lax.rem(chan, CORES)
    width = k_in.shape[1]
    tiles = width // LANES
    half = width // PIECES
    per = tiles // PIECES

    loads = [
        pltpu.make_async_copy(src, dst, load_sem.at[i])
        for i, (src, dst) in enumerate(
            [
                (rate_hbm, rate),
                (res_hbm, res),
                (taps_hbm, taps),
                (k_hbm, k_in),
                (v_hbm, v_in),
                (q_hbm, q_in),
                (skip_hbm, skip),
                (places_hbm, places),
                (weights_hbm, weights),
                (w_hbm, weight),
            ]
        )
    ]
    for i in (2, 5, 0, 1, 3, 4, 6, 7, 8, 9):
        loads[i].start()
    pending = []

    def at(zz, yy):
        return zz * ys + yy

    def signal(sem, s, c):
        pl.semaphore_signal(sem, inc=1, device_id=(s, c), device_id_type=MESH)

    def x_peer(e):
        return lax.rem(x + e, CHIPS) * CORES

    right = x_peer(1) + core
    left = x_peer(CHIPS - 1) + core
    sibling = x * CORES + 1 - core
    z_up = lax.rem(z + 1, zs)
    z_down = lax.rem(z + zs - 1, zs)

    barrier = pltpu.get_barrier_semaphore()
    for e in range(1, CHIPS):
        for c in range(CORES):
            signal(barrier, seq, x_peer(e) + c)
    signal(barrier, seq, sibling)
    for e in range(1, ys):
        signal(barrier, at(z, lax.rem(y + e, ys)), chan)
    hub = zs // 2
    early = z < hub
    place = lax.rem(z, hub)
    for d in range(1, zs):

        @pl.when(early & (z + d < zs) & ((z + d < hub) | (z >= hub - 2)))
        def _():
            signal(barrier, at(lax.rem(z + d, zs), y), chan)

    @pl.when((z >= hub) & (z < zs - 1))
    def _():
        signal(barrier, at(z_up, y), chan)

    @pl.when(z > hub)
    def _():
        signal(barrier, at(z_down, y), chan)

    row = lax.broadcasted_iota(jnp.int32, (ROWS, ROWS), 0)
    col = lax.broadcasted_iota(jnp.int32, (ROWS, ROWS), 1)
    order = jnp.where(col == (row & 7) * STEPS + (row >> 3), 1.0, 0.0).astype(BF16)
    back = jnp.where(row == (col & 7) * STEPS + (col >> 3), 1.0, 0.0).astype(BF16)

    def arranged(block):
        return jnp.dot(order, block, preferred_element_type=F32).reshape(STEPS, SUBS, width)

    sub = lax.broadcasted_iota(jnp.int32, (SUBS, LANES), 0)
    sub3 = lax.broadcasted_iota(jnp.int32, (MODES, SUBS, LANES), 1)
    first = sub == 0
    subf3 = sub3.astype(F32)

    loads[2].wait()
    loads[5].wait()
    xq[...] = arranged(q_in[...])

    pick = lax.broadcasted_iota(jnp.int32, (MODES, ROWS), 0)
    pos = lax.broadcasted_iota(jnp.int32, (MODES, ROWS), 1)

    def ends_of(base, block):
        i = pick - base
        ends = ((i >= 0) & (i < 2) & (pos == i)) | ((i >= 2) & (i < 4) & (pos == i + ROWS - 4))
        return jnp.dot(
            jnp.where(ends, 1.0, 0.0).astype(BF16), block[...], preferred_element_type=F32
        )

    def lags(block):
        last = jnp.where(first, 0.0, pltpu.roll(block[STEPS - 1], 1, 0))
        last_but_one = jnp.where(first, 0.0, pltpu.roll(block[STEPS - 2], 1, 0))
        return lagged(block, last, last_but_one)

    g_copies = {}

    def send(route, kind, piece):
        slot, to_slot, to = ROUTES[route]
        to = {"right": right, "left": left, "sibling": sibling}[to]
        copy = pltpu.make_async_remote_copy(
            hid.at[slot, kind, piece],
            hid.at[to_slot, kind, piece],
            g_send.at[route, kind, piece],
            g_recv.at[route, kind, piece],
            device_id=(seq, to),
            device_id_type=MESH,
        )
        copy.start()
        pending.append(copy.wait_send)
        g_copies[route, kind, piece] = copy

    def arrived(route, kind, piece):
        g_copies[route, kind, piece].wait_recv()

    for l in range(tiles):
        cols = slice(l * LANES, (l + 1) * LANES)
        qb = xq[:, :, cols]
        qb = tapped(taps, 0, cols, qb, *lags(qb))
        query[:, :, cols] = qb
        qb = jnp.concatenate([jnp.where(first[None], 1.0, qb[:2]), qb[2:]], axis=0)
        to = slice(l % per * LANES, (l % per + 1) * LANES)
        hid[0, FACTOR, l // per, :, to] = qb.reshape(ROWS, LANES).astype(BF16)
    loads[3].wait()
    loads[4].wait()
    info[y, MODES : MODES + 16, :] = (ends_of(0, k_in) + ends_of(4, v_in) + ends_of(8, q_in)).astype(BF16)

    pl.semaphore_wait(
        barrier,
        (CORES * CHIPS - 1 + ys - 1)
        + jnp.where(early, z, 2 + jnp.where(z > hub, 1, 0) + jnp.where(z < zs - 1, 1, 0))
    )
    for d in range(1, zs):

        @pl.when((z >= d) & (z - d < hub) & (early | (z - d >= hub - 2)))
        def _():
            signal(ready_z.at[d - 1], at(lax.rem(z + zs - d, zs), y), chan)

    @pl.when((z > hub) & (z < zs - 1))
    def _():
        signal(known.at[0], at(z_down, y), chan)

    def to_group(part):
        copies = []
        for e in sorted(range(1, ys), key=lambda e: -min(e, ys - e)):
            copy = pltpu.make_async_remote_copy(
                info.at[y, pl.ds(MODES * part, MODES)],
                info.at[y, pl.ds(MODES * part, MODES)],
                y_send.at[part, e - 1],
                y_recv.at[part, e - 1],
                device_id=(at(z, lax.rem(y + e, ys)), chan),
                device_id_type=MESH,
            )
            copy.start()
            pending.append(copy.wait_send)
            copies.append(copy)
        return copies

    row_copies = to_group(1)

    for route, piece in ((0, 0), (1, 1), (0, 1), (1, 0), (2, 0), (2, 1)):
        send(route, FACTOR, piece)

    xk[...] = arranged(k_in[...])
    xv[...] = arranged(v_in[...])
    loads[0].wait()
    loads[1].wait()
    r = rate[...]
    series = r * (1.0 - r * (1 / 2) * (1.0 - r * (1 / 3) * (1.0 - r * (1 / 4) * (1.0 - r * (1 / 5) * (1.0 - r * (1 / 6))))))
    gain = res[...] * series
    decay = jnp.exp(-r)
    for m in range(MODES):
        rate3[m] = jnp.broadcast_to(r[m : m + 1], (SUBS, width))
        decay3[m] = jnp.broadcast_to(decay[m : m + 1], (SUBS, width))
        gain3[m] = jnp.broadcast_to(gain[m : m + 1], (SUBS, width))

    for l in range(tiles):
        cols = slice(l * LANES, (l + 1) * LANES)
        kb, vb = xk[:, :, cols], xv[:, :, cols]
        g = tapped(taps, 1, cols, kb, *lags(kb)) * tapped(taps, 2, cols, vb, *lags(vb))
        g = jnp.concatenate([jnp.where(first[None], 0.0, g[:2]), g[2:]], axis=0)
        local[:, :, cols] = g
        a = decay3[:, :, cols]
        state = jnp.broadcast_to(g[0][None], a.shape)
        for j in range(1, STEPS):
            state = state * a + g[j][None]
        step = a
        for _ in range(4):
            step = step * step
        for reach in (1, 2, 4):
            state = state + jnp.where(sub3 >= reach, step, 0.0) * pltpu.roll(state, reach, 1)
            step = step * step
        enter[:, :, cols] = jnp.where(sub3 >= 1, pltpu.roll(state, 1, 1), 0.0)
        for m in range(MODES):
            own_state[m : m + 1, cols] = state[m, SUBS - 1 : SUBS, :]

    info[y, 0:MODES, :] = own_state[...].astype(BF16)

    y_copies = to_group(0)

    loads[6].wait()
    for p in range(PIECES):
        for i in range(per):
            l = p * per + i
            cols = slice(l * LANES, (l + 1) * LANES)
            r3, a, w = rate3[:, :, cols], decay3[:, :, cols], gain3[:, :, cols]
            close = w * jnp.exp(-subf3 * r3)
            a8 = a * a
            a8 = a8 * a8
            a8 = a8 * a8
            near[0:SUBS, cols] = tree_sum(close)
            near[SUBS : 2 * SUBS, cols] = tree_sum(close * a8)
            g = local[:, :, cols]
            out = g * skip[0:1, cols]
            for d in range(STEPS):
                add = g[: STEPS - d] * near[d : d + 1, cols][None]
                out = out + add if d == 0 else jnp.concatenate([out[:d], out[d:] + add], axis=0)
            state = w * a * enter[:, :, cols]
            own = []
            for j in range(STEPS):
                line = query[j, :, cols] * (out[j] + tree_sum(state))
                if j < STEPS - 1:
                    state = state * a
                own.append(jnp.where(first, 0.0, line) if j < 2 else line)
            to = slice(i * LANES, (i + 1) * LANES)
            hid[0, OWN, p, :, to] = jnp.concatenate(own, axis=0).astype(BF16)
        send(0, OWN, p)
        send(2, OWN, p)
    for p in reversed(range(PIECES)):
        send(1, OWN, p)

    for i in range(hub - 2):

        @pl.when((z >= hub) & (z + 2 + i < zs))
        def _():
            pl.semaphore_wait(known.at[i], 1)
            if i < hub - 3:
                pl.when(z > hub)(lambda: signal(known.at[i + 1], at(z_down, y), chan))

    to_half = hub - z

    def to_later(part, source, d):
        return pltpu.make_async_remote_copy(
            source.at[pl.ds(MODES * part, MODES)],
            ring_z.at[d - 1, pl.ds(MODES * part, MODES)],
            z_send.at[part, d - 1],
            z_recv.at[part, d - 1],
            device_id=(at(lax.rem(z + d, zs), y), chan),
            device_id_type=MESH,
        )

    def send_later(part, source, distances, among):
        for d in distances:

            @pl.when((z + d < zs) & among(d))
            def _():
                if part or d > 1:

                    @pl.when(early)
                    def _():
                        pl.semaphore_wait(ready_z.at[d - 1], 1)

                to_later(part, source, d).start()

            pending.append(
                functools.partial(
                    pl.when((z + d < zs) & among(d)), to_later(part, source, d).wait_send
                )
            )

    def in_half(d):
        return (z >= hub) | (d < to_half)

    for copy in row_copies:
        copy.wait_recv()
    total[MODES : MODES + 16, :] = info[ys - 1, MODES : MODES + 16, :]
    send_later(1, total, (1,), lambda d: z < zs - 1)

    arrived(0, FACTOR, 0)
    send(3, FACTOR, 0)
    arrived(1, FACTOR, 1)
    send(4, FACTOR, 1)

    r = rate[...]
    a126 = jnp.exp(-(ROWS - 2.0) * r)
    a127 = jnp.exp(-(ROWS - 1.0) * r)
    a128 = jnp.exp(-float(ROWS) * r)
    everything = slice(0, width)
    loads[7].wait()
    for l in range(tiles):
        cols = slice(l * LANES, (l + 1) * LANES)
        for m in range(MODES):
            node3[m, :, cols] = gain3[m, 0:1, cols] * jnp.exp(
                -(places[...] + 1.0) * rate[m : m + 1, cols]
            )

    for copy in y_copies:
        copy.wait_recv()
    a512 = jnp.exp(-float(ROWS * ys) * r)

    def first_two(now, ends):
        k0, k1, v0, v1 = (now[i : i + 1] for i in (0, 1, 4, 5))
        k126, k127, v126, v127 = (ends[i : i + 1] for i in (2, 3, 6, 7))
        g0 = tapped(taps, 1, everything, k0, k127, k126) * tapped(
            taps, 2, everything, v0, v127, v126
        )
        g1 = tapped(taps, 1, everything, k1, k0, k127) * tapped(taps, 2, everything, v1, v0, v127)
        return g0, g1

    def set_heads(e, now, ends):
        g0, g1 = first_two(now, ends)
        for i, line in enumerate((g0, g1, ends[10:11], ends[11:12])):
            heads[e, i : i + 1, :] = line
        return a127 * g0 + a126 * g1

    @pl.when(z == 0)
    def _():
        ends_before[...] = jnp.zeros_like(ends_before)

    @pl.when(z > 0)
    def _():
        to_later(1, total, 1).wait_recv()
        ends_before[...] = ring_z[0, MODES : MODES + 16, :].astype(F32)

    ends = ends_before[...]
    start = jnp.zeros_like(r)
    for e in range(ys):
        now = info[e, MODES : MODES + 16, :].astype(F32)
        starts[e] = start
        start = start * a128 + (info[e, 0:MODES, :].astype(F32) + set_heads(e, now, ends))
        ends = now
    total[0:MODES, :] = start.astype(BF16)

    send_later(0, total, range(hub - 1, 0, -1), in_half)
    send_later(0, total, range(hub, 0, -1), lambda d: z == hub - 1)

    arrived(0, OWN, 0)
    send(3, OWN, 0)
    arrived(1, OWN, 1)
    send(4, OWN, 1)
    send(5, FACTOR, 0)
    send(6, FACTOR, 1)
    arrived(0, FACTOR, 1)
    send(5, FACTOR, 1)
    arrived(1, FACTOR, 0)
    send(6, FACTOR, 0)
    before[...] = jnp.zeros_like(before)
    for d in range(hub + 1, 0, -1):

        @pl.when((z >= d) & (early | (z - d >= hub - 2)))
        def _():
            to_later(0, total, d).wait_recv()
            before[...] = before[...] * a512 + ring_z[d - 1, 0:MODES, :].astype(F32)

    @pl.when(z == hub - 2)
    def _():
        half_sum[...] = (total[0:MODES, :].astype(F32) + a512 * before[...]).astype(BF16)

    send_later(0, half_sum, range(hub + 1, 1, -1), lambda d: z == hub - 2)

    entering = starts[y] + jnp.exp(-float(ROWS) * y.astype(F32) * r) * before[...]
    g0, g1, q126, q127 = (heads[y, i : i + 1, :] for i in range(4))
    later = entering + jnp.exp(r) * g0 + jnp.exp(2.0 * r) * g1
    rows = lax.broadcasted_iota(jnp.int32, (STEPS, LANES), 0)
    now = info[y, MODES : MODES + 16, :].astype(F32)
    s0 = tapped(taps, 0, everything, now[8:9], q127, q126)
    s1 = tapped(taps, 0, everything, now[9:10], now[8:9], q127)
    for l in range(tiles):
        cols = slice(l * LANES, (l + 1) * LANES)
        near0, near1, direct = near[0:1, cols], near[1:2, cols], skip[0:1, cols]
        values = jnp.zeros((STEPS, LANES), F32)
        for m in range(MODES):
            values += node3[m, :, cols] * jnp.where(
                rows < NODES, later[m : m + 1, cols], entering[m : m + 1, cols]
            )
        c0, c1 = g0[:, cols], g1[:, cols]
        h0 = s0[:, cols] * (values[NODES : NODES + 1] + (near0 + direct) * c0)
        h1 = s1[:, cols] * (values[NODES + 1 : NODES + 2] + near1 * c0 + (near0 + direct) * c1)
        values = jnp.where(rows == NODES, h0, jnp.where(rows == NODES + 1, h1, values))
        flow[0, :, cols] = values.astype(BF16)

    f_copies = {}
    for ex in (1, 3, 2, 0):
        for ec in range(CORES):
            slot = ex * CORES + ec
            if slot:
                to = x_peer(CHIPS - ex) + (core if ec == 0 else 1 - core)
                copy = pltpu.make_async_remote_copy(
                    flow.at[0], flow.at[slot], f_send.at[slot], f_recv.at[slot],
                    device_id=(seq, to), device_id_type=MESH,
                )
                copy.start()
                pending.append(copy.wait_send)
                f_copies[slot] = copy

    send(5, OWN, 0)
    send(6, OWN, 1)
    arrived(0, OWN, 1)
    send(5, OWN, 1)
    arrived(1, OWN, 0)
    send(6, OWN, 0)
    for kind in (FACTOR, OWN):
        for p in range(PIECES):
            arrived(3 + p, kind, p)
            send(7, kind, p)

    loads[8].wait()
    loads[9].wait()
    for n, slot in enumerate((0, 1, 6, 2, 7, 3, 4, 5)):
        if slot % CORES:
            for kind in (FACTOR, OWN):
                for p in range(PIECES):
                    arrived({1: 2, 7: 5, 3: 6, 5: 7}[slot], kind, p)
        if slot:
            f_copies[slot].wait_recv()
        values = flow[slot]
        entering = jnp.dot(
            weights[...], jnp.concatenate([values, values], axis=0), preferred_element_type=F32
        )
        blocks = []
        for p in range(PIECES):
            own, factor = hid[slot, OWN, p].astype(F32), hid[slot, FACTOR, p].astype(F32)
            blocks.append((own + factor * entering[:, p * half : (p + 1) * half]).astype(BF16))
        owner = x_peer(slot // CORES) + (core if slot % CORES == 0 else 1 - core)
        wrows = weight[pl.ds(pl.multiple_of(owner * width, width), width), :]
        part = jnp.dot(jnp.concatenate(blocks, axis=1), wrows, preferred_element_type=F32)
        if n:
            part = part + acc[...]
        acc[...] = part

    mixed = acc[...].astype(BF16)
    out_ref[...] = jnp.dot(back, mixed, preferred_element_type=F32).astype(BF16)

    for wait in pending:
        wait()


def interpolation():
    turn = np.pi * (2 * np.arange(NODES) + 1) / (2 * NODES)
    places = ((ROWS - 1) / 2 * (1 - np.cos(turn))).astype(np.float32)
    at = places.astype(np.float64)
    share = np.array([1 / np.prod(at[i] - np.delete(at, i)) for i in range(NODES)])
    weights = np.zeros((ROWS, STEPS))
    for t in range(2, ROWS):
        part = share / (t - at)
        weights[t, :NODES] = part / part.sum()
    weights[0, NODES] = weights[1, NODES + 1] = 1
    weights = weights.reshape(SUBS, STEPS, STEPS).swapaxes(0, 1).reshape(ROWS, STEPS)
    high = weights.astype(ml_dtypes.bfloat16)
    low = (weights - high.astype(np.float64)).astype(ml_dtypes.bfloat16)
    places = np.broadcast_to(np.append(places, [0, 1]).astype(np.float32)[:, None], (STEPS, LANES))
    return np.concatenate([high, low], axis=1), np.ascontiguousarray(places)


def per_device(zs, ys, query, key, value, short_taps, residue, rate, skip, out_weight):
    width = query.shape[1]
    tiles = width // LANES
    weights, places = interpolation()
    modes = pltpu.VMEM((MODES, width), F32)
    table = pltpu.VMEM((MODES, SUBS, width), F32)
    block = pltpu.VMEM((STEPS, SUBS, width), F32)
    dma = pltpu.SemaphoreType.DMA
    regular = pltpu.SemaphoreType.REGULAR
    scratch = [
        pltpu.VMEM((ROWS, width), BF16),
        pltpu.VMEM((ROWS, width), BF16),
        pltpu.VMEM((ROWS, width), BF16),
        pltpu.VMEM(short_taps.shape, F32),
        modes,
        modes,
        pltpu.VMEM((1, width), F32),
        pltpu.VMEM(out_weight.shape, BF16),
        pltpu.VMEM(weights.shape, BF16),
        pltpu.VMEM(places.shape, F32),
        table,
        table,
        table,
        block,
        block,
        block,
        table,
        block,
        block,
        pltpu.VMEM((STEPS, width), F32),
        pltpu.VMEM((MODES, STEPS, width), F32),
        modes,
        pltpu.VMEM((ys, MODES + 16, width), BF16),
        pltpu.VMEM((16, width), F32),
        pltpu.VMEM((ys, 8, width), F32),
        pltpu.VMEM((ys, MODES, width), F32),
        pltpu.VMEM((MODES + 16, width), BF16),
        pltpu.VMEM((MODES, width), BF16),
        pltpu.VMEM((zs - 1, MODES + 16, width), BF16),
        modes,
        pltpu.VMEM((CHIPS * CORES, STEPS, width), BF16),
        pltpu.VMEM((CHIPS * CORES, 2, PIECES, ROWS, width // PIECES), BF16),
        pltpu.VMEM((ROWS, width), F32),
        dma((10,)),
        dma((2, ys - 1)),
        dma((2, ys - 1)),
        dma((2, zs - 1)),
        dma((2, zs - 1)),
        dma((len(ROUTES), 2, PIECES)),
        dma((len(ROUTES), 2, PIECES)),
        dma((CHIPS * CORES,)),
        dma((CHIPS * CORES,)),
        regular((zs - 1,)),
        regular((zs // 2 - 2,)),
    ]
    return pl.pallas_call(
        functools.partial(kernel, zs, ys),
        out_shape=pltpu.VMEM((ROWS, width), BF16),
        in_specs=[pl.BlockSpec(memory_space=pl.ANY)] * 10,
        out_specs=pl.BlockSpec(memory_space=pltpu.VMEM),
        scratch_shapes=scratch,
        compiler_params=pltpu.CompilerParams(
            collective_id=0, has_side_effects=True, vmem_limit_bytes=56 * 1024 * 1024
        ),
    )(
        query,
        key,
        value,
        short_taps,
        residue.T,
        rate.T,
        skip[None, :],
        out_weight,
        jnp.asarray(weights),
        jnp.asarray(places),
    )


def solution(mesh, ys=4):
    placed = (
        P("seq", "chan"),
        P("seq", "chan"),
        P("seq", "chan"),
        P(None, None, "chan"),
        P("chan", None),
        P("chan", None),
        P("chan"),
        P(None, "chan"),
    )
    return jax.shard_map(
        functools.partial(per_device, mesh.shape["seq"] // ys, ys),
        mesh=mesh,
        in_specs=placed,
        out_specs=P("seq", "chan"),
        check_vma=False,
    )
```

```python
import functools

import jax
import jax.numpy as jnp
import ml_dtypes
import numpy as np
from jax import lax
from jax.experimental import pallas as pl
from jax.experimental.pallas import tpu as pltpu
from jax.sharding import PartitionSpec as P

MESH = pl.DeviceIdType.MESH
F32 = jnp.float32
BF16 = jnp.bfloat16
MODES = 16
STEPS = 16
SUBS = 8
ROWS = STEPS * SUBS
LANES = 128
CHIPS = 4
CORES = 2
PIECES = 2
FACTOR, OWN = 0, 1
ROUTES = (
    (0, 6, "right"),
    (0, 2, "left"),
    (0, 1, "sibling"),
    (6, 4, "right"),
    (2, 4, "left"),
    (6, 7, "sibling"),
    (2, 3, "sibling"),
    (4, 5, "sibling"),
)
NODES = STEPS - 2


def tree_sum(array):
    while array.shape[0] > 1:
        half = array.shape[0] // 2
        array = array[:half] + array[half:]
    return array[0]


def lagged(block, last, last_but_one):
    one = jnp.concatenate([last[None], block[:-1]], axis=0)
    two = jnp.concatenate([last_but_one[None], one[:-1]], axis=0)
    return one, two


def tapped(taps, which, cols, now, one, two):
    return (
        taps[which, 0:1, cols] * now + taps[which, 1:2, cols] * one + taps[which, 2:3, cols] * two
    )


def kernel(
    zs,
    ys,
    q_hbm,
    k_hbm,
    v_hbm,
    taps_hbm,
    res_hbm,
    rate_hbm,
    skip_hbm,
    w_hbm,
    weights_hbm,
    places_hbm,
    out_ref,
    q_in,
    k_in,
    v_in,
    taps,
    res,
    rate,
    skip,
    weight,
    weights,
    places,
    rate3,
    decay3,
    gain3,
    xq,
    xk,
    xv,
    enter,
    local,
    query,
    near,
    node3,
    own_state,
    info,
    ends_before,
    heads,
    starts,
    total,
    half_sum,
    ring_z,
    before,
    flow,
    hid,
    acc,
    load_sem,
    y_send,
    y_recv,
    z_send,
    z_recv,
    g_send,
    g_recv,
    f_send,
    f_recv,
    ready_z,
    known,
):
    seq = lax.axis_index("seq")
    chan = lax.axis_index("chan")
    z, y = seq // ys, lax.rem(seq, ys)
    x, core = chan // CORES, lax.rem(chan, CORES)
    width = k_in.shape[1]
    tiles = width // LANES
    half = width // PIECES
    per = tiles // PIECES

    loads = [
        pltpu.make_async_copy(src, dst, load_sem.at[i])
        for i, (src, dst) in enumerate(
            [
                (rate_hbm, rate),
                (res_hbm, res),
                (taps_hbm, taps),
                (k_hbm, k_in),
                (v_hbm, v_in),
                (q_hbm, q_in),
                (skip_hbm, skip),
                (places_hbm, places),
                (weights_hbm, weights),
                (w_hbm, weight),
            ]
        )
    ]
    for i in (5, 3, 4, 2, 0, 1, 6, 7, 8, 9):
        loads[i].start()
    pending = []

    def at(zz, yy):
        return zz * ys + yy

    def signal(sem, s, c):
        pl.semaphore_signal(sem, inc=1, device_id=(s, c), device_id_type=MESH)

    def x_peer(e):
        return lax.rem(x + e, CHIPS) * CORES

    right = x_peer(1) + core
    left = x_peer(CHIPS - 1) + core
    sibling = x * CORES + 1 - core
    z_up = lax.rem(z + 1, zs)
    z_down = lax.rem(z + zs - 1, zs)

    barrier = pltpu.get_barrier_semaphore()
    for e in range(1, CHIPS):
        for c in range(CORES):
            signal(barrier, seq, x_peer(e) + c)
    signal(barrier, seq, sibling)
    for e in range(1, ys):
        signal(barrier, at(z, lax.rem(y + e, ys)), chan)
    hub = zs // 2
    early = z < hub
    place = lax.rem(z, hub)
    for d in range(1, zs):

        @pl.when(early & (z + d < zs) & ((z + d < hub) | (z >= hub - 2)))
        def _():
            signal(barrier, at(lax.rem(z + d, zs), y), chan)

    @pl.when((z >= hub) & (z < zs - 1))
    def _():
        signal(barrier, at(z_up, y), chan)

    @pl.when(z > hub)
    def _():
        signal(barrier, at(z_down, y), chan)

    row = lax.broadcasted_iota(jnp.int32, (ROWS, ROWS), 0)
    col = lax.broadcasted_iota(jnp.int32, (ROWS, ROWS), 1)
    order = jnp.where(col == (row & 7) * STEPS + (row >> 3), 1.0, 0.0).astype(BF16)
    back = jnp.where(row == (col & 7) * STEPS + (col >> 3), 1.0, 0.0).astype(BF16)

    def arranged(block):
        return jnp.dot(order, block, preferred_element_type=F32).reshape(STEPS, SUBS, width)

    sub = lax.broadcasted_iota(jnp.int32, (SUBS, LANES), 0)
    sub3 = lax.broadcasted_iota(jnp.int32, (MODES, SUBS, LANES), 1)
    first = sub == 0
    subf3 = sub3.astype(F32)

    loads[2].wait()
    loads[5].wait()
    xq[...] = arranged(q_in[...])

    pick = lax.broadcasted_iota(jnp.int32, (MODES, ROWS), 0)
    pos = lax.broadcasted_iota(jnp.int32, (MODES, ROWS), 1)

    def ends_of(base, block):
        i = pick - base
        ends = ((i >= 0) & (i < 2) & (pos == i)) | ((i >= 2) & (i < 4) & (pos == i + ROWS - 4))
        return jnp.dot(
            jnp.where(ends, 1.0, 0.0).astype(BF16), block[...], preferred_element_type=F32
        )

    def lags(block):
        last = jnp.where(first, 0.0, pltpu.roll(block[STEPS - 1], 1, 0))
        last_but_one = jnp.where(first, 0.0, pltpu.roll(block[STEPS - 2], 1, 0))
        return lagged(block, last, last_but_one)

    g_copies = {}

    def send(route, kind, piece):
        slot, to_slot, to = ROUTES[route]
        to = {"right": right, "left": left, "sibling": sibling}[to]
        copy = pltpu.make_async_remote_copy(
            hid.at[slot, kind, piece],
            hid.at[to_slot, kind, piece],
            g_send.at[route, kind, piece],
            g_recv.at[route, kind, piece],
            device_id=(seq, to),
            device_id_type=MESH,
        )
        copy.start()
        pending.append(copy.wait_send)
        g_copies[route, kind, piece] = copy

    def arrived(route, kind, piece):
        g_copies[route, kind, piece].wait_recv()

    for l in range(tiles):
        cols = slice(l * LANES, (l + 1) * LANES)
        qb = xq[:, :, cols]
        qb = tapped(taps, 0, cols, qb, *lags(qb))
        query[:, :, cols] = qb
        qb = jnp.concatenate([jnp.where(first[None], 1.0, qb[:2]), qb[2:]], axis=0)
        to = slice(l % per * LANES, (l % per + 1) * LANES)
        hid[0, FACTOR, l // per, :, to] = qb.reshape(ROWS, LANES).astype(BF16)
    loads[3].wait()
    loads[4].wait()
    info[y, MODES : MODES + 16, :] = (ends_of(0, k_in) + ends_of(4, v_in) + ends_of(8, q_in)).astype(BF16)

    pl.semaphore_wait(
        barrier,
        (CORES * CHIPS - 1 + ys - 1)
        + jnp.where(early, z, 2 + jnp.where(z > hub, 1, 0) + jnp.where(z < zs - 1, 1, 0))
    )
    for d in range(1, zs):

        @pl.when((z >= d) & (z - d < hub) & (early | (z - d >= hub - 2)))
        def _():
            signal(ready_z.at[d - 1], at(lax.rem(z + zs - d, zs), y), chan)

    @pl.when((z > hub) & (z < zs - 1))
    def _():
        signal(known.at[0], at(z_down, y), chan)

    def to_group(part):
        copies = []
        for e in sorted(range(1, ys), key=lambda e: -min(e, ys - e)):
            copy = pltpu.make_async_remote_copy(
                info.at[y, pl.ds(MODES * part, MODES)],
                info.at[y, pl.ds(MODES * part, MODES)],
                y_send.at[part, e - 1],
                y_recv.at[part, e - 1],
                device_id=(at(z, lax.rem(y + e, ys)), chan),
                device_id_type=MESH,
            )
            copy.start()
            pending.append(copy.wait_send)
            copies.append(copy)
        return copies

    row_copies = to_group(1)

    for route, piece in ((0, 0), (1, 1), (0, 1), (1, 0), (2, 0), (2, 1)):
        send(route, FACTOR, piece)

    xk[...] = arranged(k_in[...])
    xv[...] = arranged(v_in[...])
    loads[0].wait()
    loads[1].wait()
    r = rate[...]
    series = r * (1.0 - r * (1 / 2) * (1.0 - r * (1 / 3) * (1.0 - r * (1 / 4) * (1.0 - r * (1 / 5) * (1.0 - r * (1 / 6))))))
    gain = res[...] * series
    decay = jnp.exp(-r)
    for m in range(MODES):
        rate3[m] = jnp.broadcast_to(r[m : m + 1], (SUBS, width))
        decay3[m] = jnp.broadcast_to(decay[m : m + 1], (SUBS, width))
        gain3[m] = jnp.broadcast_to(gain[m : m + 1], (SUBS, width))

    for l in range(tiles):
        cols = slice(l * LANES, (l + 1) * LANES)
        kb, vb = xk[:, :, cols], xv[:, :, cols]
        g = tapped(taps, 1, cols, kb, *lags(kb)) * tapped(taps, 2, cols, vb, *lags(vb))
        g = jnp.concatenate([jnp.where(first[None], 0.0, g[:2]), g[2:]], axis=0)
        local[:, :, cols] = g
        a = decay3[:, :, cols]
        state = jnp.broadcast_to(g[0][None], a.shape)
        for j in range(1, STEPS):
            state = state * a + g[j][None]
        step = a
        for _ in range(4):
            step = step * step
        for reach in (1, 2, 4):
            state = state + jnp.where(sub3 >= reach, step, 0.0) * pltpu.roll(state, reach, 1)
            step = step * step
        enter[:, :, cols] = jnp.where(sub3 >= 1, pltpu.roll(state, 1, 1), 0.0)
        for m in range(MODES):
            own_state[m : m + 1, cols] = state[m, SUBS - 1 : SUBS, :]

    info[y, 0:MODES, :] = own_state[...].astype(BF16)

    y_copies = to_group(0)

    loads[6].wait()
    for p in range(PIECES):
        for i in range(per):
            l = p * per + i
            cols = slice(l * LANES, (l + 1) * LANES)
            r3, a, w = rate3[:, :, cols], decay3[:, :, cols], gain3[:, :, cols]
            close = w * jnp.exp(-subf3 * r3)
            a8 = a * a
            a8 = a8 * a8
            a8 = a8 * a8
            near[0:SUBS, cols] = tree_sum(close)
            near[SUBS : 2 * SUBS, cols] = tree_sum(close * a8)
            g = local[:, :, cols]
            out = g * skip[0:1, cols]
            for d in range(STEPS):
                add = g[: STEPS - d] * near[d : d + 1, cols][None]
                out = out + add if d == 0 else jnp.concatenate([out[:d], out[d:] + add], axis=0)
            state = w * a * enter[:, :, cols]
            own = []
            for j in range(STEPS):
                line = query[j, :, cols] * (out[j] + tree_sum(state))
                if j < STEPS - 1:
                    state = state * a
                own.append(jnp.where(first, 0.0, line) if j < 2 else line)
            to = slice(i * LANES, (i + 1) * LANES)
            hid[0, OWN, p, :, to] = jnp.concatenate(own, axis=0).astype(BF16)
        send(0, OWN, p)
        send(2, OWN, p)
    for p in reversed(range(PIECES)):
        send(1, OWN, p)

    for i in range(hub - 2):

        @pl.when((z >= hub) & (z + 2 + i < zs))
        def _():
            pl.semaphore_wait(known.at[i], 1)
            if i < hub - 3:
                pl.when(z > hub)(lambda: signal(known.at[i + 1], at(z_down, y), chan))

    to_half = hub - z

    def to_later(part, source, d):
        return pltpu.make_async_remote_copy(
            source.at[pl.ds(MODES * part, MODES)],
            ring_z.at[d - 1, pl.ds(MODES * part, MODES)],
            z_send.at[part, d - 1],
            z_recv.at[part, d - 1],
            device_id=(at(lax.rem(z + d, zs), y), chan),
            device_id_type=MESH,
        )

    def send_later(part, source, distances, among):
        for d in distances:

            @pl.when((z + d < zs) & among(d))
            def _():
                if part or d > 1:

                    @pl.when(early)
                    def _():
                        pl.semaphore_wait(ready_z.at[d - 1], 1)

                to_later(part, source, d).start()

            pending.append(
                functools.partial(
                    pl.when((z + d < zs) & among(d)), to_later(part, source, d).wait_send
                )
            )

    def in_half(d):
        return (z >= hub) | (d < to_half)

    for copy in row_copies:
        copy.wait_recv()
    total[MODES : MODES + 16, :] = info[ys - 1, MODES : MODES + 16, :]
    send_later(1, total, (1,), lambda d: z < zs - 1)

    arrived(0, FACTOR, 0)
    send(3, FACTOR, 0)
    arrived(1, FACTOR, 1)
    send(4, FACTOR, 1)

    r = rate[...]
    a126 = jnp.exp(-(ROWS - 2.0) * r)
    a127 = jnp.exp(-(ROWS - 1.0) * r)
    a128 = jnp.exp(-float(ROWS) * r)
    everything = slice(0, width)
    loads[7].wait()
    for l in range(tiles):
        cols = slice(l * LANES, (l + 1) * LANES)
        for m in range(MODES):
            node3[m, :, cols] = gain3[m, 0:1, cols] * jnp.exp(
                -(places[...] + 1.0) * rate[m : m + 1, cols]
            )

    for copy in y_copies:
        copy.wait_recv()
    a512 = jnp.exp(-float(ROWS * ys) * r)

    def first_two(now, ends):
        k0, k1, v0, v1 = (now[i : i + 1] for i in (0, 1, 4, 5))
        k126, k127, v126, v127 = (ends[i : i + 1] for i in (2, 3, 6, 7))
        g0 = tapped(taps, 1, everything, k0, k127, k126) * tapped(
            taps, 2, everything, v0, v127, v126
        )
        g1 = tapped(taps, 1, everything, k1, k0, k127) * tapped(taps, 2, everything, v1, v0, v127)
        return g0, g1

    def set_heads(e, now, ends):
        g0, g1 = first_two(now, ends)
        for i, line in enumerate((g0, g1, ends[10:11], ends[11:12])):
            heads[e, i : i + 1, :] = line
        return a127 * g0 + a126 * g1

    @pl.when(z == 0)
    def _():
        ends_before[...] = jnp.zeros_like(ends_before)

    @pl.when(z > 0)
    def _():
        to_later(1, total, 1).wait_recv()
        ends_before[...] = ring_z[0, MODES : MODES + 16, :].astype(F32)

    ends = ends_before[...]
    start = jnp.zeros_like(r)
    for e in range(ys):
        now = info[e, MODES : MODES + 16, :].astype(F32)
        starts[e] = start
        start = start * a128 + (info[e, 0:MODES, :].astype(F32) + set_heads(e, now, ends))
        ends = now
    total[0:MODES, :] = start.astype(BF16)

    send_later(0, total, range(hub - 1, 0, -1), in_half)
    send_later(0, total, range(hub, 0, -1), lambda d: z == hub - 1)

    arrived(0, OWN, 0)
    send(3, OWN, 0)
    arrived(1, OWN, 1)
    send(4, OWN, 1)
    send(5, FACTOR, 0)
    send(6, FACTOR, 1)
    arrived(0, FACTOR, 1)
    send(5, FACTOR, 1)
    arrived(1, FACTOR, 0)
    send(6, FACTOR, 0)
    before[...] = jnp.zeros_like(before)
    for d in range(hub + 1, 0, -1):

        @pl.when((z >= d) & (early | (z - d >= hub - 2)))
        def _():
            to_later(0, total, d).wait_recv()
            before[...] = before[...] * a512 + ring_z[d - 1, 0:MODES, :].astype(F32)

    @pl.when(z == hub - 2)
    def _():
        half_sum[...] = (total[0:MODES, :].astype(F32) + a512 * before[...]).astype(BF16)

    send_later(0, half_sum, range(hub + 1, 1, -1), lambda d: z == hub - 2)

    entering = starts[y] + jnp.exp(-float(ROWS) * y.astype(F32) * r) * before[...]
    g0, g1, q126, q127 = (heads[y, i : i + 1, :] for i in range(4))
    later = entering + jnp.exp(r) * g0 + jnp.exp(2.0 * r) * g1
    rows = lax.broadcasted_iota(jnp.int32, (STEPS, LANES), 0)
    now = info[y, MODES : MODES + 16, :].astype(F32)
    s0 = tapped(taps, 0, everything, now[8:9], q127, q126)
    s1 = tapped(taps, 0, everything, now[9:10], now[8:9], q127)
    for l in range(tiles):
        cols = slice(l * LANES, (l + 1) * LANES)
        near0, near1, direct = near[0:1, cols], near[1:2, cols], skip[0:1, cols]
        values = jnp.zeros((STEPS, LANES), F32)
        for m in range(MODES):
            values += node3[m, :, cols] * jnp.where(
                rows < NODES, later[m : m + 1, cols], entering[m : m + 1, cols]
            )
        c0, c1 = g0[:, cols], g1[:, cols]
        h0 = s0[:, cols] * (values[NODES : NODES + 1] + (near0 + direct) * c0)
        h1 = s1[:, cols] * (values[NODES + 1 : NODES + 2] + near1 * c0 + (near0 + direct) * c1)
        values = jnp.where(rows == NODES, h0, jnp.where(rows == NODES + 1, h1, values))
        flow[0, :, cols] = values.astype(BF16)

    f_copies = {}
    for ex in (1, 3, 2, 0):
        for ec in range(CORES):
            slot = ex * CORES + ec
            if slot:
                to = x_peer(CHIPS - ex) + (core if ec == 0 else 1 - core)
                copy = pltpu.make_async_remote_copy(
                    flow.at[0], flow.at[slot], f_send.at[slot], f_recv.at[slot],
                    device_id=(seq, to), device_id_type=MESH,
                )
                copy.start()
                pending.append(copy.wait_send)
                f_copies[slot] = copy

    send(5, OWN, 0)
    send(6, OWN, 1)
    arrived(0, OWN, 1)
    send(5, OWN, 1)
    arrived(1, OWN, 0)
    send(6, OWN, 0)
    for kind in (FACTOR, OWN):
        for p in range(PIECES):
            arrived(3 + p, kind, p)
            send(7, kind, p)

    loads[8].wait()
    loads[9].wait()
    for n, slot in enumerate((0, 1, 6, 2, 7, 3, 4, 5)):
        if slot % CORES:
            for kind in (FACTOR, OWN):
                for p in range(PIECES):
                    arrived({1: 2, 7: 5, 3: 6, 5: 7}[slot], kind, p)
        if slot:
            f_copies[slot].wait_recv()
        values = flow[slot]
        entering = jnp.dot(
            weights[...], jnp.concatenate([values, values], axis=0), preferred_element_type=F32
        )
        blocks = []
        for p in range(PIECES):
            own, factor = hid[slot, OWN, p].astype(F32), hid[slot, FACTOR, p].astype(F32)
            blocks.append((own + factor * entering[:, p * half : (p + 1) * half]).astype(BF16))
        owner = x_peer(slot // CORES) + (core if slot % CORES == 0 else 1 - core)
        wrows = weight[pl.ds(pl.multiple_of(owner * width, width), width), :]
        part = jnp.dot(jnp.concatenate(blocks, axis=1), wrows, preferred_element_type=F32)
        if n:
            part = part + acc[...]
        acc[...] = part

    mixed = acc[...].astype(BF16)
    out_ref[...] = jnp.dot(back, mixed, preferred_element_type=F32).astype(BF16)

    for wait in pending:
        wait()


def interpolation():
    turn = np.pi * (2 * np.arange(NODES) + 1) / (2 * NODES)
    places = ((ROWS - 1) / 2 * (1 - np.cos(turn))).astype(np.float32)
    at = places.astype(np.float64)
    share = np.array([1 / np.prod(at[i] - np.delete(at, i)) for i in range(NODES)])
    weights = np.zeros((ROWS, STEPS))
    for t in range(2, ROWS):
        part = share / (t - at)
        weights[t, :NODES] = part / part.sum()
    weights[0, NODES] = weights[1, NODES + 1] = 1
    weights = weights.reshape(SUBS, STEPS, STEPS).swapaxes(0, 1).reshape(ROWS, STEPS)
    high = weights.astype(ml_dtypes.bfloat16)
    low = (weights - high.astype(np.float64)).astype(ml_dtypes.bfloat16)
    places = np.broadcast_to(np.append(places, [0, 1]).astype(np.float32)[:, None], (STEPS, LANES))
    return np.concatenate([high, low], axis=1), np.ascontiguousarray(places)


def per_device(zs, ys, query, key, value, short_taps, residue, rate, skip, out_weight):
    width = query.shape[1]
    tiles = width // LANES
    weights, places = interpolation()
    modes = pltpu.VMEM((MODES, width), F32)
    table = pltpu.VMEM((MODES, SUBS, width), F32)
    block = pltpu.VMEM((STEPS, SUBS, width), F32)
    dma = pltpu.SemaphoreType.DMA
    regular = pltpu.SemaphoreType.REGULAR
    scratch = [
        pltpu.VMEM((ROWS, width), BF16),
        pltpu.VMEM((ROWS, width), BF16),
        pltpu.VMEM((ROWS, width), BF16),
        pltpu.VMEM(short_taps.shape, F32),
        modes,
        modes,
        pltpu.VMEM((1, width), F32),
        pltpu.VMEM(out_weight.shape, BF16),
        pltpu.VMEM(weights.shape, BF16),
        pltpu.VMEM(places.shape, F32),
        table,
        table,
        table,
        block,
        block,
        block,
        table,
        block,
        block,
        pltpu.VMEM((STEPS, width), F32),
        pltpu.VMEM((MODES, STEPS, width), F32),
        modes,
        pltpu.VMEM((ys, MODES + 16, width), BF16),
        pltpu.VMEM((16, width), F32),
        pltpu.VMEM((ys, 8, width), F32),
        pltpu.VMEM((ys, MODES, width), F32),
        pltpu.VMEM((MODES + 16, width), BF16),
        pltpu.VMEM((MODES, width), BF16),
        pltpu.VMEM((zs - 1, MODES + 16, width), BF16),
        modes,
        pltpu.VMEM((CHIPS * CORES, STEPS, width), BF16),
        pltpu.VMEM((CHIPS * CORES, 2, PIECES, ROWS, width // PIECES), BF16),
        pltpu.VMEM((ROWS, width), F32),
        dma((10,)),
        dma((2, ys - 1)),
        dma((2, ys - 1)),
        dma((2, zs - 1)),
        dma((2, zs - 1)),
        dma((len(ROUTES), 2, PIECES)),
        dma((len(ROUTES), 2, PIECES)),
        dma((CHIPS * CORES,)),
        dma((CHIPS * CORES,)),
        regular((zs - 1,)),
        regular((zs // 2 - 2,)),
    ]
    return pl.pallas_call(
        functools.partial(kernel, zs, ys),
        out_shape=pltpu.VMEM((ROWS, width), BF16),
        in_specs=[pl.BlockSpec(memory_space=pl.ANY)] * 10,
        out_specs=pl.BlockSpec(memory_space=pltpu.VMEM),
        scratch_shapes=scratch,
        compiler_params=pltpu.CompilerParams(
            collective_id=0, has_side_effects=True, vmem_limit_bytes=56 * 1024 * 1024
        ),
    )(
        query,
        key,
        value,
        short_taps,
        residue.T,
        rate.T,
        skip[None, :],
        out_weight,
        jnp.asarray(weights),
        jnp.asarray(places),
    )


def solution(mesh, ys=4):
    placed = (
        P("seq", "chan"),
        P("seq", "chan"),
        P("seq", "chan"),
        P(None, None, "chan"),
        P("chan", None),
        P("chan", None),
        P("chan"),
        P(None, "chan"),
    )
    return jax.shard_map(
        functools.partial(per_device, mesh.shape["seq"] // ys, ys),
        mesh=mesh,
        in_specs=placed,
        out_specs=P("seq", "chan"),
        check_vma=False,
    )
```
